32 devices in a mesh: dp: 8 (over z, y), row: 2 (over x), col: 2 (over core).
Axes of the slice: x: 2, y: 2, z: 4, core: 2. Of those that a mesh axis runs over, the one named last changes fastest.
Arguments:
- inputs: bfloat16 [150, 192, 2000], P(None, 'dp', 'row'), may hold values from -6 to 6
- w_second: bfloat16 [2000, 2000], P('row', 'col'), may hold values from -0.125 to 0.125
- gain_second: float32 [2000], P('col'), may hold values from 0.5 to 1.5
- shift_second: float32 [2000], P('col'), may hold values from -3 to 3
- recur_second: float32 [2000], P('col'), may hold values from 0.2 to 0.9
- w_third: bfloat16 [2000, 2000], P('col', 'row'), may hold values from -0.125 to 0.125
- gain_third: float32 [2000], P('row'), may hold values from 0.5 to 1.5
- shift_third: float32 [2000], P('row'), may hold values from -3 to 3
- recur_third: float32 [2000], P('row'), may hold values from 0.2 to 0.9
- cotangent: bfloat16 [150, 192, 2000], P(None, ('dp', 'col'), 'row'), may hold values from -6 to 6
Outputs:
- output: float32 [150, 192, 2000], P(None, ('dp', 'col'), 'row')
- grad_inputs: float32 [150, 192, 2000], P(None, ('dp', 'col'), 'row')
- grad_w_second: float32 [2000, 2000], P('row', 'col')
- grad_gain_second: float32 [2000], P('col')
- grad_shift_second: float32 [2000], P('col')
- grad_recur_second: float32 [2000], P('col')
- grad_w_third: float32 [2000, 2000], P('col', 'row')
- grad_gain_third: float32 [2000], P('row')
- grad_shift_third: float32 [2000], P('row')
- grad_recur_third: float32 [2000], P('row')
The draws below stay inside these ranges and needn't reach their ends.
All inputs are finite; a program needn't handle non-finite values.
Results may differ from the reference program's by a relative error of at most 0.0065.
Values may be sent and summed in bfloat16 or wider, within the bound.
No kernel may reach another device: no remote copies, remote signals or barrier semaphores. Data moves between devices by JAX's collectives and lax.ppermute only.
A program may use at most 256 MiB of HBM per device.

```python
import jax
import jax.numpy as jnp
from jax import lax

WIDTH = 2000
STEPS = 150
BLOCK = 50
SEQS = 192


def block_levels(stream_key, dims, cuts, low, high):
    level = 1.0
    for axis_at, parts in cuts:
        heights = jax.random.uniform(jax.random.fold_in(jax.random.fold_in(stream_key, 6), axis_at), (parts,), jnp.float32, low / len(cuts), high / len(cuts))
        level = level * jnp.repeat(jnp.exp(heights), dims[axis_at] // parts).reshape((-1,) + (1,) * (len(dims) - 1 - axis_at))
    return level


def noise(key, extent, scale, most, cuts=(), kind=jnp.bfloat16):
    values = scale * jax.random.normal(key, extent, jnp.float32)
    if cuts:
        values = values * block_levels(key, extent, cuts, -0.22, 0.18)
    return jnp.clip(values, -most, most).astype(kind)


def setup_inputs(seed: int = 0) -> dict:
    keys = jax.random.split(jax.random.key(seed), 11)
    inputs = noise(keys[0], (STEPS, SEQS, WIDTH), 1.0, 6.0, ((1, 8), (2, 2)))
    w_second = noise(keys[1], (WIDTH, WIDTH), WIDTH ** -0.5, 0.125, ((0, 2), (1, 2)))
    gain_second = jnp.clip(0.5 + 1.0 * jax.random.uniform(keys[2], (WIDTH,), jnp.float32) ** block_levels(keys[2], (WIDTH,), ((0, 2),), -0.2, 0.2), 0.5, 1.5)
    shift_second = noise(keys[3], (WIDTH,), 0.5, 3.0, ((0, 2),), jnp.float32)
    recur_second = jnp.clip(0.2 + 0.7 * jax.random.uniform(keys[4], (WIDTH,), jnp.float32) ** block_levels(keys[4], (WIDTH,), ((0, 2),), -0.2, 0.2), 0.2, 0.9)
    w_third = noise(keys[5], (WIDTH, WIDTH), WIDTH ** -0.5, 0.125, ((0, 2), (1, 2)))
    gain_third = jnp.clip(0.5 + 1.0 * jax.random.uniform(keys[6], (WIDTH,), jnp.float32) ** block_levels(keys[6], (WIDTH,), ((0, 2),), -0.2, 0.2), 0.5, 1.5)
    shift_third = noise(keys[7], (WIDTH,), 0.5, 3.0, ((0, 2),), jnp.float32)
    recur_third = jnp.clip(0.2 + 0.7 * jax.random.uniform(keys[8], (WIDTH,), jnp.float32) ** block_levels(keys[8], (WIDTH,), ((0, 2),), -0.2, 0.2), 0.2, 0.9)
    cotangent = noise(keys[9], (STEPS, SEQS, WIDTH), 1.0, 6.0, ((1, 16), (2, 2)))
    return dict(inputs=inputs, w_second=w_second, gain_second=gain_second, shift_second=shift_second, recur_second=recur_second, w_third=w_third, gain_third=gain_third, shift_third=shift_third, recur_third=recur_third, cotangent=cotangent)


norm_eps = 1e-05

@jax.custom_vjp
def low(v):
    return lax.optimization_barrier(v.astype(jnp.bfloat16)).astype(jnp.float32)

@jax.custom_vjp
def low_back(v):
    return v

def low_keep(v):
    return (low(v), None)

def low_pass(kept, grad):
    return (grad,)

def back_keep(v):
    return (v, None)

def back_low(kept, grad):
    return (low(grad),)
low.defvjp(low_keep, low_pass)
low_back.defvjp(back_keep, back_low)

def recurrence(pre_norm, recur):
    blocks = pre_norm.reshape((STEPS // BLOCK, BLOCK) + pre_norm.shape[1:])

    @jax.checkpoint
    def run_block(state, block_rows):

        def advance(inner, column):
            fresh = jax.nn.gelu(column + recur * inner)
            return (fresh, fresh)
        return lax.scan(advance, state, block_rows)
    start = jnp.zeros(pre_norm.shape[1:], jnp.float32)
    _, states = lax.scan(run_block, start, blocks)
    return states.reshape(pre_norm.shape)

def normalize(proj, gain, shift):
    mean = lax.optimization_barrier(jnp.mean(proj, axis=(0, 1)))
    var = lax.optimization_barrier(jnp.mean(proj * proj, axis=(0, 1))) - mean * mean
    return gain * ((proj - mean) * lax.rsqrt(var + norm_eps)) + shift

def project(left, right):
    return jnp.einsum('tsi,ij->tsj', left, right, precision=lax.Precision.HIGHEST)

def forward(inputs, w_second, gain_second, shift_second, recur_second, w_third, gain_third, shift_third, recur_third):
    proj_second = low_back(project(inputs, w_second))
    hidden = low(recurrence(normalize(proj_second, gain_second, shift_second), recur_second))
    proj_third = low_back(project(hidden, w_third))
    states_third = recurrence(normalize(proj_third, gain_third, shift_third), recur_third)
    return inputs + states_third

def reference(inputs, w_second, gain_second, shift_second, recur_second, w_third, gain_third, shift_third, recur_third, cotangent):
    floats = (inputs.astype(jnp.float32), w_second.astype(jnp.float32), gain_second, shift_second, recur_second, w_third.astype(jnp.float32), gain_third, shift_third, recur_third)
    output, pull = jax.vjp(forward, *floats)
    grads = pull(cotangent.astype(jnp.float32))
    return (output, grads[0], grads[1], grads[2], grads[3], grads[4], grads[5], grads[6], grads[7], grads[8])
```

```python
import functools

import jax
import jax.numpy as jnp
from jax import lax
from jax.experimental import pallas as pl
from jax.experimental.pallas import tpu as pltpu
from jax.sharding import PartitionSpec as P

norm_eps = 1e-05
gelu_outer = 0.7978845608028654
gelu_inner = gelu_outer * 0.044715
LANES = 128
BLOCK = 256
f32 = jnp.float32
bf16 = jnp.bfloat16


def params():
    return pltpu.CompilerParams(vmem_limit_bytes=56 * 2**20)


def round_up(value, unit):
    return -(-value // unit) * unit


def whole(shape):
    return pl.BlockSpec(shape, lambda *_: (0,) * len(shape), pipeline_mode=pl.Buffered(1))


def dot(left, right, dims):
    return lax.dot_general(left, right, (dims, ((), ())), preferred_element_type=f32)


def tie(value, after):
    return lax.optimization_barrier((value, after))[0]


def tile_of(j):
    return pl.ds(j * LANES, LANES)


def held(j, low, count):
    return jnp.clip(j - low, 0, count - 1)


def prep_kernel(seqs, pitch, width, base, at_ref, inputs, *refs):
    near, send, scratch, packed = refs[-4:]
    steps, group, block = inputs.shape
    lane = base + pl.program_id(0) * block + lax.broadcasted_iota(jnp.int32, (1, LANES), 1)
    rows = near.shape[0]
    for k in range(block // LANES):
        scratch[...] = inputs[:, :, tile_of(k)].astype(f32).reshape(steps * group, LANES)
        for place, out in ((0, near), (1, send)):
            first = at_ref[place]
            for s in range(seqs):
                packed[s * pitch : s * pitch + steps, :] = scratch[pl.ds(first + s, steps, stride=group), :]
                packed[s * pitch + steps : (s + 1) * pitch, :] = jnp.zeros((pitch - steps, LANES), f32)
            out[:, tile_of(k)] = jnp.where(lane + k * LANES < width, packed[...], 0.0).astype(bf16)


def prep(inputs, places, seqs, pitch, half, first, blocks, near=None):
    steps, group, width = inputs.shape
    rows = seqs * pitch
    near_spec = pl.BlockSpec((rows, BLOCK), lambda j, at: (0, j + first))
    return pl.pallas_call(
        functools.partial(prep_kernel, seqs, pitch, width, first * BLOCK),
        grid_spec=pltpu.PrefetchScalarGridSpec(
            num_scalar_prefetch=1,
            grid=(blocks,),
            in_specs=[pl.BlockSpec((steps, group, BLOCK), lambda j, at: (0, 0, j + first))]
            + ([] if near is None else [pl.BlockSpec(memory_space=pl.ANY)]),
            out_specs=[near_spec, pl.BlockSpec((rows, BLOCK), lambda j, at: (0, j))],
            scratch_shapes=[pltpu.VMEM((steps * group, LANES), f32), pltpu.VMEM((rows, LANES), f32)],
        ),
        out_shape=[
            jax.ShapeDtypeStruct((rows, half), bf16),
            jax.ShapeDtypeStruct((rows, blocks * BLOCK), bf16),
        ],
        input_output_aliases={} if near is None else {2: 0},
        compiler_params=params(),
        name="prep",
    )(places, inputs, *(() if near is None else (near,)))


def prep_grads_kernel(pitch, width, at_ref, own, other, near, send, packed):
    seqs, steps, block = own.shape
    lane = pl.program_id(0) * block + lax.broadcasted_iota(jnp.int32, (1, block), 1)
    for part, out in ((own, near), (other, send)):
        for s in range(seqs):
            packed[s * pitch : s * pitch + steps, :] = part[s].astype(f32)
            packed[s * pitch + steps : (s + 1) * pitch, :] = jnp.zeros((pitch - steps, block), f32)
        out[...] = jnp.where(lane < width, packed[...], 0.0).astype(bf16)


def prep_grads(grads, places, seqs, pitch, half):
    _, steps, width = grads.shape
    rows = seqs * pitch
    out = pl.BlockSpec((rows, BLOCK), lambda j, at: (0, j))
    return pl.pallas_call(
        functools.partial(prep_grads_kernel, pitch, width),
        grid_spec=pltpu.PrefetchScalarGridSpec(
            num_scalar_prefetch=1,
            grid=(half // BLOCK,),
            in_specs=[
                pl.BlockSpec((seqs, steps, BLOCK), lambda j, at: (at[0], 0, j)),
                pl.BlockSpec((seqs, steps, BLOCK), lambda j, at: (at[1], 0, j)),
            ],
            out_specs=[out, out],
            scratch_shapes=[pltpu.VMEM((rows, BLOCK), f32)],
        ),
        out_shape=[jax.ShapeDtypeStruct((rows, half), bf16)] * 2,
        compiler_params=params(),
        name="prep_grads",
    )(places, grads, grads)


def combine_kernel(pitch, at_ref, a_near, b_near, a_far0, a_far1, b_far, out):
    seqs, steps, block = out.shape

    def put(a, b):
        total = a[...].astype(f32) + b[...].astype(f32)
        for s in range(seqs):
            out[s] = total[s * pitch : s * pitch + steps, :]

    part, lanes = pl.program_id(0), pl.program_id(1)
    cut = pl.num_programs(1) // 2
    pl.when(part == 0)(lambda: put(a_near, b_near))
    pl.when((part == 1) & (lanes < cut))(lambda: put(a_far0, b_far))
    pl.when((part == 1) & (lanes >= cut))(lambda: put(a_far1, b_far))


def combine(places, a_near, b_near, a_far, b_far, seqs, steps, width):
    rows, half = a_near.shape
    nb = half // BLOCK
    far0, far1 = a_far
    cut = far0.shape[1] // BLOCK if len(a_far) > 1 else nb
    near_spec = pl.BlockSpec((rows, BLOCK), lambda p, j, at: (0, jnp.where(p == 0, j, nb - 1)))
    far_spec = pl.BlockSpec((rows, BLOCK), lambda p, j, at: (0, jnp.where(p == 0, 0, j)))
    split = far0.shape[1] < half
    far0_spec = pl.BlockSpec((rows, BLOCK), lambda p, j, at: (0, jnp.where(p == 0, 0, jnp.minimum(j, nb // 2 - 1))))
    far1_at = 0 if split else nb // 2
    far1_spec = pl.BlockSpec(
        (rows, BLOCK), lambda p, j, at: (0, far1_at + jnp.where(p == 0, 0, jnp.maximum(j - nb // 2, 0)))
    )
    return pl.pallas_call(
        functools.partial(combine_kernel, rows // seqs),
        grid_spec=pltpu.PrefetchScalarGridSpec(
            num_scalar_prefetch=1,
            grid=(2, nb),
            in_specs=[near_spec, near_spec, far0_spec, far1_spec, far_spec],
            out_specs=pl.BlockSpec((seqs, steps, BLOCK), lambda p, j, at: (at[p], 0, j)),
        ),
        out_shape=jax.ShapeDtypeStruct((2 * seqs, steps, width), f32),
        compiler_params=params(),
        name="combine",
    )(places, a_near, b_near, far0, far1, b_far)


def cut_kernel(pieces, at_ref, weight, out):
    tall, wide = out.shape
    start = (pl.program_id(0) * pieces + at_ref[0]) * tall
    row = start + lax.broadcasted_iota(jnp.int32, (tall, wide), 0)
    lane = lax.broadcasted_iota(jnp.int32, (tall, wide), 1)
    limit_rows, limit_lanes = at_ref[1], at_ref[2]
    value = weight[...].astype(f32)
    out[...] = jnp.where((row < limit_rows) & (lane < limit_lanes), value, 0.0).astype(bf16)


def cut(weight, place, chunks, pieces, half):
    tall = half // (chunks * pieces)
    at = jnp.stack([place, jnp.int32(weight.shape[0]), jnp.int32(weight.shape[1])]).astype(jnp.int32)
    return pl.pallas_call(
        functools.partial(cut_kernel, pieces),
        grid_spec=pltpu.PrefetchScalarGridSpec(
            num_scalar_prefetch=1,
            grid=(chunks,),
            in_specs=[pl.BlockSpec((tall, half), lambda j, at: (j * pieces + at[0], 0))],
            out_specs=pl.BlockSpec((tall, half), lambda j, at: (j, 0)),
        ),
        out_shape=jax.ShapeDtypeStruct((chunks * tall, half), bf16),
        compiler_params=params(),
        name="cut",
    )(at, weight)


def project_kernel(parts, halves, add, nb, *refs):
    xs = refs[:parts]
    ws = [refs[parts * (1 + h) : parts * (2 + h)] for h in range(halves)]
    refs = refs[parts * (1 + halves) :]
    proj, sums = refs[-2:]
    j = pl.program_id(0)

    def go(weights):
        acc = sum(dot(x[...], w[...], ((1,), (0,))) for x, w in zip(xs, weights))
        if add:
            acc = acc + jnp.concatenate([refs[0][k] for k in range(BLOCK // LANES)], axis=1)
        for k in range(BLOCK // LANES):
            proj[k] = acc[:, k * LANES : (k + 1) * LANES]
        sums[0:1, :] = jnp.sum(acc, axis=0, keepdims=True)
        sums[1:2, :] = jnp.sum(acc * acc, axis=0, keepdims=True)

    for h in range(halves):
        pl.when((j >= h * nb) & (j < (h + 1) * nb))(functools.partial(go, ws[h]))


def project(xs, ws, tiles, first=0, before=None, add=False):
    rows = xs[0][0].shape[0]
    half = ws[0][0].shape[1]
    nb = half // BLOCK
    specs, operands = [], []
    for x, at, depth in xs:
        specs.append(pl.BlockSpec((rows, depth), lambda j, at=at: (0, at), pipeline_mode=pl.Buffered(1)))
        operands.append(x)
    for h, weights in enumerate(ws):
        for w, (_, _, depth) in zip(weights, xs):
            specs.append(pl.BlockSpec((depth, BLOCK), lambda j, h=h: (0, held(j, h * nb, nb))))
            operands.append(w)
    tile_spec = pl.BlockSpec((BLOCK // LANES, rows, LANES), lambda j: (j + first, 0, 0))
    aliases = {}
    if before is not None:
        aliases = {len(operands): 0}
        operands.append(before)
        specs.append(tile_spec if add else pl.BlockSpec(memory_space=pl.ANY))
    width = len(ws) * half
    return pl.pallas_call(
        functools.partial(project_kernel, len(xs), len(ws), add, nb),
        grid=(len(ws) * nb,),
        in_specs=specs,
        out_specs=[tile_spec, pl.BlockSpec((2, BLOCK), lambda j: (0, j))],
        out_shape=[
            jax.ShapeDtypeStruct((tiles, rows, LANES), f32),
            jax.ShapeDtypeStruct((2, width), f32),
        ],
        input_output_aliases=aliases,
        compiler_params=params(),
        name="project",
    )(*operands)


def stats_of(sums, gains, count, j):
    mean = sums[0:1, tile_of(j)] / count
    var = sums[1:2, tile_of(j)] / count - mean * mean
    scale = lax.rsqrt(var + norm_eps)
    return mean, scale


def clear_pads(steps, seqs, array):
    tiles, rows, _ = array.shape
    pitch = rows // seqs
    if pitch > steps:
        for j in range(tiles):
            for s in range(seqs):
                array[j, s * pitch + steps : (s + 1) * pitch, :] = jnp.zeros((pitch - steps, LANES), f32)


def run_forward(steps, seqs, tiles, norm, gains, states, slopes):
    recur = [jnp.broadcast_to(gains[2:3, tile_of(j)], (seqs, LANES)) for j in range(tiles)]
    pitch = norm.shape[1] // seqs

    def advance(t, before):
        now = []
        at = pl.ds(t, seqs, stride=pitch)
        for j in range(tiles):
            arg = norm[j, at, :] + recur[j] * before[j]
            poly = gelu_inner * (arg * arg) + gelu_outer
            tanh = jnp.tanh(arg * poly)
            half = 0.5 * arg
            state = half + half * tanh
            states[j, at, :] = state
            inner = 3.0 * poly - 2.0 * gelu_outer
            slopes[j, at, :] = (0.5 * tanh + 0.5) + half * (1.0 - tanh * tanh) * inner
            now.append(state)
        return tuple(now)

    unroll = 2 if steps % 2 == 0 else 1

    def several(i, before):
        for k in range(unroll):
            before = advance(i * unroll + k, before)
        return before

    zero = jnp.zeros((seqs, LANES), f32)
    lax.fori_loop(0, steps // unroll, several, (zero,) * tiles)
    clear_pads(steps, seqs, states)


def run_backward(steps, seqs, tiles, grads, gains, slopes, arg_grads):
    recur = [jnp.broadcast_to(gains[2:3, tile_of(j)], (seqs, LANES)) for j in range(tiles)]
    pitch = arg_grads.shape[1] // seqs

    def retreat(t, after):
        now = []
        at = pl.ds(t, seqs, stride=pitch)
        for j in range(tiles):
            grad = (grads[j, at, :] + recur[j] * after[j]) * slopes[j, at, :]
            arg_grads[j, at, :] = grad
            now.append(grad)
        return tuple(now)

    unroll = 2 if steps % 2 == 0 else 1

    def several(i, after):
        for k in range(unroll):
            after = retreat(steps - 1 - (i * unroll + k), after)
        return after

    zero = jnp.zeros((seqs, LANES), f32)
    lax.fori_loop(0, steps // unroll, several, (zero,) * tiles)
    clear_pads(steps, seqs, arg_grads)


def back_sums(tiles, arg_grads, proj, states, sums, gains, count, out):
    rows = proj.shape[1]
    for j in range(tiles):
        mean, scale = stats_of(sums, gains, count, j)
        grad = arg_grads[j]
        out[0:1, tile_of(j)] = scale * jnp.sum(grad * (proj[j] - mean), axis=0, keepdims=True)
        out[1:2, tile_of(j)] = jnp.sum(grad, axis=0, keepdims=True)
        out[2:3, tile_of(j)] = jnp.sum(
            arg_grads[j, 1:rows, :] * states[j, 0 : rows - 1, :], axis=0, keepdims=True
        )


def make_norm(tiles, proj, sums, gains, count, norm):
    for j in range(tiles):
        mean, scale = stats_of(sums, gains, count, j)
        norm[j] = (proj[j] - mean) * (gains[0:1, tile_of(j)] * scale) + gains[1:2, tile_of(j)]


def first_layer_kernel(steps, seqs, count, proj, sums, gains, hidden, slopes, totals, norm, states):
    tiles = proj.shape[0]
    make_norm(tiles, proj, sums, gains, count, norm)
    run_forward(steps, seqs, tiles, norm, gains, states, slopes)
    for j in range(tiles):
        hidden[:, tile_of(j)] = states[j].astype(bf16)
        totals[0:1, tile_of(j)] = jnp.sum(states[j], axis=0, keepdims=True)


def first_layer(steps, seqs, count, proj, sums, gains):
    tiles, rows, _ = proj.shape
    return pl.pallas_call(
        functools.partial(first_layer_kernel, steps, seqs, count),
        out_shape=[
            jax.ShapeDtypeStruct((rows, tiles * LANES), bf16),
            jax.ShapeDtypeStruct((tiles, rows, LANES), f32),
            jax.ShapeDtypeStruct((1, tiles * LANES), f32),
        ],
        scratch_shapes=[pltpu.VMEM((tiles, rows, LANES), f32)] * 2,
        compiler_params=params(),
        name="first_layer",
    )(proj, sums, gains)


def second_layer_kernel(
    steps, seqs, count, proj, sums, gains, cot_near, cot_far, near, far, arg_grads, out, norm, states, slopes
):
    tiles = proj.shape[0]
    make_norm(tiles, proj, sums, gains, count, norm)
    run_forward(steps, seqs, tiles, norm, gains, states, slopes)
    half = tiles // 2
    for j in range(half):
        near[:, tile_of(j)] = states[j]
        far[:, tile_of(j)] = states[half + j].astype(bf16)
        norm[j] = cot_near[:, tile_of(j)].astype(f32)
        norm[half + j] = cot_far[:, tile_of(j)].astype(f32)
    run_backward(steps, seqs, tiles, norm, gains, slopes, arg_grads)
    back_sums(tiles, arg_grads, proj, states, sums, gains, count, out)


def second_layer(steps, seqs, count, proj, sums, gains, cot_near, cot_far):
    tiles, rows, _ = proj.shape
    width = tiles * LANES
    return pl.pallas_call(
        functools.partial(second_layer_kernel, steps, seqs, count),
        out_shape=[
            jax.ShapeDtypeStruct((rows, width // 2), f32),
            jax.ShapeDtypeStruct((rows, width // 2), bf16),
            jax.ShapeDtypeStruct((tiles, rows, LANES), f32),
            jax.ShapeDtypeStruct((3, width), f32),
        ],
        scratch_shapes=[pltpu.VMEM((tiles, rows, LANES), f32)] * 3,
        compiler_params=params(),
        name="second_layer",
    )(proj, sums, gains, cot_near, cot_far)


def norm_back(steps, pitch, arg_grads, proj, sums, gains, totals, count, out, columns):
    tiles, rows, _ = proj.shape
    row = lax.broadcasted_iota(jnp.int32, (rows, LANES), 0)
    inside = lax.rem(row, pitch) < steps
    for j in range(tiles):
        mean, scale = stats_of(sums, gains, count, j)
        factor = gains[0:1, tile_of(j)] * scale
        shift_part = totals[1:2, tile_of(j)] / count
        unit_part = scale * totals[0:1, tile_of(j)] / count
        grad = factor * (arg_grads[j] - shift_part - (proj[j] - mean) * unit_part)
        low = jnp.where(inside, grad, 0.0).astype(bf16).astype(f32)
        column = jnp.sum(low, axis=0, keepdims=True)
        high_part = column.astype(bf16).astype(f32)
        low_part = (column - high_part).astype(bf16).astype(f32)
        columns[0:1, tile_of(j)] = high_part + low_part
        low = jnp.where(row == steps, high_part, jnp.where(row == steps + 1, low_part, low))
        out[:, tile_of(j)] = low.astype(bf16)


def pull_kernel(steps, pitch, count, nb, tiled, arg_grads, proj, sums, gains, totals, w_nn, w_nf, w_fn, w_ff, low, columns, *outs):
    j = pl.program_id(0)
    half = w_nn.shape[1]

    @pl.when(j == 0)
    def _():
        norm_back(steps, pitch, arg_grads, proj, sums, gains, totals, count, low, columns)

    def go(left, right):
        return dot(low[:, :half], left[...], ((1,), (1,))) + dot(low[:, half:], right[...], ((1,), (1,)))

    if tiled:
        (out,) = outs

        def put(acc):
            for k in range(BLOCK // LANES):
                out[k] = acc[:, k * LANES : (k + 1) * LANES]

        pl.when(j < nb)(lambda: put(go(w_nn, w_nf)))
        pl.when(j >= nb)(lambda: put(go(w_fn, w_ff)))
    else:
        near, far = outs

        @pl.when(j < nb)
        def _():
            far[...] = go(w_fn, w_ff).astype(bf16)

        @pl.when(j >= nb)
        def _():
            near[...] = go(w_nn, w_nf)


def pull(steps, seqs, count, arg_grads, proj, sums, gains, totals, quarters, tiled):
    tiles, rows, _ = proj.shape
    width = tiles * LANES
    half = width // 2
    nb = half // BLOCK
    near_low, far_low = (0, nb) if tiled else (nb, 0)
    near_spec = pl.BlockSpec((BLOCK, half), lambda j: (held(j, near_low, nb), 0))
    far_spec = pl.BlockSpec((BLOCK, half), lambda j: (held(j, far_low, nb), 0))
    specs = [pl.BlockSpec((rows, width), lambda j: (0, 0)), pl.BlockSpec((1, width), lambda j: (0, 0))]
    shapes = [jax.ShapeDtypeStruct((rows, width), bf16), jax.ShapeDtypeStruct((1, width), f32)]
    if tiled:
        specs += [pl.BlockSpec((BLOCK // LANES, rows, LANES), lambda j: (j, 0, 0))]
        shapes += [jax.ShapeDtypeStruct((tiles, rows, LANES), f32)]
    else:
        specs += [
            pl.BlockSpec((rows, BLOCK), lambda j: (0, held(j, near_low, nb))),
            pl.BlockSpec((rows, BLOCK), lambda j: (0, held(j, far_low, nb))),
        ]
        shapes += [jax.ShapeDtypeStruct((rows, half), f32), jax.ShapeDtypeStruct((rows, half), bf16)]
    return pl.pallas_call(
        functools.partial(pull_kernel, steps, rows // seqs, count, nb, tiled),
        grid=(2 * nb,),
        in_specs=[
            whole((tiles, rows, LANES)),
            whole((tiles, rows, LANES)),
            whole((2, width)),
            whole((3, width)),
            whole((3, width)),
            near_spec,
            near_spec,
            far_spec,
            far_spec,
        ],
        out_specs=specs,
        out_shape=shapes,
        compiler_params=params(),
        name="pull",
    )(arg_grads, proj, sums, gains, totals, *quarters)


def first_back_kernel(steps, seqs, count, grads, slopes, hidden, proj, sums, gains, arg_grads, out, states):
    tiles = proj.shape[0]
    run_backward(steps, seqs, tiles, grads, gains, slopes, arg_grads)
    for j in range(tiles):
        states[j] = hidden[:, tile_of(j)].astype(f32)
    back_sums(tiles, arg_grads, proj, states, sums, gains, count, out)


def first_back(steps, seqs, count, grads, slopes, hidden, proj, sums, gains):
    tiles, rows, _ = proj.shape
    return pl.pallas_call(
        functools.partial(first_back_kernel, steps, seqs, count),
        out_shape=[
            jax.ShapeDtypeStruct((tiles, rows, LANES), f32),
            jax.ShapeDtypeStruct((3, tiles * LANES), f32),
        ],
        scratch_shapes=[pltpu.VMEM((tiles, rows, LANES), f32)],
        compiler_params=params(),
        name="first_back",
    )(grads, slopes, hidden, proj, sums, gains)


def weight_kernel(steps, parts, centred, *refs):
    xs, refs = refs[: len(parts)], refs[len(parts) :]
    if centred:
        centre, *refs = refs
    low, q_nn, q_nf, q_fn, q_ff = refs
    half = low.shape[1] // 2
    j = pl.program_id(0)
    total = sum(parts)

    def go(x, left, right):
        value = x[...]
        if centred:
            row = lax.broadcasted_iota(jnp.int32, value.shape, 0)
            minus = jnp.broadcast_to(-centre[...], value.shape)
            value = jnp.where((row == steps) | (row == steps + 1), minus, value.astype(f32)).astype(bf16)
        acc = dot(value, low[...], ((0,), (0,)))
        left[...] = acc[:, :half].astype(left.dtype)
        right[...] = acc[:, half:].astype(right.dtype)

    start = 0
    for x, blocks in zip(xs, parts):
        outs = (q_nn, q_nf) if start < total // 2 else (q_fn, q_ff)
        pl.when((j >= start) & (j < start + blocks))(functools.partial(go, x, *outs))
        start += blocks


def weight_grad(steps, xs, low, centre=None):
    rows, width = low.shape
    half = width // 2
    nb = half // BLOCK
    specs, start = [], 0
    for _, first, blocks in xs:
        specs.append(
            pl.BlockSpec((rows, BLOCK), lambda j, start=start, first=first, blocks=blocks: (0, first + held(j, start, blocks)))
        )
        start += blocks
    operands = [x for x, _, _ in xs]
    if centre is not None:
        specs.append(pl.BlockSpec((1, BLOCK), lambda j: (0, j)))
        operands.append(centre)
    first = pl.BlockSpec((BLOCK, half), lambda j: (held(j, 0, nb), 0))
    second = pl.BlockSpec((BLOCK, half), lambda j: (held(j, nb, nb), 0))
    return pl.pallas_call(
        functools.partial(weight_kernel, steps, [b for _, _, b in xs], centre is not None),
        grid=(2 * nb,),
        in_specs=specs + [whole((rows, width))],
        out_specs=[first, first, second, second],
        out_shape=[jax.ShapeDtypeStruct((half, half), bf16)] * 4,
        compiler_params=params(),
        name="weight_grad",
    )(*operands, low)


def over(value, axis):
    return lax.ppermute(value, axis, [(0, 1), (1, 0)])


def across(value, bit):
    size = lax.axis_size("dp")
    return lax.ppermute(value, "dp", [(i, i ^ bit) for i in range(size)])


def dp_bits():
    return [1 << k for k in range((lax.axis_size("dp") - 1).bit_length())]


def swap_halves(value):
    half = value.shape[-1] // 2
    return jnp.concatenate([value[:, half:], value[:, :half]], axis=1)


def sum_step(value, step, swaps):
    if step not in ("col", "row"):
        return value + across(value, step)
    other = over(value, step)
    rows = [swap_halves(other[k : k + 1]) if axis == step else other[k : k + 1] for k, axis in enumerate(swaps)]
    return value + jnp.concatenate(rows, axis=0)


def join(place, bit, own, other):
    mine = (place // bit) % 2
    return jnp.where(mine == 0, jnp.concatenate([own, other], axis=0), jnp.concatenate([other, own], axis=0))


def gather_dp(piece, bits):
    place = lax.axis_index("dp")
    for bit in bits:
        piece = join(place, bit, piece, across(piece, bit))
    return piece


def halve_dp(total, bit):
    mine = (lax.axis_index("dp") // bit) % 2
    half = total.shape[0] // 2
    kept = lax.dynamic_slice_in_dim(total, mine * half, half, 0)
    sent = lax.dynamic_slice_in_dim(total, (1 - mine) * half, half, 0)
    return kept + across(sent.astype(bf16), bit).astype(f32)


def reduce_row_first(own, other):
    total = own + over(other.astype(bf16), "row").astype(f32)
    for bit in dp_bits():
        total = halve_dp(total, bit)
    return gather_dp(total.astype(bf16), reversed(dp_bits()))


def reduce_row_last(own, other):
    for bit in dp_bits():
        own, other = halve_dp(own, bit), halve_dp(other, bit)
    total = own + over(other.astype(bf16), "row").astype(f32)
    return gather_dp(total.astype(bf16), reversed(dp_bits()))


def on_device(
    inputs,
    w_second,
    gain_second,
    shift_second,
    recur_second,
    w_third,
    gain_third,
    shift_third,
    recur_third,
    cotangent,
):
    steps, seq_group, width = inputs.shape
    share = cotangent.shape[1]
    seqs = share // lax.axis_size("row")
    pitch = round_up(steps + 2, 8)
    rows = seqs * pitch
    half = round_up(width, 2 * BLOCK)
    nb = half // BLOCK
    tiles = 2 * half // LANES
    pieces = lax.axis_size("dp")
    count = steps * seq_group * pieces
    row, col, place = lax.axis_index("row"), lax.axis_index("col"), lax.axis_index("dp")
    bits = dp_bits()
    turned = sum(((place // bit) % 2) * (pieces // 2 // bit) for bit in bits)

    def pad_weight(w):
        return jnp.pad(w, ((0, half - w.shape[0]), (0, half - w.shape[1])))

    def pad_params(*vectors):
        return jnp.pad(jnp.stack(vectors), ((0, 0), (0, half - width)))

    chunks = 2
    spread = half // (chunks * pieces) >= 16
    if spread:
        cut_second = cut(w_second, turned, chunks, pieces, half)
        cut_third = cut(w_third, turned, 1, pieces, half)
        tall = half // (chunks * pieces)
        far_second = [over(cut_second[k * tall : (k + 1) * tall], "row") for k in range(chunks)]
        far_third = over(cut_third, "row")

    places = jnp.stack([col * share + row * seqs, col * share + (1 - row) * seqs]).astype(jnp.int32)
    parts = jnp.stack([row, 1 - row]).astype(jnp.int32)
    x_near, send0 = prep(inputs, places, seqs, pitch, half, 0, nb // 2)
    x_far0 = over(send0, "row")
    x_near, send1 = prep(inputs, places, seqs, pitch, half, nb // 2, nb // 2, x_near)
    x_far1 = over(send1, "row")

    nn2 = pad_weight(w_second)
    nf2 = over(nn2, "col")
    own_second = pad_params(gain_second, shift_second, recur_second)
    own_third = pad_params(gain_third, shift_third, recur_third)
    gains_second = jnp.concatenate([own_second, over(own_second, "col")], axis=1)
    nn3 = pad_weight(w_third)
    fn3 = over(nn3, "col")
    if spread:
        fn2 = [gather_dp(piece, reversed(bits)) for piece in far_second]
        nf3 = gather_dp(far_third, reversed(bits[1:]))
    else:
        far = over(nn2, "row")
        fn2 = [far[: half // 2], far[half // 2 :]]
        nf3 = over(nn3, "row")
    ff2 = [over(chunk, "col") for chunk in fn2]

    proj_second, _ = project([(x_near, 0, half)], [[nn2], [nf2]], tiles)
    proj_second, _ = project([(x_far0, 0, half // 2)], [[fn2[0]], [ff2[0]]], tiles, 0, proj_second, True)
    proj_second, sums = project([(x_far1, 0, half // 2)], [[fn2[1]], [ff2[1]]], tiles, 0, proj_second, True)

    swaps = ("col", "col")
    sums = sum_step(sums, "col", swaps)
    sums = sum_step(sums, "row", swaps)
    grads = tie(jnp.transpose(cotangent, (1, 0, 2)), sums)
    cot_near, cot_send = prep_grads(grads, parts, seqs, pitch, half)
    cot_far = over(cot_send, "row")
    sums = sum_step(sums, bits[0], swaps) if bits else sums
    if spread and bits:
        nf3 = gather_dp(tie(nf3, sums), bits[:1])
    for bit in bits[1:]:
        sums = sum_step(sums, bit, swaps)
    sums_second = sums
    ff3 = over(nf3, "col")
    gains_third = jnp.concatenate([own_third, over(own_third, "row")], axis=1)
    hidden, slopes_second, hidden_sums = first_layer(steps, seqs, count, proj_second, sums_second, gains_second)
    hidden_parts = [(hidden, 0, half), (hidden, 1, half)]
    proj_third, sums_near = project(hidden_parts, [[nn3, fn3]], tiles)
    proj_third, sums_far = project(hidden_parts, [[nf3, ff3]], tiles, nb, proj_third)

    swaps = ("row", "row", "col")
    sums = jnp.concatenate([jnp.concatenate([sums_near, sums_far], axis=1), hidden_sums], axis=0)
    for step in ("col", *bits, "row"):
        sums = sum_step(sums, step, swaps)
    sums_third, centre = sums[:2], (sums[2:3] / count).astype(bf16).astype(f32)
    states_near, states_far, arg_grads_third, sums = second_layer(
        steps, seqs, count, proj_third, sums_third, gains_third, cot_near, cot_far
    )
    swaps = ("row", "row", "row")
    sums = sum_step(sums, "col", swaps)
    sums = sum_step(sums, "row", swaps)
    states_far = over(tie(states_far, sums), "row")
    for bit in bits:
        sums = sum_step(sums, bit, swaps)
    totals_third = sums
    low_third, columns, grad_hidden = pull(
        steps, seqs, count, arg_grads_third, proj_third, sums_third, gains_third, totals_third, [nn3, nf3, fn3, ff3], True
    )
    nn, nf, fn, ff = weight_grad(steps, [(hidden, 0, nb), (hidden, nb, nb)], low_third, centre)
    own3 = nn.astype(f32) + over(fn, "col").astype(f32)
    other3 = nf.astype(f32) + over(ff, "col").astype(f32)
    arg_grads_second, sums = first_back(
        steps, seqs, count, grad_hidden, slopes_second, hidden, proj_second, sums_second, gains_second
    )
    swaps = ("col", "col", "col", "row")
    sums = jnp.concatenate([sums, columns], axis=0)
    for step in ("col", *bits, "row"):
        sums = sum_step(sums, step, swaps)
    totals_second, columns = sums[:3], sums[3:4]
    grad_w_third = reduce_row_last(tie(own3, sums), tie(other3, sums))
    low_second, _, grad_near, grad_far = pull(
        steps,
        seqs,
        count,
        arg_grads_second,
        proj_second,
        sums_second,
        gains_second,
        totals_second,
        [nn2, nf2, jnp.concatenate(fn2, axis=0), jnp.concatenate(ff2, axis=0)],
        False,
    )
    grad_far = over(grad_far, "row")
    nn, nf, fn, ff = weight_grad(
        steps, [(x_near, 0, nb), (x_far0, 0, nb // 2), (x_far1, 0, nb // 2)], low_second
    )
    own2 = nn.astype(f32) + over(nf, "col").astype(f32)
    other2 = fn.astype(f32) + over(ff, "col").astype(f32)
    grad_w_second = reduce_row_last(own2, other2)

    output = combine(parts, x_near, states_near, (send0, send1), states_far, seqs, steps, width)
    grad_inputs = combine(parts, cot_near, grad_near, (cot_send, cot_send), grad_far, seqs, steps, width)
    output = jnp.transpose(output, (1, 0, 2))
    grad_inputs = jnp.transpose(grad_inputs, (1, 0, 2))
    restore = centre[0, :width, None] * columns[0, None, :width]
    return (
        output,
        grad_inputs,
        grad_w_second[:width, :width].astype(f32),
        totals_second[0, :width],
        totals_second[1, :width],
        totals_second[2, :width],
        grad_w_third[:width, :width].astype(f32) + restore,
        totals_third[0, :width],
        totals_third[1, :width],
        totals_third[2, :width],
    )


def solution(mesh):
    in_specs = (
        P(None, "dp", "row"),
        P("row", "col"),
        P("col"),
        P("col"),
        P("col"),
        P("col", "row"),
        P("row"),
        P("row"),
        P("row"),
        P(None, ("dp", "col"), "row"),
    )
    out_specs = (
        P(None, ("dp", "col"), "row"),
        P(None, ("dp", "col"), "row"),
        P("row", "col"),
        P("col"),
        P("col"),
        P("col"),
        P("col", "row"),
        P("row"),
        P("row"),
        P("row"),
    )
    return jax.shard_map(
        on_device, mesh=mesh, in_specs=in_specs, out_specs=out_specs, check_vma=False
    )
```

```python
import functools

import jax
import jax.numpy as jnp
from jax import lax
from jax.experimental import pallas as pl
from jax.experimental.pallas import tpu as pltpu
from jax.sharding import PartitionSpec as P

norm_eps = 1e-05
gelu_outer = 0.7978845608028654
gelu_inner = gelu_outer * 0.044715
LANES = 128
BLOCK = 256
WIDE = 512
f32 = jnp.float32
bf16 = jnp.bfloat16


def params(mebibytes=56):
    return pltpu.CompilerParams(vmem_limit_bytes=mebibytes * 2**20)


def cost(microseconds):
    return pl.CostEstimate(flops=0, bytes_accessed=int(microseconds * 3_690), transcendentals=0)


def round_up(value, unit):
    return -(-value // unit) * unit


def after(deps):
    return [pl.BlockSpec(memory_space=pl.ANY)] * len(deps)


def without(kernel, at, count, token=None):
    def body(*refs):
        refs = list(refs)
        if token is not None:
            refs.pop(token)[...] = jnp.zeros((8, LANES), f32)
        kernel(*refs[:at], *refs[at + count :])

    return body


token_spec = pl.BlockSpec((8, LANES), lambda *_: (0, 0))
token_shape = jax.ShapeDtypeStruct((8, LANES), f32)


def whole(shape):
    return pl.BlockSpec(shape, lambda *_: (0,) * len(shape), pipeline_mode=pl.Buffered(1))


def dot(left, right, dims):
    return lax.dot_general(left, right, (dims, ((), ())), preferred_element_type=f32)


def tile_of(j):
    return pl.ds(j * LANES, LANES)


def held(j, low, count):
    return jnp.clip(j - low, 0, count - 1)


def prep_kernel(seqs, pitch, width, base, at_ref, inputs, *refs):
    near, send, scratch, packed = refs[-4:]
    steps, group, block = inputs.shape
    lane = base + pl.program_id(0) * block + lax.broadcasted_iota(jnp.int32, (1, LANES), 1)
    rows = near.shape[0]
    for k in range(block // LANES):
        scratch[...] = inputs[:, :, tile_of(k)].astype(f32).reshape(steps * group, LANES)
        for place, out in ((0, near), (1, send)):
            first = at_ref[place]
            for s in range(seqs):
                packed[s * pitch : s * pitch + steps, :] = scratch[pl.ds(first + s, steps, stride=group), :]
                packed[s * pitch + steps : (s + 1) * pitch, :] = jnp.zeros((pitch - steps, LANES), f32)
            out[:, tile_of(k)] = jnp.where(lane + k * LANES < width, packed[...], 0.0).astype(bf16)


def prep(inputs, places, seqs, pitch, half, first, blocks, near=None, deps=()):
    steps, group, width = inputs.shape
    rows = seqs * pitch
    near_spec = pl.BlockSpec((rows, BLOCK), lambda j, at: (0, j + first))
    return pl.pallas_call(
        without(functools.partial(prep_kernel, seqs, pitch, width, first * BLOCK), 2, len(deps)),
        grid_spec=pltpu.PrefetchScalarGridSpec(
            num_scalar_prefetch=1,
            grid=(blocks,),
            in_specs=[pl.BlockSpec((steps, group, BLOCK), lambda j, at: (0, 0, j + first))]
            + after(deps)
            + ([] if near is None else [pl.BlockSpec(memory_space=pl.ANY)]),
            out_specs=[near_spec, pl.BlockSpec((rows, BLOCK), lambda j, at: (0, j))],
            scratch_shapes=[pltpu.VMEM((steps * group, LANES), f32), pltpu.VMEM((rows, LANES), f32)],
        ),
        out_shape=[
            jax.ShapeDtypeStruct((rows, half), bf16),
            jax.ShapeDtypeStruct((rows, blocks * BLOCK), bf16),
        ],
        input_output_aliases={} if near is None else {2 + len(deps): 0},
        compiler_params=params(),
        cost_estimate=cost(4.6),
        name="prep",
    )(places, inputs, *deps, *(() if near is None else (near,)))


def prep_grads_kernel(pitch, width, at_ref, own, other, near, send, packed):
    seqs, steps, block = own.shape
    lane = pl.program_id(0) * block + lax.broadcasted_iota(jnp.int32, (1, block), 1)
    for part, out in ((own, near), (other, send)):
        for s in range(seqs):
            packed[s * pitch : s * pitch + steps, :] = part[s].astype(f32)
            packed[s * pitch + steps : (s + 1) * pitch, :] = jnp.zeros((pitch - steps, block), f32)
        out[...] = jnp.where(lane < width, packed[...], 0.0).astype(bf16)


def prep_grads(grads, places, seqs, pitch, half):
    _, steps, width = grads.shape
    rows = seqs * pitch
    out = pl.BlockSpec((rows, BLOCK), lambda j, at: (0, j))
    return pl.pallas_call(
        without(functools.partial(prep_grads_kernel, pitch, width), 0, 0, -2),
        grid_spec=pltpu.PrefetchScalarGridSpec(
            num_scalar_prefetch=1,
            grid=(half // BLOCK,),
            in_specs=[
                pl.BlockSpec((seqs, steps, BLOCK), lambda j, at: (at[0], 0, j)),
                pl.BlockSpec((seqs, steps, BLOCK), lambda j, at: (at[1], 0, j)),
            ],
            out_specs=[out, out, token_spec],
            scratch_shapes=[pltpu.VMEM((rows, BLOCK), f32)],
        ),
        out_shape=[jax.ShapeDtypeStruct((rows, half), bf16)] * 2 + [token_shape],
        compiler_params=params(),
        cost_estimate=cost(5.4),
        name="prep_grads",
    )(places, grads, grads)


def combine_kernel(pitch, at_ref, *refs):
    *parts, out = refs
    seqs, steps, width = out.shape

    def put(halves, b):
        total = jnp.concatenate([part[...].astype(f32) for part in halves], axis=1) + b[...].astype(f32)
        for s in range(seqs):
            out[s] = total[s * pitch : s * pitch + steps, :width]

    near, b_near, *far, b_far = parts
    pl.when(pl.program_id(0) == 0)(lambda: put([near], b_near))
    pl.when(pl.program_id(0) == 1)(lambda: put(far, b_far))


def combine(places, a_near, b_near, a_far, b_far, seqs, steps, width, deps=()):
    rows = a_near.shape[0]
    pitch = rows // seqs
    group = 2 if seqs % 2 == 0 and 2 * pitch % 16 == 0 else seqs
    nb = seqs // group
    near_at = lambda p, j, at: (jnp.where(p == 0, j, nb - 1), 0)
    far_at = lambda p, j, at: (jnp.where(p == 0, 0, j), 0)
    operands = [a_near, b_near, *a_far, b_far]
    specs = [pl.BlockSpec((group * pitch, x.shape[1]), near_at if k < 2 else far_at) for k, x in enumerate(operands)]
    return pl.pallas_call(
        without(functools.partial(combine_kernel, pitch), 1 + len(operands), len(deps), -1),
        grid_spec=pltpu.PrefetchScalarGridSpec(
            num_scalar_prefetch=1,
            grid=(2, nb),
            in_specs=specs + after(deps),
            out_specs=[pl.BlockSpec((group, steps, width), lambda p, j, at: (at[p] * nb + j, 0, 0)), token_spec],
        ),
        out_shape=[jax.ShapeDtypeStruct((2 * seqs, steps, width), f32), token_shape],
        compiler_params=params(24),
        cost_estimate=cost(6),
        name="combine",
    )(places, *operands, *deps)


def cut_kernel(pieces, chunks, limit, at_ref, second, third, out_second, out_third):
    tall, wide = out_second.shape
    j = pl.program_id(0)
    lane = lax.broadcasted_iota(jnp.int32, (tall, wide), 1)
    for block, weight, out in ((j * pieces + at_ref[0], second, out_second), (at_ref[0] * chunks + j, third, out_third)):
        row = block * tall + lax.broadcasted_iota(jnp.int32, (tall, wide), 0)
        out[...] = jnp.where((row < limit) & (lane < limit), weight[...].astype(f32), 0.0).astype(bf16)


def cut(second, third, place, chunks, pieces, half):
    tall = half // (chunks * pieces)
    out_spec = pl.BlockSpec((tall, half), lambda j, at: (j, 0))
    return pl.pallas_call(
        functools.partial(cut_kernel, pieces, chunks, second.shape[0]),
        grid_spec=pltpu.PrefetchScalarGridSpec(
            num_scalar_prefetch=1,
            grid=(chunks,),
            in_specs=[
                pl.BlockSpec((tall, half), lambda j, at: (j * pieces + at[0], 0)),
                pl.BlockSpec((tall, half), lambda j, at: (at[0] * chunks + j, 0)),
            ],
            out_specs=[out_spec, out_spec],
        ),
        out_shape=[jax.ShapeDtypeStruct((chunks * tall, half), bf16)] * 2,
        compiler_params=params(),
        cost_estimate=cost(2.5),
        name="cut",
    )(jnp.reshape(place, (1,)).astype(jnp.int32), second, third)


def project_kernel(parts, halves, add, nb, *refs):
    xs = refs[:parts]
    ws = [refs[parts * (1 + h) : parts * (2 + h)] for h in range(halves)]
    refs = refs[parts * (1 + halves) :]
    proj, sums = refs[-2:]
    j = pl.program_id(0)

    def go(weights):
        acc = sum(dot(x[...], w[...], ((1,), (0,))) for x, w in zip(xs, weights))
        if add:
            acc = acc + jnp.concatenate([refs[0][k] for k in range(WIDE // LANES)], axis=1)
        for k in range(WIDE // LANES):
            proj[k] = acc[:, k * LANES : (k + 1) * LANES]
        sums[0:1, :] = jnp.sum(acc, axis=0, keepdims=True)
        sums[1:2, :] = jnp.sum(acc * acc, axis=0, keepdims=True)

    for h in range(halves):
        pl.when((j >= h * nb) & (j < (h + 1) * nb))(functools.partial(go, ws[h]))


def project(xs, ws, tiles, first=0, before=None, add=False, deps=()):
    rows = xs[0][0].shape[0]
    half = ws[0][0].shape[1]
    nb = half // WIDE
    specs, operands = [], []
    for x, at, depth in xs:
        specs.append(pl.BlockSpec((rows, depth), lambda j, at=at: (0, at), pipeline_mode=pl.Buffered(1)))
        operands.append(x)
    for h, weights in enumerate(ws):
        for w, (_, _, depth) in zip(weights, xs):
            specs.append(pl.BlockSpec((depth, WIDE), lambda j, h=h: (0, held(j, h * nb, nb))))
            operands.append(w)
    tile_spec = pl.BlockSpec((WIDE // LANES, rows, LANES), lambda j: (j + first, 0, 0))
    aliases = {}
    if before is not None:
        aliases = {len(operands): 0}
        operands.append(before)
        specs.append(tile_spec if add else pl.BlockSpec(memory_space=pl.ANY))
    width = len(ws) * half
    kernel = functools.partial(project_kernel, len(xs), len(ws), add, nb)
    return pl.pallas_call(
        without(kernel, len(operands), len(deps)),
        grid=(len(ws) * nb,),
        in_specs=specs + after(deps),
        out_specs=[tile_spec, pl.BlockSpec((2, WIDE), lambda j: (0, j))],
        out_shape=[
            jax.ShapeDtypeStruct((tiles, rows, LANES), f32),
            jax.ShapeDtypeStruct((2, width), f32),
        ],
        input_output_aliases=aliases,
        compiler_params=params(),
        cost_estimate=cost(8),
        name="project",
    )(*operands, *deps)


def stats_of(sums, gains, count, j):
    mean = sums[0:1, tile_of(j)] / count
    var = sums[1:2, tile_of(j)] / count - mean * mean
    scale = lax.rsqrt(var + norm_eps)
    return mean, scale


def clear_pads(steps, seqs, array):
    tiles, rows, _ = array.shape
    pitch = rows // seqs
    if pitch > steps:
        for j in range(tiles):
            for s in range(seqs):
                array[j, s * pitch + steps : (s + 1) * pitch, :] = jnp.zeros((pitch - steps, LANES), f32)


def run_forward(steps, seqs, tiles, norm, gains, states, slopes):
    recur = [jnp.broadcast_to(gains[2:3, tile_of(j)], (seqs, LANES)) for j in range(tiles)]
    pitch = norm.shape[1] // seqs

    def advance(t, before):
        now = []
        at = pl.ds(t, seqs, stride=pitch)
        for j in range(tiles):
            arg = norm[j, at, :] + recur[j] * before[j]
            poly = gelu_inner * (arg * arg) + gelu_outer
            tanh = jnp.tanh(arg * poly)
            half = 0.5 * arg
            state = half + half * tanh
            states[j, at, :] = state
            inner = 3.0 * poly - 2.0 * gelu_outer
            slopes[j, at, :] = (0.5 * tanh + 0.5) + half * (1.0 - tanh * tanh) * inner
            now.append(state)
        return tuple(now)

    unroll = 2 if steps % 2 == 0 else 1

    def several(i, before):
        for k in range(unroll):
            before = advance(i * unroll + k, before)
        return before

    zero = jnp.zeros((seqs, LANES), f32)
    lax.fori_loop(0, steps // unroll, several, (zero,) * tiles)
    clear_pads(steps, seqs, states)


def run_backward(steps, seqs, tiles, grads, gains, slopes, arg_grads):
    recur = [jnp.broadcast_to(gains[2:3, tile_of(j)], (seqs, LANES)) for j in range(tiles)]
    pitch = arg_grads.shape[1] // seqs

    def retreat(t, after):
        now = []
        at = pl.ds(t, seqs, stride=pitch)
        for j in range(tiles):
            grad = (grads[j, at, :] + recur[j] * after[j]) * slopes[j, at, :]
            arg_grads[j, at, :] = grad
            now.append(grad)
        return tuple(now)

    unroll = 2 if steps % 2 == 0 else 1

    def several(i, after):
        for k in range(unroll):
            after = retreat(steps - 1 - (i * unroll + k), after)
        return after

    zero = jnp.zeros((seqs, LANES), f32)
    lax.fori_loop(0, steps // unroll, several, (zero,) * tiles)
    clear_pads(steps, seqs, arg_grads)


def back_sums(tiles, arg_grads, proj, states, sums, gains, count, out):
    rows = proj.shape[1]
    for j in range(tiles):
        mean, scale = stats_of(sums, gains, count, j)
        grad = arg_grads[j]
        out[0:1, tile_of(j)] = scale * jnp.sum(grad * (proj[j] - mean), axis=0, keepdims=True)
        out[1:2, tile_of(j)] = jnp.sum(grad, axis=0, keepdims=True)
        out[2:3, tile_of(j)] = jnp.sum(
            arg_grads[j, 1:rows, :] * states[j, 0 : rows - 1, :], axis=0, keepdims=True
        )


def make_norm(tiles, proj, sums, gains, count, norm):
    for j in range(tiles):
        mean, scale = stats_of(sums, gains, count, j)
        norm[j] = (proj[j] - mean) * (gains[0:1, tile_of(j)] * scale) + gains[1:2, tile_of(j)]


def first_layer_kernel(steps, seqs, count, proj, sums, gains, hidden, slopes, totals, norm, states):
    tiles = proj.shape[0]
    make_norm(tiles, proj, sums, gains, count, norm)
    run_forward(steps, seqs, tiles, norm, gains, states, slopes)
    for j in range(tiles):
        hidden[:, tile_of(j)] = states[j].astype(bf16)
        totals[0:1, tile_of(j)] = jnp.sum(states[j], axis=0, keepdims=True)


def first_layer(steps, seqs, count, proj, sums, gains):
    tiles, rows, _ = proj.shape
    return pl.pallas_call(
        functools.partial(first_layer_kernel, steps, seqs, count),
        out_shape=[
            jax.ShapeDtypeStruct((rows, tiles * LANES), bf16),
            jax.ShapeDtypeStruct((tiles, rows, LANES), f32),
            jax.ShapeDtypeStruct((1, tiles * LANES), f32),
        ],
        scratch_shapes=[pltpu.VMEM((tiles, rows, LANES), f32)] * 2,
        compiler_params=params(),
        cost_estimate=cost(16.5),
        name="first_layer",
    )(proj, sums, gains)


def second_layer_kernel(
    steps, seqs, count, proj, sums, gains, cot_near, cot_far, near, far, arg_grads, out, norm, states, slopes
):
    tiles = proj.shape[0]
    make_norm(tiles, proj, sums, gains, count, norm)
    run_forward(steps, seqs, tiles, norm, gains, states, slopes)
    half = tiles // 2
    for j in range(half):
        near[:, tile_of(j)] = states[j]
        far[:, tile_of(j)] = states[half + j].astype(bf16)
        norm[j] = cot_near[:, tile_of(j)].astype(f32)
        norm[half + j] = cot_far[:, tile_of(j)].astype(f32)
    run_backward(steps, seqs, tiles, norm, gains, slopes, arg_grads)
    back_sums(tiles, arg_grads, proj, states, sums, gains, count, out)


def second_layer(steps, seqs, count, proj, sums, gains, cot_near, cot_far):
    tiles, rows, _ = proj.shape
    width = tiles * LANES
    return pl.pallas_call(
        functools.partial(second_layer_kernel, steps, seqs, count),
        out_shape=[
            jax.ShapeDtypeStruct((rows, width // 2), f32),
            jax.ShapeDtypeStruct((rows, width // 2), bf16),
            jax.ShapeDtypeStruct((tiles, rows, LANES), f32),
            jax.ShapeDtypeStruct((3, width), f32),
        ],
        scratch_shapes=[pltpu.VMEM((tiles, rows, LANES), f32)] * 3,
        compiler_params=params(),
        cost_estimate=cost(25),
        name="second_layer",
    )(proj, sums, gains, cot_near, cot_far)


def norm_back(steps, pitch, arg_grads, proj, sums, gains, totals, count, low_ref, columns):
    tiles, rows, _ = proj.shape
    row = lax.broadcasted_iota(jnp.int32, (rows, LANES), 0)
    inside = lax.rem(row, pitch) < steps
    for j in range(tiles):
        mean, scale = stats_of(sums, gains, count, j)
        factor = gains[0:1, tile_of(j)] * scale
        shift_part = totals[1:2, tile_of(j)] / count
        unit_part = scale * totals[0:1, tile_of(j)] / count
        grad = factor * (arg_grads[j] - shift_part - (proj[j] - mean) * unit_part)
        low = jnp.where(inside, grad, 0.0).astype(bf16).astype(f32)
        column = jnp.sum(low, axis=0, keepdims=True)
        high_part = column.astype(bf16).astype(f32)
        low_part = (column - high_part).astype(bf16).astype(f32)
        columns[0:1, tile_of(j)] = high_part + low_part
        low = jnp.where(row == steps, high_part, jnp.where(row == steps + 1, low_part, low))
        low_ref[:, tile_of(j)] = low.astype(bf16)


def weight_kernel(steps, pitch, count, parts, centred, norm_steps, *refs):
    xs, refs = refs[: len(parts)], refs[len(parts) :]
    if centred:
        centre, *refs = refs
    j = pl.program_id(0)
    if norm_steps:
        arg_grads, proj, sums, gains, totals, low_out, columns, left, right, low = refs

        @pl.when(j < norm_steps)
        def _():
            norm_back(steps, pitch, arg_grads, proj, sums, gains, totals, count, low_out, columns)
            low[:, pl.ds(pl.multiple_of(j * BLOCK, BLOCK), BLOCK)] = low_out[...]
    else:
        low, left, right = refs
    half = low.shape[1] // 2

    def go(x):
        value = x[...]
        if centred:
            row = lax.broadcasted_iota(jnp.int32, value.shape, 0)
            minus = jnp.broadcast_to(-centre[...], value.shape)
            value = jnp.where((row == steps) | (row == steps + 1), minus, value.astype(f32)).astype(bf16)
        acc = dot(value, low[...], ((0,), (0,)))
        left[...] = acc[:, :half].astype(left.dtype)
        right[...] = acc[:, half:].astype(right.dtype)

    at = norm_steps
    for x, blocks in zip(xs, parts):
        pl.when((j >= at) & (j < at + blocks))(functools.partial(go, x))
        at += blocks


def weight_grad(steps, seqs, count, xs, grads, centre=None, centre_at=0, deps=()):
    rows = grads[0].shape[-2]
    made = len(grads) == 1
    width = grads[0].shape[1] if made else grads[0].shape[0] * LANES
    half = width // 2
    nb = half // WIDE
    norm_steps = 0 if made else width // BLOCK
    specs, start = [], norm_steps
    for _, first, blocks in xs:
        specs.append(
            pl.BlockSpec((rows, WIDE), lambda j, start=start, first=first, blocks=blocks: (0, first + held(j, start, blocks)))
        )
        start += blocks
    operands = [x for x, _, _ in xs]
    if centre is not None:
        specs.append(pl.BlockSpec((1, WIDE), lambda j: (0, centre_at + held(j, norm_steps, nb))))
        operands.append(centre)
    quarter = pl.BlockSpec((WIDE, half), lambda j: (held(j, norm_steps, nb), 0))
    out_specs, out_shape, scratch = [quarter] * 2, [jax.ShapeDtypeStruct((half, half), bf16)] * 2, []
    if made:
        specs.append(whole((rows, width)))
    else:
        tile_spec = pl.BlockSpec((BLOCK // LANES, rows, LANES), lambda j: (held(j, 0, norm_steps), 0, 0))
        lanes = lambda tall: pl.BlockSpec((tall, BLOCK), lambda j: (0, held(j, 0, norm_steps)))
        specs += [tile_spec, tile_spec, lanes(2), lanes(3), lanes(3)]
        out_specs = [lanes(rows), lanes(1)] + out_specs
        out_shape = [jax.ShapeDtypeStruct((rows, width), bf16), jax.ShapeDtypeStruct((1, width), f32)] + out_shape
        scratch = [pltpu.VMEM((rows, width), bf16)]
    kernel = functools.partial(
        weight_kernel, steps, rows // seqs, count, [b for _, _, b in xs], centre is not None, norm_steps
    )
    return pl.pallas_call(
        without(kernel, len(specs), len(deps), -1 - len(scratch)),
        grid=(norm_steps + nb,),
        in_specs=specs + after(deps),
        out_specs=out_specs + [token_spec],
        out_shape=out_shape + [token_shape],
        scratch_shapes=scratch,
        compiler_params=params(),
        cost_estimate=cost(8 if made else 16),
        name="weight_grad",
    )(*operands, *grads, *deps)


def pull_kernel(nb, tiled, low, *refs):
    *weights, out = refs
    j = pl.program_id(0)
    half = weights[0].shape[1]

    def go(left, right):
        acc = dot(low[:, :half], left[...], ((1,), (1,))) + dot(low[:, half:], right[...], ((1,), (1,)))
        if tiled:
            for k in range(WIDE // LANES):
                out[k] = acc[:, k * LANES : (k + 1) * LANES]
        else:
            out[...] = acc.astype(out.dtype)

    for k in range(len(weights) // 2):
        pl.when((j >= k * nb) & (j < (k + 1) * nb))(functools.partial(go, *weights[2 * k : 2 * k + 2]))


def pull(low, quarters, tiled, dtype, deps=()):
    rows, width = low.shape
    half = width // 2
    nb = half // WIDE
    halves = len(quarters) // 2
    specs = [pl.BlockSpec((WIDE, half), lambda j, k=k: (held(j, k // 2 * nb, nb), 0)) for k in range(2 * halves)]
    if tiled:
        out_spec = pl.BlockSpec((WIDE // LANES, rows, LANES), lambda j: (j, 0, 0))
        shape = (halves * half // LANES, rows, LANES)
    else:
        out_spec = pl.BlockSpec((rows, WIDE), lambda j: (0, j))
        shape = (rows, halves * half)
    return pl.pallas_call(
        without(functools.partial(pull_kernel, nb, tiled), 1 + len(quarters), len(deps), -1),
        grid=(halves * nb,),
        in_specs=[whole((rows, width))] + specs + after(deps),
        out_specs=[out_spec, token_spec],
        out_shape=[jax.ShapeDtypeStruct(shape, dtype), token_shape],
        compiler_params=params(),
        cost_estimate=cost(7 * halves),
        name="pull",
    )(low, *quarters, *deps)


def first_back_kernel(steps, seqs, count, grads, slopes, hidden, proj, sums, gains, arg_grads, out, states):
    tiles = proj.shape[0]
    run_backward(steps, seqs, tiles, grads, gains, slopes, arg_grads)
    for j in range(tiles):
        states[j] = hidden[:, tile_of(j)].astype(f32)
    back_sums(tiles, arg_grads, proj, states, sums, gains, count, out)


def first_back(steps, seqs, count, grads, slopes, hidden, proj, sums, gains, deps=()):
    tiles, rows, _ = proj.shape
    return pl.pallas_call(
        without(functools.partial(first_back_kernel, steps, seqs, count), 6, len(deps)),
        in_specs=[pl.BlockSpec(memory_space=pltpu.VMEM)] * 6 + after(deps),
        out_shape=[
            jax.ShapeDtypeStruct((tiles, rows, LANES), f32),
            jax.ShapeDtypeStruct((3, tiles * LANES), f32),
        ],
        scratch_shapes=[pltpu.VMEM((tiles, rows, LANES), f32)],
        compiler_params=params(),
        cost_estimate=cost(17),
        name="first_back",
    )(grads, slopes, hidden, proj, sums, gains, *deps)


def fold_kernel(counts, at_ref, *refs):
    kept, sent = refs[-2:]
    at = 0
    for k, n in enumerate(counts):
        parts = refs[at : at + 2 * n]
        kept[k] = sum(p[...].astype(f32) for p in parts[:n])
        sent[k] = sum(p[...].astype(f32) for p in parts[n:]).astype(bf16)
        at += 2 * n


def fold(mine, stacks, rows, deps=()):
    specs, operands = [], []
    width = stacks[0][0][0].shape[-1]
    lanes = width // 2
    for stack in stacks:
        for side in (0, 1):
            for array, index, base in stack:
                operands.append(array)
                specs.append(
                    pl.BlockSpec(
                        (None, rows, lanes),
                        lambda j, at, side=side, index=index, base=base: (index, base + (at[0] + side) % 2, j),
                    )
                )
    count = len(stacks)
    out_spec = pl.BlockSpec((count, rows, lanes), lambda j, at: (0, 0, j))
    kernel = functools.partial(fold_kernel, [len(stack) for stack in stacks])
    return pl.pallas_call(
        without(kernel, 1 + len(operands), len(deps), -1),
        grid_spec=pltpu.PrefetchScalarGridSpec(
            num_scalar_prefetch=1, grid=(2,), in_specs=specs + after(deps), out_specs=[out_spec, out_spec, token_spec]
        ),
        out_shape=[
            jax.ShapeDtypeStruct((count, rows, width), f32),
            jax.ShapeDtypeStruct((count, rows, width), bf16),
            token_shape,
        ],
        compiler_params=params(16),
        cost_estimate=cost(1.5),
        name="fold",
    )(jnp.reshape(mine, (1,)).astype(jnp.int32), *operands, *deps)


def total_kernel(*refs):
    *parts, out = refs
    out[...] = sum(p[...].astype(f32) for p in parts).astype(bf16)


def total(parts, rows, deps=()):
    width = parts[0][0].shape[-1]
    lanes = width // 2
    specs = [
        pl.BlockSpec((None, rows, lanes), lambda j, index=index, block=block: (index, block, j)) for _, index, block in parts
    ]
    return pl.pallas_call(
        without(total_kernel, len(parts), len(deps), -1),
        grid=(2,),
        in_specs=specs + after(deps),
        out_specs=[pl.BlockSpec((rows, lanes), lambda j: (0, j)), token_spec],
        out_shape=[jax.ShapeDtypeStruct((rows, width), bf16), token_shape],
        compiler_params=params(16),
        cost_estimate=cost(1.5),
        name="total",
    )(*[array for array, _, _ in parts], *deps)


def join_kernel(at_ref, own, other, out):
    @pl.when(pl.program_id(0) == 0)
    def _():
        out[...] = own[...]

    @pl.when(pl.program_id(0) == 1)
    def _():
        out[...] = other[...]


def join(mine, own, other, deps=()):
    rows, width = own.shape
    spec = pl.BlockSpec((rows, width), lambda j, at: (0, 0))
    return pl.pallas_call(
        without(join_kernel, 3, len(deps), -1),
        grid_spec=pltpu.PrefetchScalarGridSpec(
            num_scalar_prefetch=1,
            grid=(2,),
            in_specs=[spec, spec] + after(deps),
            out_specs=[pl.BlockSpec((rows, width), lambda j, at: ((at[0] + j) % 2, 0)), token_spec],
        ),
        out_shape=[jax.ShapeDtypeStruct((2 * rows, width), bf16), token_shape],
        compiler_params=params(16),
        cost_estimate=cost(1.5),
        name="join",
    )(jnp.reshape(mine, (1,)).astype(jnp.int32), own, other, *deps)


def over(value, axis):
    return lax.ppermute(value, axis, [(0, 1), (1, 0)])


def across(value, bit):
    size = lax.axis_size("dp")
    return lax.ppermute(value, "dp", [(i, i ^ bit) for i in range(size)])


def dp_bits():
    return [1 << k for k in range((lax.axis_size("dp") - 1).bit_length())]


def swap_halves(value):
    half = value.shape[-1] // 2
    return jnp.concatenate([value[:, half:], value[:, :half]], axis=1)


def sum_step(value, step, swaps):
    if step not in ("col", "row"):
        return value + across(value, step)
    other = over(value, step)
    rows = [swap_halves(other[k : k + 1]) if axis == step else other[k : k + 1] for k, axis in enumerate(swaps)]
    return value + jnp.concatenate(rows, axis=0)


def on_device(
    inputs,
    w_second,
    gain_second,
    shift_second,
    recur_second,
    w_third,
    gain_third,
    shift_third,
    recur_third,
    cotangent,
):
    steps, seq_group, width = inputs.shape
    share = cotangent.shape[1]
    seqs = share // lax.axis_size("row")
    pitch = round_up(steps + 2, 8)
    rows = seqs * pitch
    half = round_up(width, 2 * BLOCK)
    nb = half // BLOCK
    tiles = 2 * half // LANES
    pieces = lax.axis_size("dp")
    count = steps * seq_group * pieces
    row, col, place = lax.axis_index("row"), lax.axis_index("col"), lax.axis_index("dp")
    bits = dp_bits()
    turned = sum(((place // bit) % 2) * (pieces // 2 // bit) for bit in bits)

    def pad_weight(w):
        return jnp.pad(w, ((0, half - w.shape[0]), (0, half - w.shape[1])))

    def pad_params(*vectors):
        return jnp.pad(jnp.stack(vectors), ((0, 0), (0, half - width)))

    def bit_of(bit):
        return (place // bit) % 2

    chunks = 2
    spread = len(bits) > 1 and half // (chunks * pieces) >= 16
    places = jnp.stack([col * share + row * seqs, col * share + (1 - row) * seqs]).astype(jnp.int32)
    parts = jnp.stack([row, 1 - row]).astype(jnp.int32)
    own_second = pad_params(gain_second, shift_second, recur_second)
    own_third = pad_params(gain_third, shift_third, recur_third)
    gains_second = jnp.concatenate([own_second, over(own_second, "col")], axis=1)
    gains_third = jnp.concatenate([own_third, over(own_third, "row")], axis=1)
    nn2, nn3 = pad_weight(w_second), pad_weight(w_third)
    nf2, fn3 = over(nn2, "col"), over(nn3, "col")
    deps = ()
    if spread:
        cut_second, cut_third = cut(w_second, w_third, turned, chunks, pieces, half)
        tall = half // (chunks * pieces)
        far_second, far_third = over(cut_second, "row"), over(cut_third, "row")
        deps = (cut_second, cut_third)
    x_near, send0 = prep(inputs, places, seqs, pitch, half, 0, nb // 2, None, deps)
    x_near, send1 = prep(inputs, places, seqs, pitch, half, nb // 2, nb // 2, x_near)
    if spread:
        send0, send1, far_second, far_third, gains_second, gains_third = lax.optimization_barrier(
            (send0, send1, far_second, far_third, gains_second, gains_third)
        )
    x_far0 = over(send0, "row")
    x_far1 = over(send1, "row")
    proj_second, near_done = project([(x_near, 0, half)], [[nn2], [nf2]], tiles)
    cot_near, cot_send, cot_done = prep_grads(jnp.transpose(cotangent, (1, 0, 2)), parts, seqs, pitch, half)
    if spread:
        fn2 = [far_second[k * tall : (k + 1) * tall] for k in range(chunks)]
        nf3 = far_third
        deps = (near_done,)
        for k, bit in enumerate(reversed(bits)):
            others = [across(piece, bit) for piece in fn2]
            if k > 0:
                nf3_other = across(nf3, bits[len(bits) - k])
            joined = [join(bit_of(bit), piece, other, deps) for piece, other in zip(fn2, others)]
            fn2 = [piece for piece, _ in joined]
            if k == len(bits) - 1:
                break
            deps = (cot_done,)
            if k > 0:
                nf3, done = join(bit_of(bits[len(bits) - k]), nf3, nf3_other, tuple(done for _, done in joined))
                deps = (done,)
            if k == len(bits) - 2:
                x_far0, *fn2 = lax.optimization_barrier((x_far0, *fn2))
        x_far1, *fn2 = lax.optimization_barrier((x_far1, *fn2))
    else:
        far = over(nn2, "row")
        fn2 = [far[: half // 2], far[half // 2 :]]
        nf3 = over(nn3, "row")
    ff2 = [over(chunk, "col") for chunk in fn2]
    proj_second, far_done = project(
        [(x_far0, 0, half // 2)], [[fn2[0]], [ff2[0]]], tiles, 0, proj_second, True, (cot_done,)
    )
    deps = (far_done,)
    if spread:
        nf3, done = join(bit_of(bits[1]), nf3, nf3_other, deps)
        deps = (done,)
    proj_second, sums = project([(x_far1, 0, half // 2)], [[fn2[1]], [ff2[1]]], tiles, 0, proj_second, True, deps)

    swaps = ("col", "col")
    sums = sum_step(sums, "row", swaps)
    sums, cot_send = lax.optimization_barrier((sums, cot_send))
    cot_far = over(cot_send, "row")
    if spread:
        sums = sum_step(sums, bits[0], swaps)
        sums, nf3 = lax.optimization_barrier((sums, nf3))
        nf3_other = across(nf3, bits[0])
    sums = sum_step(sums, "col", swaps)
    for bit in bits[1:] if spread else bits:
        sums = sum_step(sums, bit, swaps)
    sums_second = sums
    hidden, slopes_second, hidden_sums = first_layer(steps, seqs, count, proj_second, sums_second, gains_second)
    deps = ()
    if spread:
        nf3, done = join(bit_of(bits[0]), nf3, nf3_other, (hidden_sums,))
        deps = (done,)
    ff3 = over(nf3, "col")
    hidden_parts = [(hidden, 0, half), (hidden, 1, half)]
    proj_third, sums_near = project(hidden_parts, [[nn3, fn3]], tiles, deps=deps)
    proj_third, sums_far = project(hidden_parts, [[nf3, ff3]], tiles, half // WIDE, proj_third)

    swaps = ("row", "row", "col")
    sums = jnp.concatenate([jnp.concatenate([sums_near, sums_far], axis=1), hidden_sums], axis=0)
    for step in ("col", *bits):
        sums = sum_step(sums, step, swaps)
    sums, cot_far = lax.optimization_barrier((sums, cot_far))
    sums = sum_step(sums, "row", swaps)
    sums_third, centre = sums[:2], (sums[2:3] / count).astype(bf16).astype(f32)
    states_near, states_far, arg_grads_third, sums = second_layer(
        steps, seqs, count, proj_third, sums_third, gains_third, cot_near, cot_far
    )
    swaps = ("row", "row", "row")
    sums = sum_step(sums, "col", swaps)
    sums = sum_step(sums, "row", swaps)
    sums, states_far = lax.optimization_barrier((sums, states_far))
    states_far = over(states_far, "row")
    for bit in bits:
        sums = sum_step(sums, bit, swaps)
    totals_third = sums

    wide = half // WIDE
    cutting = half // 2
    grads = (arg_grads_third, proj_third, sums_third, gains_third, totals_third)
    low_third, columns, fn, ff, _ = weight_grad(steps, seqs, count, [(hidden, wide, wide)], grads, centre, wide)
    from_fn, from_ff = over(fn, "col"), over(ff, "col")
    nn, nf, done = weight_grad(steps, seqs, count, [(hidden, 0, wide)], (low_third,), centre, 0)
    grad_hidden, done = pull(low_third, [nn3, nf3, fn3, ff3], True, f32, (done,))

    def begin_across(nn, from_fn, nf, from_ff, deps):
        own, other = [(nn[None], 0), (from_fn[None], 0)], [(nf[None], 0), (from_ff[None], 0)]
        tall = cutting // 2
        stacks = [[(array, index, 2) for array, index in part] for part in (own, other)]
        return fold(bit_of(bits[0]), stacks, tall, deps)

    class Chain:
        def __init__(self, kept, sent, rows, done, first=None):
            self.count, self.rows, self.left = kept.shape[0], rows, list(bits[done:])
            self.kept = kept
            self.other = across(sent, bits[done - 1])

        def step(self, deps):
            bit = self.left.pop(0)
            self.rows //= 2
            stacks = [[(self.kept, k, 0), (self.other, k, 0)] for k in range(self.count)]
            self.kept, sent, done = fold(bit_of(bit), stacks, self.rows, deps)
            self.other = across(sent, bit)
            return (done,)

        def to_row(self, deps):
            while self.left:
                deps = self.step(deps)
            sent, done = total([(self.kept, 1, 0), (self.other, 1, 0)], self.rows, deps)
            self.from_row = over(sent, "row")
            return (done,)

        def piece(self, deps):
            while self.left:
                deps = self.step(deps)
            parts = [(self.kept, 0, 0), (self.other, 0, 0)]
            if self.count > 1:
                parts.append((self.from_row[None], 0, 0))
            self.whole, done = total(parts, self.rows, deps)
            self.back = list(reversed(bits))
            self.other = across(self.whole, self.back[0])
            return (done,)

        def gather(self, deps):
            bit = self.back.pop(0)
            self.whole, done = join(bit_of(bit), self.whole, self.other, deps)
            if self.back:
                self.other = across(self.whole, self.back[0])
            return (done,)

    x3, done = total([(nf[None], 0, 0), (from_ff[None], 0, 0)], cutting, (done,))
    x3_come = over(x3, "row")
    kept, sent, done = begin_across(nn, from_fn, nf, from_ff, (done,))
    b3 = Chain(kept, sent, cutting // 2, 1)
    arg_grads_second, sums = first_back(
        steps, seqs, count, grad_hidden, slopes_second, hidden, proj_second, sums_second, gains_second, (done,)
    )
    swaps = ("col", "col", "col", "row")
    sums = jnp.concatenate([sums, columns], axis=0)
    sums, states_far, b3.other, x3_come = lax.optimization_barrier((sums, states_far, b3.other, x3_come))
    sums = sum_step(sums, "col", swaps)
    for bit in bits[1:]:
        sums = sum_step(sums, bit, swaps)
    sums, b3.other = lax.optimization_barrier((sums, b3.other))
    seen = b3.step(())
    sums = sum_step(sums, bits[0], swaps)
    sums, x3_come = lax.optimization_barrier((sums, x3_come))
    sums = sum_step(sums, "row", swaps)
    kept, sent, done = fold(
        bit_of(bits[0]), [[(nn[None], 0, 0), (from_fn[None], 0, 0), (x3_come[None], 0, 0)]], cutting // 2, seen
    )
    a3 = Chain(kept, sent, cutting // 2, 1)
    totals_second, columns = sums[:3], sums[3:4]

    grads = (arg_grads_second, proj_second, sums_second, gains_second, totals_second)
    low_second, seen, fn, ff, _ = weight_grad(steps, seqs, count, [(x_far0, 0, 1), (x_far1, 0, 1)], grads, deps=(done,))
    from_ff = over(ff, "col")
    seen = b3.step((seen,))
    seen = a3.step(seen)
    nn, nf, done = weight_grad(steps, seqs, count, [(x_near, 0, wide)], (low_second,), deps=seen)
    from_nf = over(nf, "col")
    x2, done = total([(fn[None], 0, 0), (from_ff[None], 0, 0)], cutting, (done,))
    x2_come = over(x2, "row")
    far_rows = [jnp.concatenate(fn2, axis=0), jnp.concatenate(ff2, axis=0)]
    grad_far, done = pull(low_second, far_rows, False, bf16, (done,))
    seen = b3.to_row((done,))
    kept, sent, done = begin_across(nn, from_nf, fn, from_ff, seen)
    b2 = Chain(kept, sent, cutting // 2, 1)
    seen = a3.step((done,)) if a3.left else (done,)
    grad_near, done = pull(low_second, [nn2, nf2], False, f32, seen)
    grad_far, b3.from_row, done = lax.optimization_barrier((grad_far, b3.from_row, done))
    grad_far = over(grad_far, "row")
    seen = b3.piece((done,))
    kept, sent, done = fold(
        bit_of(bits[0]), [[(nn[None], 0, 0), (from_nf[None], 0, 0), (x2_come[None], 0, 0)]], cutting // 2, seen
    )
    a2 = Chain(kept, sent, cutting // 2, 1)
    seen = a3.piece((done,))
    seen = b2.step(seen)
    output, done = combine(parts, x_near, states_near, (send0, send1), states_far, seqs, steps, width, seen)
    seen = b3.gather((done,))
    seen = a2.step(seen)
    seen = a3.gather(seen)
    seen = b2.step(seen)
    seen = b3.gather(seen)
    seen = a2.step(seen) if a2.left else seen
    seen = a3.gather(seen)
    seen = b2.to_row(seen)
    seen = a2.piece(seen)
    seen = b3.gather(seen)
    seen = a3.gather(seen)
    seen = a2.gather(seen)
    grad_inputs, done = combine(parts, cot_near, grad_near, (cot_send,), grad_far, seqs, steps, width, seen)
    seen = b2.piece((done,))
    chains = [a3, b3, a2, b2]
    while any(chain.back for chain in chains):
        for chain in chains:
            if chain.back:
                seen = chain.gather(seen)
    grad_w_third = jnp.concatenate([a3.whole, b3.whole], axis=0)
    grad_w_second = jnp.concatenate([a2.whole, b2.whole], axis=0)

    output = jnp.transpose(output, (1, 0, 2))
    grad_inputs = jnp.transpose(grad_inputs, (1, 0, 2))
    restore = centre[0, :width, None] * columns[0, None, :width]
    return (
        output,
        grad_inputs,
        grad_w_second[:width, :width].astype(f32),
        totals_second[0, :width],
        totals_second[1, :width],
        totals_second[2, :width],
        grad_w_third[:width, :width].astype(f32) + restore,
        totals_third[0, :width],
        totals_third[1, :width],
        totals_third[2, :width],
    )


def solution(mesh):
    in_specs = (
        P(None, "dp", "row"),
        P("row", "col"),
        P("col"),
        P("col"),
        P("col"),
        P("col", "row"),
        P("row"),
        P("row"),
        P("row"),
        P(None, ("dp", "col"), "row"),
    )
    out_specs = (
        P(None, ("dp", "col"), "row"),
        P(None, ("dp", "col"), "row"),
        P("row", "col"),
        P("col"),
        P("col"),
        P("col"),
        P("col", "row"),
        P("row"),
        P("row"),
        P("row"),
    )
    return jax.shard_map(
        on_device, mesh=mesh, in_specs=in_specs, out_specs=out_specs, check_vma=False
    )
```

```python
import functools

import jax
import jax.numpy as jnp
from jax import lax
from jax.experimental import pallas as pl
from jax.experimental.pallas import tpu as pltpu
from jax.sharding import PartitionSpec as P

norm_eps = 1e-05
gelu_outer = 0.7978845608028654
gelu_inner = gelu_outer * 0.044715
LANES = 128
BLOCK = 256
WIDE = 512
f32 = jnp.float32
bf16 = jnp.bfloat16


def params(mebibytes=56):
    return pltpu.CompilerParams(vmem_limit_bytes=mebibytes * 2**20)


def round_up(value, unit):
    return -(-value // unit) * unit


def after(deps):
    return [pl.BlockSpec(memory_space=pl.ANY)] * len(deps)


def without(kernel, at, count, token=None):
    def body(*refs):
        refs = list(refs)
        if token is not None:
            refs.pop(token)[...] = jnp.zeros((8, LANES), f32)
        kernel(*refs[:at], *refs[at + count :])

    return body


token_spec = pl.BlockSpec((8, LANES), lambda *_: (0, 0))
token_shape = jax.ShapeDtypeStruct((8, LANES), f32)


def whole(shape):
    return pl.BlockSpec(shape, lambda *_: (0,) * len(shape), pipeline_mode=pl.Buffered(1))


def dot(left, right, dims):
    return lax.dot_general(left, right, (dims, ((), ())), preferred_element_type=f32)


def tile_of(j):
    return pl.ds(j * LANES, LANES)


def held(j, low, count):
    return jnp.clip(j - low, 0, count - 1)


def prep_kernel(seqs, pitch, width, base, at_ref, inputs, *refs):
    near, send, scratch, packed = refs[-4:]
    steps, group, block = inputs.shape
    lane = base + pl.program_id(0) * block + lax.broadcasted_iota(jnp.int32, (1, LANES), 1)
    rows = near.shape[0]
    for k in range(block // LANES):
        scratch[...] = inputs[:, :, tile_of(k)].astype(f32).reshape(steps * group, LANES)
        for place, out in ((0, near), (1, send)):
            first = at_ref[place]
            for s in range(seqs):
                packed[s * pitch : s * pitch + steps, :] = scratch[pl.ds(first + s, steps, stride=group), :]
                packed[s * pitch + steps : (s + 1) * pitch, :] = jnp.zeros((pitch - steps, LANES), f32)
            out[:, tile_of(k)] = jnp.where(lane + k * LANES < width, packed[...], 0.0).astype(bf16)


def prep(inputs, places, seqs, pitch, half, first, blocks, near=None, deps=()):
    steps, group, width = inputs.shape
    rows = seqs * pitch
    near_spec = pl.BlockSpec((rows, BLOCK), lambda j, at: (0, j + first))
    return pl.pallas_call(
        without(functools.partial(prep_kernel, seqs, pitch, width, first * BLOCK), 2, len(deps)),
        grid_spec=pltpu.PrefetchScalarGridSpec(
            num_scalar_prefetch=1,
            grid=(blocks,),
            in_specs=[pl.BlockSpec((steps, group, BLOCK), lambda j, at: (0, 0, j + first))]
            + after(deps)
            + ([] if near is None else [pl.BlockSpec(memory_space=pl.ANY)]),
            out_specs=[near_spec, pl.BlockSpec((rows, BLOCK), lambda j, at: (0, j))],
            scratch_shapes=[pltpu.VMEM((steps * group, LANES), f32), pltpu.VMEM((rows, LANES), f32)],
        ),
        out_shape=[
            jax.ShapeDtypeStruct((rows, half), bf16),
            jax.ShapeDtypeStruct((rows, blocks * BLOCK), bf16),
        ],
        input_output_aliases={} if near is None else {2 + len(deps): 0},
        compiler_params=params(),
        name="prep",
    )(places, inputs, *deps, *(() if near is None else (near,)))


def prep_grads_kernel(pitch, width, at_ref, own, other, near, send0, send1, packed):
    seqs, steps, block = own.shape
    lane = pl.program_id(0) * block + lax.broadcasted_iota(jnp.int32, (1, block), 1)
    for part in (own, other):
        for s in range(seqs):
            packed[s * pitch : s * pitch + steps, :] = part[s].astype(f32)
            packed[s * pitch + steps : (s + 1) * pitch, :] = jnp.zeros((pitch - steps, block), f32)
        value = jnp.where(lane < width, packed[...], 0.0).astype(bf16)
        if part is own:
            near[...] = value
        else:
            cut = pl.num_programs(0) // 2

            @pl.when(pl.program_id(0) < cut)
            def _():
                send0[...] = value

            @pl.when(pl.program_id(0) >= cut)
            def _():
                send1[...] = value


def prep_grads(grads, places, seqs, pitch, half):
    _, steps, width = grads.shape
    rows = seqs * pitch
    out = pl.BlockSpec((rows, BLOCK), lambda j, at: (0, j))
    cut = half // BLOCK // 2
    first = pl.BlockSpec((rows, BLOCK), lambda j, at: (0, held(j, 0, cut)))
    second = pl.BlockSpec((rows, BLOCK), lambda j, at: (0, held(j, cut, cut)))
    return pl.pallas_call(
        without(functools.partial(prep_grads_kernel, pitch, width), 0, 0, -2),
        grid_spec=pltpu.PrefetchScalarGridSpec(
            num_scalar_prefetch=1,
            grid=(half // BLOCK,),
            in_specs=[
                pl.BlockSpec((seqs, steps, BLOCK), lambda j, at: (at[0], 0, j)),
                pl.BlockSpec((seqs, steps, BLOCK), lambda j, at: (at[1], 0, j)),
            ],
            out_specs=[out, first, second, token_spec],
            scratch_shapes=[pltpu.VMEM((rows, BLOCK), f32)],
        ),
        out_shape=[jax.ShapeDtypeStruct((rows, half), bf16)]
        + [jax.ShapeDtypeStruct((rows, half // 2), bf16)] * 2
        + [token_shape],
        compiler_params=params(),
        name="prep_grads",
    )(places, grads, grads)


def combine_kernel(pitch, counts, at_ref, *refs):
    *parts, out = refs
    seqs, steps, width = out.shape

    def put(a, b):
        a, b = (jnp.concatenate([part[...].astype(f32) for part in x], axis=1) for x in (a, b))
        total = a + b
        for s in range(seqs):
            out[s] = total[s * pitch : s * pitch + steps, :width]

    near, b_near, *far = parts
    cut = counts[0]
    pl.when(pl.program_id(0) == 0)(lambda: put([near], [b_near]))
    pl.when(pl.program_id(0) == 1)(lambda: put(far[:cut], far[cut:]))


def combine(places, a_near, b_near, a_far, b_far, seqs, steps, width, deps=()):
    rows = a_near.shape[0]
    pitch = rows // seqs
    group = 2 if seqs % 2 == 0 and 2 * pitch % 16 == 0 else seqs
    nb = seqs // group
    near_at = lambda p, j, at: (jnp.where(p == 0, j, nb - 1), 0)
    far_at = lambda p, j, at: (jnp.where(p == 0, 0, j), 0)
    operands = [a_near, b_near, *a_far, *b_far]
    specs = [pl.BlockSpec((group * pitch, x.shape[1]), near_at if k < 2 else far_at) for k, x in enumerate(operands)]
    return pl.pallas_call(
        without(functools.partial(combine_kernel, pitch, [len(a_far)]), 1 + len(operands), len(deps), -1),
        grid_spec=pltpu.PrefetchScalarGridSpec(
            num_scalar_prefetch=1,
            grid=(2, nb),
            in_specs=specs + after(deps),
            out_specs=[pl.BlockSpec((group, steps, width), lambda p, j, at: (at[p] * nb + j, 0, 0)), token_spec],
        ),
        out_shape=[jax.ShapeDtypeStruct((2 * seqs, steps, width), f32), token_shape],
        compiler_params=params(24),
        name="combine",
    )(places, *operands, *deps)


def cut_kernel(pieces, chunks, limit, at_ref, second, third, out_second, out_third):
    tall, wide = out_second.shape
    j = pl.program_id(0)
    lane = lax.broadcasted_iota(jnp.int32, (tall, wide), 1)
    for block, weight, out in ((j * pieces + at_ref[j], second, out_second), (at_ref[0] * chunks + j, third, out_third)):
        row = block * tall + lax.broadcasted_iota(jnp.int32, (tall, wide), 0)
        out[...] = jnp.where((row < limit) & (lane < limit), weight[...].astype(f32), 0.0).astype(bf16)


def cut(second, third, places, chunks, pieces, half):
    tall = half // (chunks * pieces)
    out_spec = pl.BlockSpec((tall, half), lambda j, at: (j, 0))
    return pl.pallas_call(
        functools.partial(cut_kernel, pieces, chunks, second.shape[0]),
        grid_spec=pltpu.PrefetchScalarGridSpec(
            num_scalar_prefetch=1,
            grid=(chunks,),
            in_specs=[
                pl.BlockSpec((tall, half), lambda j, at: (j * pieces + at[j], 0)),
                pl.BlockSpec((tall, half), lambda j, at: (at[0] * chunks + j, 0)),
            ],
            out_specs=[out_spec, out_spec],
        ),
        out_shape=[jax.ShapeDtypeStruct((chunks * tall, half), bf16)] * 2,
        compiler_params=params(),
        name="cut",
    )(jnp.stack(places).astype(jnp.int32), second, third)


def project_kernel(parts, halves, add, nb, *refs):
    xs = refs[:parts]
    ws = [refs[parts * (1 + h) : parts * (2 + h)] for h in range(halves)]
    refs = refs[parts * (1 + halves) :]
    proj, sums = refs[-2:]
    j = pl.program_id(0)

    def go(weights):
        acc = sum(dot(x[...], w[...], ((1,), (0,))) for x, w in zip(xs, weights))
        if add:
            acc = acc + jnp.concatenate([refs[0][k] for k in range(WIDE // LANES)], axis=1)
        for k in range(WIDE // LANES):
            proj[k] = acc[:, k * LANES : (k + 1) * LANES]
        sums[0:1, :] = jnp.sum(acc, axis=0, keepdims=True)
        sums[1:2, :] = jnp.sum(acc * acc, axis=0, keepdims=True)

    for h in range(halves):
        pl.when((j >= h * nb) & (j < (h + 1) * nb))(functools.partial(go, ws[h]))


def project(xs, ws, tiles, first=0, before=None, add=False, deps=()):
    rows = xs[0][0].shape[0]
    half = ws[0][0].shape[1]
    nb = half // WIDE
    specs, operands = [], []
    for x, at, depth in xs:
        specs.append(pl.BlockSpec((rows, depth), lambda j, at=at: (0, at), pipeline_mode=pl.Buffered(1)))
        operands.append(x)
    for h, weights in enumerate(ws):
        for w, (_, _, depth) in zip(weights, xs):
            specs.append(pl.BlockSpec((depth, WIDE), lambda j, h=h: (0, held(j, h * nb, nb))))
            operands.append(w)
    tile_spec = pl.BlockSpec((WIDE // LANES, rows, LANES), lambda j: (j + first, 0, 0))
    aliases = {}
    if before is not None:
        aliases = {len(operands): 0}
        operands.append(before)
        specs.append(tile_spec if add else pl.BlockSpec(memory_space=pl.ANY))
    width = len(ws) * half
    kernel = functools.partial(project_kernel, len(xs), len(ws), add, nb)
    return pl.pallas_call(
        without(kernel, len(operands), len(deps)),
        grid=(len(ws) * nb,),
        in_specs=specs + after(deps),
        out_specs=[tile_spec, pl.BlockSpec((2, WIDE), lambda j: (0, j))],
        out_shape=[
            jax.ShapeDtypeStruct((tiles, rows, LANES), f32),
            jax.ShapeDtypeStruct((2, width), f32),
        ],
        input_output_aliases=aliases,
        compiler_params=params(),
        name="project",
    )(*operands, *deps)


def stats_of(sums, gains, count, j):
    mean = sums[0:1, tile_of(j)] / count
    var = sums[1:2, tile_of(j)] / count - mean * mean
    scale = lax.rsqrt(var + norm_eps)
    return mean, scale


def clear_pads(steps, seqs, array):
    tiles, rows, _ = array.shape
    pitch = rows // seqs
    if pitch > steps:
        for j in range(tiles):
            for s in range(seqs):
                array[j, s * pitch + steps : (s + 1) * pitch, :] = jnp.zeros((pitch - steps, LANES), f32)


def run_forward(steps, seqs, tiles, norm, gains, states, slopes):
    recur = [jnp.broadcast_to(gains[2:3, tile_of(j)], (seqs, LANES)) for j in range(tiles)]
    pitch = norm.shape[1] // seqs

    def advance(t, before):
        now = []
        at = pl.ds(t, seqs, stride=pitch)
        for j in range(tiles):
            arg = norm[j, at, :] + recur[j] * before[j]
            poly = gelu_inner * (arg * arg) + gelu_outer
            tanh = jnp.tanh(arg * poly)
            half = 0.5 * arg
            state = half + half * tanh
            states[j, at, :] = state
            inner = 3.0 * poly - 2.0 * gelu_outer
            slopes[j, at, :] = (0.5 * tanh + 0.5) + half * (1.0 - tanh * tanh) * inner
            now.append(state)
        return tuple(now)

    unroll = 2 if steps % 2 == 0 else 1

    def several(i, before):
        for k in range(unroll):
            before = advance(i * unroll + k, before)
        return before

    zero = jnp.zeros((seqs, LANES), f32)
    lax.fori_loop(0, steps // unroll, several, (zero,) * tiles)
    clear_pads(steps, seqs, states)


def run_backward(steps, seqs, tiles, grads, gains, slopes, arg_grads):
    recur = [jnp.broadcast_to(gains[2:3, tile_of(j)], (seqs, LANES)) for j in range(tiles)]
    pitch = arg_grads.shape[1] // seqs

    def retreat(t, after):
        now = []
        at = pl.ds(t, seqs, stride=pitch)
        for j in range(tiles):
            grad = (grads[j, at, :] + recur[j] * after[j]) * slopes[j, at, :]
            arg_grads[j, at, :] = grad
            now.append(grad)
        return tuple(now)

    unroll = 2 if steps % 2 == 0 else 1

    def several(i, after):
        for k in range(unroll):
            after = retreat(steps - 1 - (i * unroll + k), after)
        return after

    zero = jnp.zeros((seqs, LANES), f32)
    lax.fori_loop(0, steps // unroll, several, (zero,) * tiles)
    clear_pads(steps, seqs, arg_grads)


def back_sums(tiles, arg_grads, proj, states, sums, gains, count, out, shifted):
    rows = proj.shape[1]
    for j in range(tiles):
        mean, scale = stats_of(sums, gains, count, j)
        grad = arg_grads[j]
        out[0:1, tile_of(j)] = scale * jnp.sum(grad * (proj[j] - mean), axis=0, keepdims=True)
        out[1:2, tile_of(j)] = jnp.sum(grad, axis=0, keepdims=True)
        shifted[...] = states(j)
        out[2:3, tile_of(j)] = jnp.sum(
            arg_grads[j, 1:rows, :] * shifted[0 : rows - 1, :], axis=0, keepdims=True
        )


def make_norm(tiles, proj, sums, gains, count, norm):
    for j in tiles:
        mean, scale = stats_of(sums, gains, count, j)
        norm[j] = (proj[j] - mean) * (gains[0:1, tile_of(j)] * scale) + gains[1:2, tile_of(j)]


def load_norm(parts, proj_hbm, proj, sems, sums, gains, count, norm):
    tiles = proj.shape[0]
    size = tiles // parts
    copies = [
        pltpu.make_async_copy(proj_hbm.at[pl.ds(k * size, size)], proj.at[pl.ds(k * size, size)], sems.at[k])
        for k in range(parts)
    ]
    for copy in copies:
        copy.start()

    def finish():
        for k, copy in enumerate(copies):
            copy.wait()
            make_norm(range(k * size, (k + 1) * size), proj, sums, gains, count, norm)

    return finish


parts_in = 4


def first_layer_kernel(
    steps, seqs, count, proj_hbm, sums, gains, top_hbm, bottom_hbm,
    hidden, slopes_hbm, totals, proj_out, moments,
    proj, norm, states, slopes, top, bottom, sems, out_sems,
):
    tiles, rows, _ = proj.shape
    half = tiles * LANES // 2
    finish = load_norm(parts_in, proj_hbm, proj, sems, sums, gains, count, norm)
    weights = [
        pltpu.make_async_copy(top_hbm, top, sems.at[parts_in]),
        pltpu.make_async_copy(bottom_hbm, bottom, sems.at[parts_in + 1]),
    ]
    for copy in weights:
        copy.start()
    finish()
    run_forward(steps, seqs, tiles, norm, gains, states, slopes)
    keep = pltpu.make_async_copy(slopes, slopes_hbm, out_sems.at[0])
    keep.start()
    for j in range(tiles):
        hidden[:, tile_of(j)] = states[j].astype(bf16)
        totals[0:1, tile_of(j)] = jnp.sum(states[j], axis=0, keepdims=True)
    for copy in weights:
        copy.wait()
    sends = []
    for k in range(half // WIDE):
        lanes = pl.ds(k * WIDE, WIDE)
        acc = dot(hidden[:, :half], top[:, lanes], ((1,), (0,))) + dot(hidden[:, half:], bottom[:, lanes], ((1,), (0,)))
        moments[0:1, lanes] = jnp.sum(acc, axis=0, keepdims=True)
        moments[1:2, lanes] = jnp.sum(acc * acc, axis=0, keepdims=True)
        size = WIDE // LANES
        for i in range(size):
            norm[k * size + i] = acc[:, i * LANES : (i + 1) * LANES]
        place = pl.ds(k * size, size)
        sends.append(pltpu.make_async_copy(norm.at[place], proj_out.at[place], out_sems.at[1 + k]))
        sends[-1].start()
    for copy in [keep, *sends]:
        copy.wait()


def first_layer(steps, seqs, count, proj, sums, gains, top, bottom):
    tiles, rows, _ = proj.shape
    width = tiles * LANES
    half = width // 2
    vmem, hbm = pl.BlockSpec(memory_space=pltpu.VMEM), pl.BlockSpec(memory_space=pl.ANY)
    tiled = pltpu.VMEM((tiles, rows, LANES), f32)
    return pl.pallas_call(
        functools.partial(first_layer_kernel, steps, seqs, count),
        in_specs=[hbm, vmem, vmem, hbm, hbm],
        out_specs=[vmem, hbm, vmem, hbm, vmem],
        out_shape=[
            jax.ShapeDtypeStruct((rows, width), bf16),
            jax.ShapeDtypeStruct((tiles, rows, LANES), f32),
            jax.ShapeDtypeStruct((1, width), f32),
            jax.ShapeDtypeStruct((tiles, rows, LANES), f32),
            jax.ShapeDtypeStruct((2, half), f32),
        ],
        scratch_shapes=[tiled] * 4
        + [pltpu.VMEM((half, half), bf16)] * 2
        + [pltpu.SemaphoreType.DMA((parts_in + 2,)), pltpu.SemaphoreType.DMA((1 + half // WIDE,))],
        compiler_params=params(),
        name="first_layer",
    )(proj, sums, gains, top, bottom)


def second_layer_kernel(
    steps, seqs, count, proj_hbm, sums, gains, near_hbm, far_hbm0, far_hbm1,
    near_out, far_out0, far_out1, grads_out, out,
    proj, norm, states, slopes, near, far, shifted, sems, out_sems,
):
    tiles, rows, _ = proj.shape
    half = tiles // 2
    cut = far.shape[1] // 2
    finish = load_norm(parts_in, proj_hbm, proj, sems, sums, gains, count, norm)
    upstream = [
        pltpu.make_async_copy(near_hbm, near, sems.at[parts_in]),
        pltpu.make_async_copy(far_hbm0, far.at[:, :cut], sems.at[parts_in + 1]),
        pltpu.make_async_copy(far_hbm1, far.at[:, cut:], sems.at[parts_in + 2]),
    ]
    for copy in upstream:
        copy.start()
    finish()
    run_forward(steps, seqs, tiles, norm, gains, states, slopes)
    for copy in upstream:
        copy.wait()
    for j in range(half):
        for part, at in ((near, j), (far, half + j)):
            norm[at] = part[:, tile_of(j)].astype(f32)
            part[:, tile_of(j)] = states[at].astype(bf16)
    sends = [
        pltpu.make_async_copy(near, near_out, out_sems.at[0]),
        pltpu.make_async_copy(far.at[:, :cut], far_out0, out_sems.at[1]),
        pltpu.make_async_copy(far.at[:, cut:], far_out1, out_sems.at[2]),
        pltpu.make_async_copy(norm, grads_out, out_sems.at[3]),
    ]
    for copy in sends[:3]:
        copy.start()
    run_backward(steps, seqs, tiles, norm, gains, slopes, norm)
    sends[3].start()
    back_sums(tiles, norm, proj, lambda j: states[j], sums, gains, count, out, shifted)
    for copy in sends:
        copy.wait()


def second_layer(steps, seqs, count, proj, sums, gains, cot_near, cot_far):
    tiles, rows, _ = proj.shape
    width = tiles * LANES
    vmem, hbm = pl.BlockSpec(memory_space=pltpu.VMEM), pl.BlockSpec(memory_space=pl.ANY)
    low = jax.ShapeDtypeStruct((rows, width // 2), bf16)
    low_half = jax.ShapeDtypeStruct((rows, width // 4), bf16)
    return pl.pallas_call(
        functools.partial(second_layer_kernel, steps, seqs, count),
        in_specs=[hbm, vmem, vmem, hbm, hbm, hbm],
        out_specs=[hbm, hbm, hbm, hbm, vmem],
        out_shape=[low, low_half, low_half, jax.ShapeDtypeStruct((tiles, rows, LANES), f32), jax.ShapeDtypeStruct((3, width), f32)],
        scratch_shapes=[pltpu.VMEM((tiles, rows, LANES), f32)] * 4
        + [pltpu.VMEM((rows, width // 2), bf16)] * 2
        + [
            pltpu.VMEM((rows, LANES), f32),
            pltpu.SemaphoreType.DMA((parts_in + 3,)),
            pltpu.SemaphoreType.DMA((4,)),
        ],
        compiler_params=params(),
        name="second_layer",
    )(proj, sums, gains, cot_near, *cot_far)


def first_back_kernel(
    steps, seqs, count, nb, low, w_nn, w_nf, w_fn, w_ff, slopes_hbm, hidden_hbm, proj_hbm, sums, gains,
    grads_out, out, grads, slopes, hidden, proj, shifted, sems,
):
    tiles = proj.shape[0]
    half = w_nn.shape[1]
    j = pl.program_id(0)
    copies = [
        pltpu.make_async_copy(slopes_hbm, slopes, sems.at[0]),
        pltpu.make_async_copy(hidden_hbm, hidden, sems.at[1]),
        pltpu.make_async_copy(proj_hbm, proj, sems.at[2]),
    ]

    @pl.when(j == 0)
    def _():
        for copy in copies:
            copy.start()

    def go(left, right):
        acc = dot(low[:, :half], left[...], ((1,), (1,))) + dot(low[:, half:], right[...], ((1,), (1,)))
        for k in range(WIDE // LANES):
            grads[j * (WIDE // LANES) + k] = acc[:, k * LANES : (k + 1) * LANES]

    pl.when(j < nb)(functools.partial(go, w_nn, w_nf))
    pl.when((j >= nb) & (j < 2 * nb))(functools.partial(go, w_fn, w_ff))

    @pl.when(j == 2 * nb)
    def _():
        for copy in copies:
            copy.wait()
        run_backward(steps, seqs, tiles, grads, gains, slopes, grads)
        send = pltpu.make_async_copy(grads, grads_out, sems.at[3])
        send.start()
        states = lambda k: hidden[:, tile_of(k)].astype(f32)
        back_sums(tiles, grads, proj, states, sums, gains, count, out, shifted)
        send.wait()


def first_back(steps, seqs, count, low, quarters, slopes, hidden, proj, sums, gains, deps=()):
    tiles, rows, _ = proj.shape
    width = tiles * LANES
    half = width // 2
    nb = half // WIDE
    hbm = pl.BlockSpec(memory_space=pl.ANY)
    weights = [pl.BlockSpec((WIDE, half), lambda j, k=k: (held(j, k // 2 * nb, nb), 0)) for k in range(4)]
    return pl.pallas_call(
        without(functools.partial(first_back_kernel, steps, seqs, count, nb), 10, len(deps)),
        grid=(2 * nb + 1,),
        in_specs=[whole((rows, width)), *weights, hbm, hbm, hbm, whole((2, width)), whole((3, width))] + after(deps),
        out_specs=[hbm, pl.BlockSpec((3, width), lambda j: (0, 0))],
        out_shape=[
            jax.ShapeDtypeStruct((tiles, rows, LANES), f32),
            jax.ShapeDtypeStruct((3, width), f32),
        ],
        scratch_shapes=[
            pltpu.VMEM((tiles, rows, LANES), f32),
            pltpu.VMEM((tiles, rows, LANES), f32),
            pltpu.VMEM((rows, width), bf16),
            pltpu.VMEM((tiles, rows, LANES), f32),
            pltpu.VMEM((rows, LANES), f32),
            pltpu.SemaphoreType.DMA((4,)),
        ],
        compiler_params=params(),
        name="first_back",
    )(low, *quarters, slopes, hidden, proj, sums, gains, *deps)


def norm_back(steps, seqs, arg_grads, proj, sums, gains, totals, count, low_ref, columns):
    tiles, rows, _ = proj.shape
    pitch = rows // seqs
    first = steps // 16 * 16
    row = first + lax.broadcasted_iota(jnp.int32, (16, LANES), 0)
    for j in range(tiles):
        mean, scale = stats_of(sums, gains, count, j)
        factor = gains[0:1, tile_of(j)] * scale
        shift_part = factor * totals[1:2, tile_of(j)] / count
        unit_part = factor * scale * totals[0:1, tile_of(j)] / count
        low = (factor * arg_grads[j] - shift_part - (proj[j] - mean) * unit_part).astype(bf16)
        low_ref[:, tile_of(j)] = low
        if columns is None:
            continue
        past = (mean * unit_part - shift_part).astype(bf16).astype(f32)
        column = jnp.sum(low.astype(f32), axis=0, keepdims=True) - (rows - seqs * steps) * past
        high_part = column.astype(bf16).astype(f32)
        low_part = (column - high_part).astype(bf16).astype(f32)
        columns[0:1, tile_of(j)] = high_part + low_part
        edge = low_ref[first : first + 16, tile_of(j)].astype(f32)
        edge = jnp.where(row == steps, high_part, jnp.where(row == steps + 1, low_part, edge))
        low_ref[first : first + 16, tile_of(j)] = edge.astype(bf16)


def weight_kernel(steps, seqs, count, parts, centred, norm_steps, *refs):
    xs, refs = refs[: len(parts)], refs[len(parts) :]
    if centred:
        centre, *refs = refs
    j = pl.program_id(0)
    if norm_steps:
        arg_grads, proj, sums, gains, totals, low_out, columns, left, right, low = refs

        @pl.when(j < norm_steps)
        def _():
            norm_back(steps, seqs, arg_grads, proj, sums, gains, totals, count, low_out, columns if centred else None)
            if not centred:
                columns[...] = jnp.zeros_like(columns)
            low[:, pl.ds(pl.multiple_of(j * BLOCK, BLOCK), BLOCK)] = low_out[...]
    else:
        low, left, right = refs
    half = low.shape[1] // 2

    def go(x):
        value = x[...]
        if centred:
            row = lax.broadcasted_iota(jnp.int32, value.shape, 0)
            minus = jnp.broadcast_to(-centre[...], value.shape)
            value = jnp.where((row == steps) | (row == steps + 1), minus, value.astype(f32)).astype(bf16)
        acc = dot(value, low[...], ((0,), (0,)))
        left[...] = acc[:, :half].astype(left.dtype)
        right[...] = acc[:, half:].astype(right.dtype)

    at = norm_steps
    for x, blocks in zip(xs, parts):
        pl.when((j >= at) & (j < at + blocks))(functools.partial(go, x))
        at += blocks


def weight_grad(steps, seqs, count, xs, grads, centre=None, centre_at=0, deps=()):
    rows = grads[0].shape[-2]
    made = len(grads) == 1
    width = grads[0].shape[1] if made else grads[0].shape[0] * LANES
    half = width // 2
    nb = half // WIDE
    norm_steps = 0 if made else width // BLOCK
    specs, start = [], norm_steps
    for _, first, blocks in xs:
        specs.append(
            pl.BlockSpec((rows, WIDE), lambda j, start=start, first=first, blocks=blocks: (0, first + held(j, start, blocks)))
        )
        start += blocks
    operands = [x for x, _, _ in xs]
    if centre is not None:
        specs.append(pl.BlockSpec((1, WIDE), lambda j: (0, centre_at + held(j, norm_steps, nb))))
        operands.append(centre)
    quarter = pl.BlockSpec((WIDE, half), lambda j: (held(j, norm_steps, nb), 0))
    out_specs, out_shape, scratch = [quarter] * 2, [jax.ShapeDtypeStruct((half, half), bf16)] * 2, []
    if made:
        specs.append(whole((rows, width)))
    else:
        tile_spec = pl.BlockSpec((BLOCK // LANES, rows, LANES), lambda j: (held(j, 0, norm_steps), 0, 0))
        lanes = lambda tall: pl.BlockSpec((tall, BLOCK), lambda j: (0, held(j, 0, norm_steps)))
        specs += [tile_spec, tile_spec, lanes(2), lanes(3), lanes(3)]
        out_specs = [lanes(rows), lanes(1)] + out_specs
        out_shape = [jax.ShapeDtypeStruct((rows, width), bf16), jax.ShapeDtypeStruct((1, width), f32)] + out_shape
        scratch = [pltpu.VMEM((rows, width), bf16)]
    kernel = functools.partial(
        weight_kernel, steps, seqs, count, [b for _, _, b in xs], centre is not None, norm_steps
    )
    return pl.pallas_call(
        without(kernel, len(specs), len(deps), -1 - len(scratch)),
        grid=(norm_steps + nb,),
        in_specs=specs + after(deps),
        out_specs=out_specs + [token_spec],
        out_shape=out_shape + [token_shape],
        scratch_shapes=scratch,
        compiler_params=params(),
        name="weight_grad",
    )(*operands, *grads, *deps)


def pull_kernel(nb, tiled, low, *refs):
    *weights, out = refs
    j = pl.program_id(0)
    half = weights[0].shape[1]

    def go(left, right):
        acc = dot(low[:, :half], left[...], ((1,), (1,))) + dot(low[:, half:], right[...], ((1,), (1,)))
        if tiled:
            for k in range(WIDE // LANES):
                out[k] = acc[:, k * LANES : (k + 1) * LANES]
        else:
            out[...] = acc.astype(out.dtype)

    for k in range(len(weights) // 2):
        pl.when((j >= k * nb) & (j < (k + 1) * nb))(functools.partial(go, *weights[2 * k : 2 * k + 2]))


def pull(low, quarters, tiled, dtype, deps=()):
    rows, width = low.shape
    half = width // 2
    nb = half // WIDE
    halves = len(quarters) // 2
    specs = [pl.BlockSpec((WIDE, half), lambda j, k=k: (held(j, k // 2 * nb, nb), 0)) for k in range(2 * halves)]
    if tiled:
        out_spec = pl.BlockSpec((WIDE // LANES, rows, LANES), lambda j: (j, 0, 0))
        shape = (halves * half // LANES, rows, LANES)
    else:
        out_spec = pl.BlockSpec((rows, WIDE), lambda j: (0, j))
        shape = (rows, halves * half)
    return pl.pallas_call(
        without(functools.partial(pull_kernel, nb, tiled), 1 + len(quarters), len(deps), -1),
        grid=(halves * nb,),
        in_specs=[whole((rows, width))] + specs + after(deps),
        out_specs=[out_spec, token_spec],
        out_shape=[jax.ShapeDtypeStruct(shape, dtype), token_shape],
        compiler_params=params(),
        name="pull",
    )(low, *quarters, *deps)


def fold_kernel(counts, at_ref, *refs):
    kept, sent = refs[-2:]
    at = 0
    for k, n in enumerate(counts):
        parts = refs[at : at + 2 * n]
        kept[k] = sum(p[...].astype(f32) for p in parts[:n])
        sent[k] = sum(p[...].astype(f32) for p in parts[n:]).astype(bf16)
        at += 2 * n


def fold(mine, stacks, rows, deps=(), mebibytes=16):
    specs, operands = [], []
    width = stacks[0][0][0].shape[-1]
    lanes = width // 2
    for stack in stacks:
        for side in (0, 1):
            for array, index, base in stack:
                operands.append(array)
                specs.append(
                    pl.BlockSpec(
                        (None, rows, lanes),
                        lambda j, at, side=side, index=index, base=base: (index, base + (at[0] + side) % 2, j),
                    )
                )
    count = len(stacks)
    out_spec = pl.BlockSpec((count, rows, lanes), lambda j, at: (0, 0, j))
    kernel = functools.partial(fold_kernel, [len(stack) for stack in stacks])
    return pl.pallas_call(
        without(kernel, 1 + len(operands), len(deps), -1),
        grid_spec=pltpu.PrefetchScalarGridSpec(
            num_scalar_prefetch=1, grid=(2,), in_specs=specs + after(deps), out_specs=[out_spec, out_spec, token_spec]
        ),
        out_shape=[
            jax.ShapeDtypeStruct((count, rows, width), f32),
            jax.ShapeDtypeStruct((count, rows, width), bf16),
            token_shape,
        ],
        compiler_params=params(mebibytes),
        name="fold",
    )(jnp.reshape(mine, (1,)).astype(jnp.int32), *operands, *deps)


def total_kernel(counts, *refs):
    *parts, out = refs
    at = 0
    for k, n in enumerate(counts):
        out[k] = sum(p[...].astype(f32) for p in parts[at : at + n]).astype(bf16)
        at += n


def total(stacks, rows, deps=(), mebibytes=16):
    parts = [part for stack in stacks for part in stack]
    count, width = len(stacks), parts[0][0].shape[-1]
    lanes = width // 2
    specs = [
        pl.BlockSpec((None, rows, lanes), lambda j, index=index, block=block: (index, block, j)) for _, index, block in parts
    ]
    out, done = pl.pallas_call(
        without(functools.partial(total_kernel, [len(stack) for stack in stacks]), len(parts), len(deps), -1),
        grid=(2,),
        in_specs=specs + after(deps),
        out_specs=[pl.BlockSpec((count, rows, lanes), lambda j: (0, 0, j)), token_spec],
        out_shape=[jax.ShapeDtypeStruct((count, rows, width), bf16), token_shape],
        compiler_params=params(mebibytes),
        name="total",
    )(*[array for array, _, _ in parts], *deps)
    return out.reshape(count * rows, width), done


def join_kernel(at_ref, own, other, out):
    @pl.when(pl.program_id(0) == 0)
    def _():
        out[...] = own[...]

    @pl.when(pl.program_id(0) == 1)
    def _():
        out[...] = other[...]


def join(mine, own, other, deps=()):
    rows, width = own.shape
    spec = pl.BlockSpec((rows, width), lambda j, at: (0, 0))
    return pl.pallas_call(
        without(join_kernel, 3, len(deps), -1),
        grid_spec=pltpu.PrefetchScalarGridSpec(
            num_scalar_prefetch=1,
            grid=(2,),
            in_specs=[spec, spec] + after(deps),
            out_specs=[pl.BlockSpec((rows, width), lambda j, at: ((at[0] + j) % 2, 0)), token_spec],
        ),
        out_shape=[jax.ShapeDtypeStruct((2 * rows, width), bf16), token_shape],
        compiler_params=params(16),
        name="join",
    )(jnp.reshape(mine, (1,)).astype(jnp.int32), own, other, *deps)


def over(value, axis):
    return lax.ppermute(value, axis, [(0, 1), (1, 0)])


def across(value, bit):
    size = lax.axis_size("dp")
    return lax.ppermute(value, "dp", [(i, i ^ bit) for i in range(size)])


def dp_bits():
    return [1 << k for k in range((lax.axis_size("dp") - 1).bit_length())]


def swap_halves(value):
    half = value.shape[-1] // 2
    return jnp.concatenate([value[:, half:], value[:, :half]], axis=1)


def sum_step(value, step, swaps):
    if step not in ("col", "row"):
        return value + across(value, step)
    other = over(value, step)
    rows = [swap_halves(other[k : k + 1]) if axis == step else other[k : k + 1] for k, axis in enumerate(swaps)]
    return value + jnp.concatenate(rows, axis=0)


def on_device(
    inputs,
    w_second,
    gain_second,
    shift_second,
    recur_second,
    w_third,
    gain_third,
    shift_third,
    recur_third,
    cotangent,
):
    steps, seq_group, width = inputs.shape
    share = cotangent.shape[1]
    seqs = share // lax.axis_size("row")
    pitch = round_up(steps + 2, 8)
    rows = seqs * pitch
    half = round_up(width, 2 * BLOCK)
    nb = half // BLOCK
    tiles = 2 * half // LANES
    pieces = lax.axis_size("dp")
    count = steps * seq_group * pieces
    row, col, place = lax.axis_index("row"), lax.axis_index("col"), lax.axis_index("dp")
    bits = dp_bits()

    def turned(order):
        return sum(((place // bit) % 2) << k for k, bit in enumerate(order))


    def pad_weight(w):
        return jnp.pad(w, ((0, half - w.shape[0]), (0, half - w.shape[1])))

    def pad_params(*vectors):
        return jnp.pad(jnp.stack(vectors), ((0, 0), (0, half - width)))

    def bit_of(bit):
        return (place // bit) % 2

    chunks = 2
    spread = len(bits) > 1 and half // (chunks * pieces) >= 16
    orders = [bits[::-1], bits[:1] + bits[:0:-1]]
    places = jnp.stack([col * share + row * seqs, col * share + (1 - row) * seqs]).astype(jnp.int32)
    parts = jnp.stack([row, 1 - row]).astype(jnp.int32)
    own_second = pad_params(gain_second, shift_second, recur_second)
    own_third = pad_params(gain_third, shift_third, recur_third)
    gains_second = jnp.concatenate([own_second, over(own_second, "col")], axis=1)
    gains_third = jnp.concatenate([own_third, over(own_third, "row")], axis=1)
    nn2, nn3 = pad_weight(w_second), pad_weight(w_third)
    nf2, fn3 = over(nn2, "col"), over(nn3, "col")
    deps = ()
    if spread:
        cut_second, cut_third = cut(w_second, w_third, [turned(order) for order in orders], chunks, pieces, half)
        tall = half // (chunks * pieces)
        far_second, far_third = over(cut_second, "row"), over(cut_third, "row")
        deps = (cut_second, cut_third)
    x_near, send0 = prep(inputs, places, seqs, pitch, half, 0, nb // 2, None, deps)
    x_near, send1 = prep(inputs, places, seqs, pitch, half, nb // 2, nb // 2, x_near)
    if spread:
        send0, send1, far_second, far_third, gains_second, gains_third = lax.optimization_barrier(
            (send0, send1, far_second, far_third, gains_second, gains_third)
        )
    x_far0 = over(send0, "row")
    x_far1 = over(send1, "row")
    proj_second, near_done = project([(x_near, 0, half)], [[nn2], [nf2]], tiles)
    cot_near, cot_send0, cot_send1, cot_done = prep_grads(jnp.transpose(cotangent, (1, 0, 2)), parts, seqs, pitch, half)
    if spread:
        fn2 = [far_second[k * tall : (k + 1) * tall] for k in range(chunks)]
        nf3 = far_third
        deps = (near_done,)
        for k in range(len(bits)):
            others = [across(piece, order[k]) for piece, order in zip(fn2, orders)]
            if k > 0:
                nf3_other = across(nf3, orders[0][k - 1])
            joined = [join(bit_of(order[k]), piece, other, deps) for piece, order, other in zip(fn2, orders, others)]
            fn2 = [piece for piece, _ in joined]
            if k == len(bits) - 1:
                break
            deps = (cot_done,)
            if k > 0:
                nf3, done = join(bit_of(orders[0][k - 1]), nf3, nf3_other, tuple(done for _, done in joined))
                deps = (done,)
            if k == len(bits) - 2:
                x_far0, *fn2 = lax.optimization_barrier((x_far0, *fn2))
        x_far1, *fn2 = lax.optimization_barrier((x_far1, *fn2))
    else:
        far = over(nn2, "row")
        fn2 = [far[: half // 2], far[half // 2 :]]
        nf3 = over(nn3, "row")
    ff2 = [over(chunk, "col") for chunk in fn2]
    x_parts = [(x_far0, 0, half // 2), (x_far1, 0, half // 2)]
    proj_second, sums_near = project(x_parts, [fn2], tiles, 0, proj_second, True, (cot_done, nn3))
    proj_second, sums_far = project(x_parts, [ff2], tiles, half // WIDE, proj_second, True)
    sums = jnp.concatenate([sums_near, sums_far], axis=1)
    if spread:
        nf3, done = join(bit_of(bits[1]), nf3, nf3_other, (sums,))
        sums, done = lax.optimization_barrier((sums, done))

    swaps = ("col", "col")
    sums = sum_step(sums, "row", swaps)
    sums, cot_send0, cot_send1 = lax.optimization_barrier((sums, cot_send0, cot_send1))
    cot_far0, cot_far1 = over(cot_send0, "row"), over(cot_send1, "row")
    if spread:
        sums = sum_step(sums, bits[0], swaps)
        sums, nf3 = lax.optimization_barrier((sums, nf3))
        nf3_other = across(nf3, bits[0])
    sums = sum_step(sums, "col", swaps)
    for bit in bits[1:] if spread else bits:
        sums = sum_step(sums, bit, swaps)
    sums_second, cot_far0 = lax.optimization_barrier((sums, cot_far0))
    hidden, slopes_second, hidden_sums, proj_third, sums_near = first_layer(
        steps, seqs, count, proj_second, sums_second, gains_second, nn3, fn3
    )
    if spread:
        nf3, done = join(bit_of(bits[0]), nf3, nf3_other, (hidden_sums,))
    ff3 = over(nf3, "col")
    hidden_parts = [(hidden, 0, half), (hidden, 1, half)]
    proj_third, sums_far = project(
        hidden_parts, [[nf3, ff3]], tiles, half // WIDE, proj_third, False
    )

    swaps = ("row", "row", "col")
    sums = jnp.concatenate([jnp.concatenate([sums_near, sums_far], axis=1), hidden_sums], axis=0)
    for step in ("col", *bits):
        sums = sum_step(sums, step, swaps)
    sums, cot_far1 = lax.optimization_barrier((sums, cot_far1))
    sums = sum_step(sums, "row", swaps)
    sums_third, centre = sums[:2], (sums[2:3] / count).astype(bf16).astype(f32)
    states_near, out_send0, out_send1, arg_grads_third, sums = second_layer(
        steps, seqs, count, proj_third, sums_third, gains_third, cot_near, (cot_far0, cot_far1)
    )
    swaps = ("row", "row", "row")
    sums = sum_step(sums, "col", swaps)
    sums = sum_step(sums, "row", swaps)
    sums, out_send0 = lax.optimization_barrier((sums, out_send0))
    out_far0 = over(out_send0, "row")
    for bit in bits:
        sums = sum_step(sums, bit, swaps)
    totals_third = sums

    wide = half // WIDE
    cutting = half // 2
    grads = (arg_grads_third, proj_third, sums_third, gains_third, totals_third)
    low_third, columns, fn, ff, _ = weight_grad(steps, seqs, count, [(hidden, wide, wide)], grads, centre, wide)
    from_fn, from_ff = over(fn, "col"), over(ff, "col")
    nn, nf, done = weight_grad(steps, seqs, count, [(hidden, 0, wide)], (low_third,), centre, 0)

    def begin_across(nn, from_fn, nf, from_ff, deps):
        own, other = [(nn[None], 0), (from_fn[None], 0)], [(nf[None], 0), (from_ff[None], 0)]
        tall = cutting // 2
        stacks = [[(array, index, 2) for array, index in part] for part in (own, other)]
        return fold(bit_of(bits[0]), stacks, tall, deps, 56)

    class Chain:
        def __init__(self, stacks, rows, left):
            self.stacks, self.rows, self.left = stacks, rows, list(left)

        def step(self, deps):
            bit = self.left.pop(0)
            self.rows //= 2
            stacks = [[(array, index, 0) for array, index in stack] for stack in self.stacks]
            kept, sent, done = fold(bit_of(bit), stacks, self.rows, deps)
            other = across(sent, bit)
            self.stacks = [[(kept, k), (other, k)] for k in range(len(stacks))]
            return (done,)

        def piece(self, deps):
            while self.left:
                deps = self.step(deps)
            stacks = [[(array, index, 0) for array, index in stack] for stack in self.stacks]
            self.whole, done = total(stacks, self.rows, deps)
            self.back = list(reversed(bits))
            self.other = across(self.whole, self.back[0])
            return (done,)

        def gather(self, deps):
            bit = self.back.pop(0)
            self.whole, done = join(bit_of(bit), self.whole, self.other, deps)
            if self.back:
                self.other = across(self.whole, self.back[0])
            return (done,)

    x3, done = total([[(nf[None], 0, 0), (from_ff[None], 0, 0)]], cutting, (done,), 56)
    x3_come = over(x3, "row")
    kept, sent, done = begin_across(nn, from_fn, nf, from_ff, (done,))
    b3_kept, b3_other = kept, across(sent, bits[0])
    arg_grads_second, sums = first_back(
        steps, seqs, count, low_third, [nn3, nf3, fn3, ff3], slopes_second, hidden, proj_second, sums_second, gains_second,
        (done, out_far0),
    )
    swaps = ("col", "col", "col", "row")
    sums = jnp.concatenate([sums, columns], axis=0)
    sums, b3_other, x3_come = lax.optimization_barrier((sums, b3_other, x3_come))
    sums = sum_step(sums, "col", swaps)
    sums = sum_step(sums, "row", swaps)
    sums, b3_other = lax.optimization_barrier((sums, b3_other))

    def to_row(kept, other, deps):
        sent, done = total([[(kept, 1, 0), (other, 1, 0)]], cutting // 2, deps)
        return over(sent, "row")[None], done

    def to_across(nn, from_other, come, deps):
        stack = [(nn[None], 0, 0), (from_other[None], 0, 0), (come[None], 0, 0)]
        kept, sent, done = fold(bit_of(bits[0]), [stack], cutting // 2, deps, 56)
        return [(kept, 0), (across(sent, bits[0]), 0)], done

    b3_row, done = to_row(b3_kept, b3_other, ())
    sums = sum_step(sums, bits[0], swaps)
    sums, x3_come = lax.optimization_barrier((sums, x3_come))
    a3, done = to_across(nn, from_fn, x3_come, (done,))
    for bit in bits[1:]:
        sums = sum_step(sums, bit, swaps)
    totals_second, columns = sums[:3], sums[3:4]
    c3 = Chain([a3, [(b3_kept, 0), (b3_other, 0), (b3_row, 0)]], cutting // 2, bits[1:])
    totals_second, done = lax.optimization_barrier((totals_second, done))
    seen = c3.step((done,))

    grads = (arg_grads_second, proj_second, sums_second, gains_second, totals_second)
    low_second, seen, fn, ff, _ = weight_grad(steps, seqs, count, [(x_far0, 0, 1), (x_far1, 0, 1)], grads, deps=seen)
    from_ff = over(ff, "col")
    seen = c3.step((seen,)) if c3.left else (seen,)
    nn, nf, done = weight_grad(steps, seqs, count, [(x_near, 0, wide)], (low_second,), deps=seen)
    from_nf = over(nf, "col")
    x2, done = total([[(fn[None], 0, 0), (from_ff[None], 0, 0)]], cutting, (done,), 56)
    x2_come = over(x2, "row")
    kept, sent, done = begin_across(nn, from_nf, fn, from_ff, (done,))
    b2_kept, b2_other = kept, across(sent, bits[0])
    far_rows = [jnp.concatenate(fn2, axis=0), jnp.concatenate(ff2, axis=0)]
    grad_far, done = pull(low_second, far_rows, False, bf16, (done,))
    seen = c3.piece((done,))
    b2_row, done = to_row(b2_kept, b2_other, seen)
    a2, done = to_across(nn, from_nf, x2_come, (done,))
    seen = c3.gather((done,))
    grad_near, done = pull(low_second, [nn2, nf2], False, f32, seen)
    seen = (done,)
    b2 = Chain([[(b2_kept, 0), (b2_other, 0), (b2_row, 0)]], cutting // 2, bits[1:])
    seen = b2.step(seen)
    grad_far, done = lax.optimization_barrier((grad_far, *seen))
    grad_far = over(grad_far, "row")
    a2 = Chain([a2], cutting // 2, bits[1:])
    seen = a2.step((done,))
    out_send1, done = lax.optimization_barrier((out_send1, *seen))
    out_far1 = over(out_send1, "row")
    seen = c3.gather((done,)) if c3.back else (done,)
    seen = b2.step(seen) if b2.left else seen
    seen = a2.step(seen) if a2.left else seen
    seen = b2.piece(seen)
    seen = c3.gather(seen) if c3.back else seen
    seen = a2.piece(seen)
    seen = b2.gather(seen)
    seen = a2.gather(seen)
    seen = b2.gather(seen)
    seen = a2.gather(seen)
    grad_inputs, done = combine(
        parts, cot_near, grad_near, (cot_send0, cot_send1), (grad_far,), seqs, steps, width, seen
    )
    output, done = combine(
        parts, x_near, states_near, (send0, send1), (out_far0, out_far1), seqs, steps, width, (done,)
    )
    seen = (done,)
    chains = [c3, b2, a2]
    while any(chain.back for chain in chains):
        for chain in chains:
            if chain.back:
                seen = chain.gather(seen)
    grad_w_third = jnp.transpose(c3.whole.reshape(pieces, 2, -1, half), (1, 0, 2, 3)).reshape(half, half)
    grad_w_second = jnp.concatenate([a2.whole, b2.whole], axis=0)

    output = jnp.transpose(output, (1, 0, 2))
    grad_inputs = jnp.transpose(grad_inputs, (1, 0, 2))
    restore = centre[0, :width, None] * columns[0, None, :width]
    return (
        output,
        grad_inputs,
        grad_w_second[:width, :width].astype(f32),
        totals_second[0, :width],
        totals_second[1, :width],
        totals_second[2, :width],
        grad_w_third[:width, :width].astype(f32) + restore,
        totals_third[0, :width],
        totals_third[1, :width],
        totals_third[2, :width],
    )


def solution(mesh):
    in_specs = (
        P(None, "dp", "row"),
        P("row", "col"),
        P("col"),
        P("col"),
        P("col"),
        P("col", "row"),
        P("row"),
        P("row"),
        P("row"),
        P(None, ("dp", "col"), "row"),
    )
    out_specs = (
        P(None, ("dp", "col"), "row"),
        P(None, ("dp", "col"), "row"),
        P("row", "col"),
        P("col"),
        P("col"),
        P("col"),
        P("col", "row"),
        P("row"),
        P("row"),
        P("row"),
    )
    return jax.shard_map(
        on_device, mesh=mesh, in_specs=in_specs, out_specs=out_specs, check_vma=False
    )
```

```python
import functools

import jax
import jax.numpy as jnp
from jax import lax
from jax.experimental import pallas as pl
from jax.experimental.pallas import tpu as pltpu
from jax.sharding import PartitionSpec as P

norm_eps = 1e-05
gelu_outer = 0.7978845608028654
gelu_inner = gelu_outer * 0.044715
LANES = 128
BLOCK = 256
WIDE = 512
f32 = jnp.float32
bf16 = jnp.bfloat16


def params(mebibytes=56):
    return pltpu.CompilerParams(vmem_limit_bytes=mebibytes * 2**20)


def round_up(value, unit):
    return -(-value // unit) * unit


def after(deps):
    return [pl.BlockSpec(memory_space=pl.ANY)] * len(deps)


def without(kernel, at, count, token=None):
    def body(*refs):
        refs = list(refs)
        if token is not None:
            refs.pop(token)[...] = jnp.zeros((8, LANES), f32)
        kernel(*refs[:at], *refs[at + count :])

    return body


token_spec = pl.BlockSpec((8, LANES), lambda *_: (0, 0))
token_shape = jax.ShapeDtypeStruct((8, LANES), f32)


def whole(shape):
    return pl.BlockSpec(shape, lambda *_: (0,) * len(shape), pipeline_mode=pl.Buffered(1))


def dot(left, right, dims):
    return lax.dot_general(left, right, (dims, ((), ())), preferred_element_type=f32)


def tile_of(j):
    return pl.ds(j * LANES, LANES)


def held(j, low, count):
    return jnp.clip(j - low, 0, count - 1)


def prep_kernel(seqs, pitch, width, base, at_ref, inputs, *refs):
    near, send, scratch, packed = refs[-4:]
    steps, group, block = inputs.shape
    lane = base + pl.program_id(0) * block + lax.broadcasted_iota(jnp.int32, (1, LANES), 1)
    rows = near.shape[0]
    for k in range(block // LANES):
        scratch[...] = inputs[:, :, tile_of(k)].astype(f32).reshape(steps * group, LANES)
        for place, out in ((0, near), (1, send)):
            first = at_ref[place]
            for s in range(seqs):
                packed[s * pitch : s * pitch + steps, :] = scratch[pl.ds(first + s, steps, stride=group), :]
                packed[s * pitch + steps : (s + 1) * pitch, :] = jnp.zeros((pitch - steps, LANES), f32)
            out[:, tile_of(k)] = jnp.where(lane + k * LANES < width, packed[...], 0.0).astype(bf16)


def prep(inputs, places, seqs, pitch, half, first, blocks, near=None, deps=()):
    steps, group, width = inputs.shape
    rows = seqs * pitch
    near_spec = pl.BlockSpec((rows, BLOCK), lambda j, at: (0, j + first))
    return pl.pallas_call(
        without(functools.partial(prep_kernel, seqs, pitch, width, first * BLOCK), 2, len(deps)),
        grid_spec=pltpu.PrefetchScalarGridSpec(
            num_scalar_prefetch=1,
            grid=(blocks,),
            in_specs=[pl.BlockSpec((steps, group, BLOCK), lambda j, at: (0, 0, j + first))]
            + after(deps)
            + ([] if near is None else [pl.BlockSpec(memory_space=pl.ANY)]),
            out_specs=[near_spec, pl.BlockSpec((rows, BLOCK), lambda j, at: (0, j))],
            scratch_shapes=[pltpu.VMEM((steps * group, LANES), f32), pltpu.VMEM((rows, LANES), f32)],
        ),
        out_shape=[
            jax.ShapeDtypeStruct((rows, half), bf16),
            jax.ShapeDtypeStruct((rows, blocks * BLOCK), bf16),
        ],
        input_output_aliases={} if near is None else {2 + len(deps): 0},
        compiler_params=params(),
        name="prep",
    )(places, inputs, *deps, *(() if near is None else (near,)))


def prep_grads_kernel(pitch, width, at_ref, own, other, near, send0, send1, packed):
    seqs, steps, block = own.shape
    lane = pl.program_id(0) * block + lax.broadcasted_iota(jnp.int32, (1, block), 1)

    def pack(part, out):
        for s in range(seqs):
            packed[s * pitch : s * pitch + steps, :] = part[s].astype(f32)
            packed[s * pitch + steps : (s + 1) * pitch, :] = jnp.zeros((pitch - steps, block), f32)
        out[...] = jnp.where(lane < width, packed[...], 0.0).astype(bf16)

    pack(own, near)
    pl.when(pl.program_id(0) == 0)(lambda: pack(other, send0))
    pl.when(pl.program_id(0) > 0)(lambda: pack(other, send1))


def prep_grads(grads, places, seqs, pitch, half):
    _, steps, width = grads.shape
    rows = seqs * pitch
    out = pl.BlockSpec((rows, BLOCK), lambda j, at: (0, j))
    return pl.pallas_call(
        without(functools.partial(prep_grads_kernel, pitch, width), 0, 0, -2),
        grid_spec=pltpu.PrefetchScalarGridSpec(
            num_scalar_prefetch=1,
            grid=(half // BLOCK,),
            in_specs=[
                pl.BlockSpec((seqs, steps, BLOCK), lambda j, at: (at[0], 0, j)),
                pl.BlockSpec((seqs, steps, BLOCK), lambda j, at: (at[1], 0, j)),
            ],
            out_specs=[
                out,
                pl.BlockSpec((rows, BLOCK), lambda j, at: (0, 0)),
                pl.BlockSpec((rows, BLOCK), lambda j, at: (0, jnp.maximum(j - 1, 0))),
                token_spec,
            ],
            scratch_shapes=[pltpu.VMEM((rows, BLOCK), f32)],
        ),
        out_shape=[jax.ShapeDtypeStruct((rows, lanes), bf16) for lanes in (half, BLOCK, half - BLOCK)] + [token_shape],
        compiler_params=params(),
        name="prep_grads",
    )(places, grads, grads)


def combine_kernel(pitch, counts, at_ref, *refs):
    *parts, out = refs
    seqs, steps, width = out.shape

    def put(a, b):
        a, b = (jnp.concatenate([part[...].astype(f32) for part in x], axis=1) for x in (a, b))
        total = a + b
        for s in range(seqs):
            out[s] = total[s * pitch : s * pitch + steps, :width]

    near, b_near, *far = parts
    cut = counts[0]
    pl.when(pl.program_id(0) == 0)(lambda: put([near], [b_near]))
    pl.when(pl.program_id(0) == 1)(lambda: put(far[:cut], far[cut:]))


def combine(places, a_near, b_near, a_far, b_far, seqs, steps, width, deps=()):
    rows = a_near.shape[0]
    pitch = rows // seqs
    group = 2 if seqs % 2 == 0 and 2 * pitch % 16 == 0 else seqs
    nb = seqs // group
    near_at = lambda p, j, at: (jnp.where(p == 0, j, nb - 1), 0)
    far_at = lambda p, j, at: (jnp.where(p == 0, 0, j), 0)
    operands = [a_near, b_near, *a_far, *b_far]
    specs = [pl.BlockSpec((group * pitch, x.shape[1]), near_at if k < 2 else far_at) for k, x in enumerate(operands)]
    return pl.pallas_call(
        without(functools.partial(combine_kernel, pitch, [len(a_far)]), 1 + len(operands), len(deps), -1),
        grid_spec=pltpu.PrefetchScalarGridSpec(
            num_scalar_prefetch=1,
            grid=(2, nb),
            in_specs=specs + after(deps),
            out_specs=[pl.BlockSpec((group, steps, width), lambda p, j, at: (at[p] * nb + j, 0, 0)), token_spec],
        ),
        out_shape=[jax.ShapeDtypeStruct((2 * seqs, steps, width), f32), token_shape],
        compiler_params=params(24),
        name="combine",
    )(places, *operands, *deps)


def cut_kernel(pieces, chunks, limit, at_ref, second, third, out_second, out_third):
    tall, wide = out_second.shape
    j = pl.program_id(0)
    lane = lax.broadcasted_iota(jnp.int32, (tall, wide), 1)
    for block, weight, out in ((j * pieces + at_ref[j], second, out_second), (at_ref[0] * chunks + j, third, out_third)):
        row = block * tall + lax.broadcasted_iota(jnp.int32, (tall, wide), 0)
        out[...] = jnp.where((row < limit) & (lane < limit), weight[...].astype(f32), 0.0).astype(bf16)


def cut(second, third, places, chunks, pieces, half):
    tall = half // (chunks * pieces)
    out_spec = pl.BlockSpec((tall, half), lambda j, at: (j, 0))
    return pl.pallas_call(
        functools.partial(cut_kernel, pieces, chunks, second.shape[0]),
        grid_spec=pltpu.PrefetchScalarGridSpec(
            num_scalar_prefetch=1,
            grid=(chunks,),
            in_specs=[
                pl.BlockSpec((tall, half), lambda j, at: (j * pieces + at[j], 0)),
                pl.BlockSpec((tall, half), lambda j, at: (at[0] * chunks + j, 0)),
            ],
            out_specs=[out_spec, out_spec],
        ),
        out_shape=[jax.ShapeDtypeStruct((chunks * tall, half), bf16)] * 2,
        compiler_params=params(),
        name="cut",
    )(jnp.stack(places).astype(jnp.int32), second, third)


def project_kernel(parts, halves, add, nb, *refs):
    xs = refs[:parts]
    ws = [refs[parts * (1 + h) : parts * (2 + h)] for h in range(halves)]
    refs = refs[parts * (1 + halves) :]
    proj, sums = refs[-2:]
    j = pl.program_id(0)

    def go(weights):
        acc = sum(dot(x[...], w[...], ((1,), (0,))) for x, w in zip(xs, weights))
        if add:
            acc = acc + jnp.concatenate([refs[0][k] for k in range(WIDE // LANES)], axis=1)
        for k in range(WIDE // LANES):
            proj[k] = acc[:, k * LANES : (k + 1) * LANES]
        sums[0:1, :] = jnp.sum(acc, axis=0, keepdims=True)
        sums[1:2, :] = jnp.sum(acc * acc, axis=0, keepdims=True)

    for h in range(halves):
        pl.when((j >= h * nb) & (j < (h + 1) * nb))(functools.partial(go, ws[h]))


def project(xs, ws, tiles, first=0, before=None, add=False, deps=()):
    rows = xs[0][0].shape[0]
    half = ws[0][0].shape[1]
    nb = half // WIDE
    specs, operands = [], []
    for x, at, depth in xs:
        specs.append(pl.BlockSpec((rows, depth), lambda j, at=at: (0, at), pipeline_mode=pl.Buffered(1)))
        operands.append(x)
    for h, weights in enumerate(ws):
        for w, (_, _, depth) in zip(weights, xs):
            specs.append(pl.BlockSpec((depth, WIDE), lambda j, h=h: (0, held(j, h * nb, nb))))
            operands.append(w)
    tile_spec = pl.BlockSpec((WIDE // LANES, rows, LANES), lambda j: (j + first, 0, 0))
    aliases = {}
    if before is not None:
        aliases = {len(operands): 0}
        operands.append(before)
        specs.append(tile_spec if add else pl.BlockSpec(memory_space=pl.ANY))
    width = len(ws) * half
    kernel = functools.partial(project_kernel, len(xs), len(ws), add, nb)
    return pl.pallas_call(
        without(kernel, len(operands), len(deps)),
        grid=(len(ws) * nb,),
        in_specs=specs + after(deps),
        out_specs=[tile_spec, pl.BlockSpec((2, WIDE), lambda j: (0, j))],
        out_shape=[
            jax.ShapeDtypeStruct((tiles, rows, LANES), f32),
            jax.ShapeDtypeStruct((2, width), f32),
        ],
        input_output_aliases=aliases,
        compiler_params=params(),
        name="project",
    )(*operands, *deps)


def stats_of(sums, gains, count, j):
    mean = sums[0:1, tile_of(j)] / count
    var = sums[1:2, tile_of(j)] / count - mean * mean
    scale = lax.rsqrt(var + norm_eps)
    return mean, scale


def clear_pads(steps, seqs, array):
    tiles, rows, _ = array.shape
    pitch = rows // seqs
    if pitch > steps:
        for j in range(tiles):
            for s in range(seqs):
                array[j, s * pitch + steps : (s + 1) * pitch, :] = jnp.zeros((pitch - steps, LANES), f32)


def run_forward(steps, seqs, tiles, norm, gains, states, slopes):
    recur = [jnp.broadcast_to(gains[2:3, tile_of(j)], (seqs, LANES)) for j in range(tiles)]
    pitch = norm.shape[1] // seqs

    def advance(t, before):
        now = []
        at = pl.ds(t, seqs, stride=pitch)
        for j in range(tiles):
            arg = norm[j, at, :] + recur[j] * before[j]
            poly = gelu_inner * (arg * arg) + gelu_outer
            tanh = jnp.tanh(arg * poly)
            half = 0.5 * arg
            state = half + half * tanh
            states[j, at, :] = state
            inner = 3.0 * poly - 2.0 * gelu_outer
            slopes[j, at, :] = (0.5 * tanh + 0.5) + half * (1.0 - tanh * tanh) * inner
            now.append(state)
        return tuple(now)

    unroll = next(k for k in (5, 3, 2, 1) if steps % k == 0)

    def several(i, before):
        for k in range(unroll):
            before = advance(i * unroll + k, before)
        return before

    zero = jnp.zeros((seqs, LANES), f32)
    lax.fori_loop(0, steps // unroll, several, (zero,) * tiles)
    clear_pads(steps, seqs, states)


def run_backward(steps, seqs, tiles, grads, gains, slopes, arg_grads):
    recur = [jnp.broadcast_to(gains[2:3, tile_of(j)], (seqs, LANES)) for j in range(tiles)]
    pitch = arg_grads.shape[1] // seqs

    def retreat(t, after):
        now = []
        at = pl.ds(t, seqs, stride=pitch)
        for j in range(tiles):
            grad = (grads[j, at, :] + recur[j] * after[j]) * slopes[j, at, :]
            arg_grads[j, at, :] = grad
            now.append(grad)
        return tuple(now)

    unroll = next(k for k in (2, 3, 1) if steps % k == 0)

    def several(i, after):
        for k in range(unroll):
            after = retreat(steps - 1 - (i * unroll + k), after)
        return after

    zero = jnp.zeros((seqs, LANES), f32)
    lax.fori_loop(0, steps // unroll, several, (zero,) * tiles)
    clear_pads(steps, seqs, arg_grads)


def back_sums(tiles, arg_grads, proj, states, sums, gains, count, out, shifted):
    rows = proj.shape[1]
    for j in range(tiles):
        mean, scale = stats_of(sums, gains, count, j)
        grad = arg_grads[j]
        out[0:1, tile_of(j)] = scale * jnp.sum(grad * (proj[j] - mean), axis=0, keepdims=True)
        out[1:2, tile_of(j)] = jnp.sum(grad, axis=0, keepdims=True)
        shifted[...] = states(j)
        out[2:3, tile_of(j)] = jnp.sum(
            arg_grads[j, 1:rows, :] * shifted[0 : rows - 1, :], axis=0, keepdims=True
        )


def make_norm(tiles, proj, sums, gains, count, norm):
    for j in tiles:
        mean, scale = stats_of(sums, gains, count, j)
        norm[j] = (proj[j] - mean) * (gains[0:1, tile_of(j)] * scale) + gains[1:2, tile_of(j)]


def load_norm(parts, proj_hbm, proj, sems, sums, gains, count, norm):
    tiles = proj.shape[0]
    size = tiles // parts
    copies = [
        pltpu.make_async_copy(proj_hbm.at[pl.ds(k * size, size)], proj.at[pl.ds(k * size, size)], sems.at[k])
        for k in range(parts)
    ]
    for copy in copies:
        copy.start()

    def finish():
        for k, copy in enumerate(copies):
            copy.wait()
            make_norm(range(k * size, (k + 1) * size), proj, sums, gains, count, norm)

    return finish


parts_in = 4


def first_layer_kernel(
    steps, seqs, count, proj_hbm, sums, gains, top_hbm, bottom_hbm,
    hidden, slopes_hbm, totals, proj_out, moments,
    proj, norm, states, slopes, top, bottom, sems, out_sems,
):
    tiles, rows, _ = proj.shape
    half = tiles * LANES // 2
    finish = load_norm(parts_in, proj_hbm, proj, sems, sums, gains, count, norm)
    weights = [
        pltpu.make_async_copy(top_hbm, top, sems.at[parts_in]),
        pltpu.make_async_copy(bottom_hbm, bottom, sems.at[parts_in + 1]),
    ]
    for copy in weights:
        copy.start()
    finish()
    run_forward(steps, seqs, tiles, norm, gains, states, slopes)
    keep = pltpu.make_async_copy(slopes, slopes_hbm, out_sems.at[0])
    keep.start()
    for j in range(tiles):
        hidden[:, tile_of(j)] = states[j].astype(bf16)
        totals[0:1, tile_of(j)] = jnp.sum(states[j], axis=0, keepdims=True)
    for copy in weights:
        copy.wait()
    sends = []
    for k in range(half // WIDE):
        lanes = pl.ds(k * WIDE, WIDE)
        acc = dot(hidden[:, :half], top[:, lanes], ((1,), (0,))) + dot(hidden[:, half:], bottom[:, lanes], ((1,), (0,)))
        moments[0:1, lanes] = jnp.sum(acc, axis=0, keepdims=True)
        moments[1:2, lanes] = jnp.sum(acc * acc, axis=0, keepdims=True)
        size = WIDE // LANES
        for i in range(size):
            norm[k * size + i] = acc[:, i * LANES : (i + 1) * LANES]
        place = pl.ds(k * size, size)
        sends.append(pltpu.make_async_copy(norm.at[place], proj_out.at[place], out_sems.at[1 + k]))
        sends[-1].start()
    for copy in [keep, *sends]:
        copy.wait()


def first_layer(steps, seqs, count, proj, sums, gains, top, bottom):
    tiles, rows, _ = proj.shape
    width = tiles * LANES
    half = width // 2
    vmem, hbm = pl.BlockSpec(memory_space=pltpu.VMEM), pl.BlockSpec(memory_space=pl.ANY)
    tiled = pltpu.VMEM((tiles, rows, LANES), f32)
    return pl.pallas_call(
        functools.partial(first_layer_kernel, steps, seqs, count),
        in_specs=[hbm, vmem, vmem, hbm, hbm],
        out_specs=[vmem, hbm, vmem, hbm, vmem],
        out_shape=[
            jax.ShapeDtypeStruct((rows, width), bf16),
            jax.ShapeDtypeStruct((tiles, rows, LANES), f32),
            jax.ShapeDtypeStruct((1, width), f32),
            jax.ShapeDtypeStruct((tiles, rows, LANES), f32),
            jax.ShapeDtypeStruct((2, half), f32),
        ],
        scratch_shapes=[tiled] * 4
        + [pltpu.VMEM((half, half), bf16)] * 2
        + [pltpu.SemaphoreType.DMA((parts_in + 2,)), pltpu.SemaphoreType.DMA((1 + half // WIDE,))],
        compiler_params=params(),
        name="first_layer",
    )(proj, sums, gains, top, bottom)


def second_layer_kernel(
    steps, seqs, count, proj_hbm, sums, gains, near_hbm, far_hbm0, far_hbm1,
    near_out, far_out0, far_out1, grads_out, out,
    proj, norm, states, slopes, near, far, shifted, sems, out_sems,
):
    tiles, rows, _ = proj.shape
    half = tiles // 2
    cut = far.shape[1] // 2
    finish = load_norm(parts_in, proj_hbm, proj, sems, sums, gains, count, norm)
    upstream = [
        pltpu.make_async_copy(near_hbm, near, sems.at[parts_in]),
        pltpu.make_async_copy(far_hbm0, far.at[:, :BLOCK], sems.at[parts_in + 1]),
        pltpu.make_async_copy(far_hbm1, far.at[:, BLOCK:], sems.at[parts_in + 2]),
    ]
    for copy in upstream:
        copy.start()
    finish()
    run_forward(steps, seqs, tiles, norm, gains, states, slopes)
    for copy in upstream:
        copy.wait()
    for j in range(half):
        for part, at in ((near, j), (far, half + j)):
            norm[at] = part[:, tile_of(j)].astype(f32)
            part[:, tile_of(j)] = states[at].astype(bf16)
    sends = [
        pltpu.make_async_copy(near, near_out, out_sems.at[0]),
        pltpu.make_async_copy(far.at[:, :cut], far_out0, out_sems.at[1]),
        pltpu.make_async_copy(far.at[:, cut:], far_out1, out_sems.at[2]),
        pltpu.make_async_copy(norm, grads_out, out_sems.at[3]),
    ]
    for copy in sends[:3]:
        copy.start()
    run_backward(steps, seqs, tiles, norm, gains, slopes, norm)
    sends[3].start()
    back_sums(tiles, norm, proj, lambda j: states[j], sums, gains, count, out, shifted)
    for copy in sends:
        copy.wait()


def second_layer(steps, seqs, count, proj, sums, gains, cot_near, cot_far):
    tiles, rows, _ = proj.shape
    width = tiles * LANES
    vmem, hbm = pl.BlockSpec(memory_space=pltpu.VMEM), pl.BlockSpec(memory_space=pl.ANY)
    low = jax.ShapeDtypeStruct((rows, width // 2), bf16)
    low_half = jax.ShapeDtypeStruct((rows, width // 4), bf16)
    return pl.pallas_call(
        functools.partial(second_layer_kernel, steps, seqs, count),
        in_specs=[hbm, vmem, vmem, hbm, hbm, hbm],
        out_specs=[hbm, hbm, hbm, hbm, vmem],
        out_shape=[low, low_half, low_half, jax.ShapeDtypeStruct((tiles, rows, LANES), f32), jax.ShapeDtypeStruct((3, width), f32)],
        scratch_shapes=[pltpu.VMEM((tiles, rows, LANES), f32)] * 4
        + [pltpu.VMEM((rows, width // 2), bf16)] * 2
        + [
            pltpu.VMEM((rows, LANES), f32),
            pltpu.SemaphoreType.DMA((parts_in + 3,)),
            pltpu.SemaphoreType.DMA((4,)),
        ],
        compiler_params=params(),
        name="second_layer",
    )(proj, sums, gains, cot_near, *cot_far)


def first_back_kernel(
    steps, seqs, count, nb, low, *refs,
):
    weights, refs = refs[: 2 * nb], refs[2 * nb :]
    slopes_hbm, hidden_hbm, proj_hbm, sums, gains, grads_out, out, grads, slopes, hidden, proj, shifted, sems = refs
    tiles = proj.shape[0]
    half = weights[0].shape[1]
    j = pl.program_id(0)
    copies = [
        pltpu.make_async_copy(slopes_hbm, slopes, sems.at[0]),
        pltpu.make_async_copy(hidden_hbm, hidden, sems.at[1]),
        pltpu.make_async_copy(proj_hbm, proj, sems.at[2]),
    ]

    @pl.when(j == 0)
    def _():
        for copy in copies:
            copy.start()

    def go(left, right):
        acc = dot(low[:, :half], left[...], ((1,), (1,))) + dot(low[:, half:], right[...], ((1,), (1,)))
        for k in range(WIDE // LANES):
            grads[j * (WIDE // LANES) + k] = acc[:, k * LANES : (k + 1) * LANES]

    for k in range(nb):
        pl.when(j == k)(functools.partial(go, *weights[2 * k : 2 * k + 2]))

    @pl.when(j == nb)
    def _():
        for copy in copies:
            copy.wait()
        run_backward(steps, seqs, tiles, grads, gains, slopes, grads)
        send = pltpu.make_async_copy(grads, grads_out, sems.at[3])
        send.start()
        states = lambda k: hidden[:, tile_of(k)].astype(f32)
        back_sums(tiles, grads, proj, states, sums, gains, count, out, shifted)
        send.wait()


def first_back(steps, seqs, count, low, blocks, slopes, hidden, proj, sums, gains, deps=()):
    tiles, rows, _ = proj.shape
    width = tiles * LANES
    half = width // 2
    nb = len(blocks)
    hbm = pl.BlockSpec(memory_space=pl.ANY)
    operands = [x for pair in blocks for x, _ in pair]
    weights = [pl.BlockSpec((WIDE, half), lambda j, at=at: (at, 0)) for pair in blocks for _, at in pair]
    return pl.pallas_call(
        without(functools.partial(first_back_kernel, steps, seqs, count, nb), 6 + 2 * nb, len(deps)),
        grid=(nb + 1,),
        in_specs=[whole((rows, width)), *weights, hbm, hbm, hbm, whole((2, width)), whole((3, width))] + after(deps),
        out_specs=[hbm, pl.BlockSpec((3, width), lambda j: (0, 0))],
        out_shape=[
            jax.ShapeDtypeStruct((tiles, rows, LANES), f32),
            jax.ShapeDtypeStruct((3, width), f32),
        ],
        scratch_shapes=[
            pltpu.VMEM((tiles, rows, LANES), f32),
            pltpu.VMEM((tiles, rows, LANES), f32),
            pltpu.VMEM((rows, width), bf16),
            pltpu.VMEM((tiles, rows, LANES), f32),
            pltpu.VMEM((rows, LANES), f32),
            pltpu.SemaphoreType.DMA((4,)),
        ],
        compiler_params=params(),
        name="first_back",
    )(low, *operands, slopes, hidden, proj, sums, gains, *deps)


def norm_back(steps, seqs, arg_grads, proj, sums, gains, totals, count, low_ref, columns):
    tiles, rows, _ = proj.shape
    pitch = rows // seqs
    first = steps // 16 * 16
    row = first + lax.broadcasted_iota(jnp.int32, (16, LANES), 0)
    for j in range(tiles):
        mean, scale = stats_of(sums, gains, count, j)
        factor = gains[0:1, tile_of(j)] * scale
        shift_part = factor * totals[1:2, tile_of(j)] / count
        unit_part = factor * scale * totals[0:1, tile_of(j)] / count
        low = (factor * arg_grads[j] - shift_part - (proj[j] - mean) * unit_part).astype(bf16)
        low_ref[:, tile_of(j)] = low
        if columns is None:
            continue
        past = (mean * unit_part - shift_part).astype(bf16).astype(f32)
        column = jnp.sum(low.astype(f32), axis=0, keepdims=True) - (rows - seqs * steps) * past
        high_part = column.astype(bf16).astype(f32)
        low_part = (column - high_part).astype(bf16).astype(f32)
        columns[0:1, tile_of(j)] = high_part + low_part
        edge = low_ref[first : first + 16, tile_of(j)].astype(f32)
        edge = jnp.where(row == steps, high_part, jnp.where(row == steps + 1, low_part, edge))
        low_ref[first : first + 16, tile_of(j)] = edge.astype(bf16)


def weight_kernel(steps, seqs, count, parts, centred, norm_steps, *refs):
    xs, refs = refs[: len(parts)], refs[len(parts) :]
    if centred:
        centre, *refs = refs
    j = pl.program_id(0)
    if norm_steps:
        arg_grads, proj, sums, gains, totals, low_out, columns, left, right, low = refs

        @pl.when(j < norm_steps)
        def _():
            norm_back(steps, seqs, arg_grads, proj, sums, gains, totals, count, low_out, columns if centred else None)
            if not centred:
                columns[...] = jnp.zeros_like(columns)
            low[:, pl.ds(pl.multiple_of(j * BLOCK, BLOCK), BLOCK)] = low_out[...]
    else:
        low, left, right = refs
    half = low.shape[1] // 2

    def go(x):
        value = x[...]
        if centred:
            row = lax.broadcasted_iota(jnp.int32, value.shape, 0)
            minus = jnp.broadcast_to(-centre[...], value.shape)
            value = jnp.where((row == steps) | (row == steps + 1), minus, value.astype(f32)).astype(bf16)
        acc = dot(value, low[...], ((0,), (0,)))
        left[...] = acc[:, :half].astype(left.dtype)
        right[...] = acc[:, half:].astype(right.dtype)

    at = norm_steps
    for x, blocks in zip(xs, parts):
        pl.when((j >= at) & (j < at + blocks))(functools.partial(go, x))
        at += blocks


def weight_grad(steps, seqs, count, xs, grads, centre=None, centre_at=0, deps=()):
    rows = grads[0].shape[-2]
    made = len(grads) == 1
    width = grads[0].shape[1] if made else grads[0].shape[0] * LANES
    half = width // 2
    nb = half // WIDE
    norm_steps = 0 if made else width // BLOCK
    specs, start = [], norm_steps
    for _, first, blocks in xs:
        specs.append(
            pl.BlockSpec((rows, WIDE), lambda j, start=start, first=first, blocks=blocks: (0, first + held(j, start, blocks)))
        )
        start += blocks
    operands = [x for x, _, _ in xs]
    if centre is not None:
        specs.append(pl.BlockSpec((1, WIDE), lambda j: (0, centre_at + held(j, norm_steps, nb))))
        operands.append(centre)
    quarter = pl.BlockSpec((WIDE, half), lambda j: (held(j, norm_steps, nb), 0))
    out_specs, out_shape, scratch = [quarter] * 2, [jax.ShapeDtypeStruct((half, half), bf16)] * 2, []
    if made:
        specs.append(whole((rows, width)))
    else:
        tile_spec = pl.BlockSpec((BLOCK // LANES, rows, LANES), lambda j: (held(j, 0, norm_steps), 0, 0))
        lanes = lambda tall: pl.BlockSpec((tall, BLOCK), lambda j: (0, held(j, 0, norm_steps)))
        specs += [tile_spec, tile_spec, lanes(2), lanes(3), lanes(3)]
        out_specs = [lanes(rows), lanes(1)] + out_specs
        out_shape = [jax.ShapeDtypeStruct((rows, width), bf16), jax.ShapeDtypeStruct((1, width), f32)] + out_shape
        scratch = [pltpu.VMEM((rows, width), bf16)]
    kernel = functools.partial(
        weight_kernel, steps, seqs, count, [b for _, _, b in xs], centre is not None, norm_steps
    )
    return pl.pallas_call(
        without(kernel, len(specs), len(deps), -1 - len(scratch)),
        grid=(norm_steps + nb,),
        in_specs=specs + after(deps),
        out_specs=out_specs + [token_spec],
        out_shape=out_shape + [token_shape],
        scratch_shapes=scratch,
        compiler_params=params(),
        name="weight_grad",
    )(*operands, *grads, *deps)


def row_blocks(left, right):
    pairs = []
    for x in (left, right):
        if isinstance(x, (list, tuple)):
            pairs.append([(part, 0) for part in x])
        else:
            pairs.append([(x, k) for k in range(x.shape[0] // WIDE)])
    return list(zip(*pairs))


def pull_kernel(nb, tiled, low, *refs):
    *weights, out = refs
    j = pl.program_id(0)
    half = weights[0].shape[1]

    def go(left, right):
        acc = dot(low[:, :half], left[...], ((1,), (1,))) + dot(low[:, half:], right[...], ((1,), (1,)))
        if tiled:
            for k in range(WIDE // LANES):
                out[k] = acc[:, k * LANES : (k + 1) * LANES]
        else:
            out[...] = acc.astype(out.dtype)

    for k in range(len(weights) // 2):
        pl.when((j >= k * nb) & (j < (k + 1) * nb))(functools.partial(go, *weights[2 * k : 2 * k + 2]))


def pull(low, left, right, dtype, deps=()):
    rows, width = low.shape
    half = width // 2
    blocks = row_blocks(left, right)
    operands = [x for pair in blocks for x, _ in pair]
    specs = [pl.BlockSpec((WIDE, half), lambda j, at=at: (at, 0)) for pair in blocks for _, at in pair]
    return pl.pallas_call(
        without(functools.partial(pull_kernel, 1, False), 1 + len(operands), len(deps), -1),
        grid=(len(blocks),),
        in_specs=[whole((rows, width))] + specs + after(deps),
        out_specs=[pl.BlockSpec((rows, WIDE), lambda j: (0, j)), token_spec],
        out_shape=[jax.ShapeDtypeStruct((rows, len(blocks) * WIDE), dtype), token_shape],
        compiler_params=params(),
        name="pull",
    )(low, *operands, *deps)


def fold_kernel(counts, at_ref, *refs):
    kept, sent = refs[-2:]
    at = 0
    for k, n in enumerate(counts):
        parts = refs[at : at + 2 * n]
        kept[k] = sum(p[...].astype(f32) for p in parts[:n])
        sent[k] = sum(p[...].astype(f32) for p in parts[n:]).astype(bf16)
        at += 2 * n


def fold(mine, stacks, rows, deps=(), mebibytes=16):
    specs, operands = [], []
    width = stacks[0][0][0].shape[-1]
    cuts = 2
    lanes = width // cuts
    for stack in stacks:
        for side in (0, 1):
            for array, index, base in stack:
                operands.append(array)
                specs.append(
                    pl.BlockSpec(
                        (None, rows, lanes),
                        lambda j, at, side=side, index=index, base=base: (index, base + (at[0] + side) % 2, j),
                    )
                )
    count = len(stacks)
    out_spec = pl.BlockSpec((count, rows, lanes), lambda j, at: (0, 0, j))
    kernel = functools.partial(fold_kernel, [len(stack) for stack in stacks])
    return pl.pallas_call(
        without(kernel, 1 + len(operands), len(deps), -1),
        grid_spec=pltpu.PrefetchScalarGridSpec(
            num_scalar_prefetch=1, grid=(cuts,), in_specs=specs + after(deps), out_specs=[out_spec, out_spec, token_spec]
        ),
        out_shape=[
            jax.ShapeDtypeStruct((count, rows, width), f32),
            jax.ShapeDtypeStruct((count, rows, width), bf16),
            token_shape,
        ],
        compiler_params=params(mebibytes),
        name="fold",
    )(jnp.reshape(mine, (1,)).astype(jnp.int32), *operands, *deps)


def total_kernel(counts, *refs):
    *parts, out = refs
    at = 0
    for k, n in enumerate(counts):
        out[k] = sum(p[...].astype(f32) for p in parts[at : at + n]).astype(bf16)
        at += n


def total(stacks, rows, deps=(), mebibytes=16):
    parts = [part for stack in stacks for part in stack]
    count, width = len(stacks), parts[0][0].shape[-1]
    cuts = 2
    lanes = width // cuts
    specs = [
        pl.BlockSpec((None, rows, lanes), lambda j, index=index, block=block: (index, block, j)) for _, index, block in parts
    ]
    out, done = pl.pallas_call(
        without(functools.partial(total_kernel, [len(stack) for stack in stacks]), len(parts), len(deps), -1),
        grid=(cuts,),
        in_specs=specs + after(deps),
        out_specs=[pl.BlockSpec((count, rows, lanes), lambda j: (0, 0, j)), token_spec],
        out_shape=[jax.ShapeDtypeStruct((count, rows, width), bf16), token_shape],
        compiler_params=params(mebibytes),
        name="total",
    )(*[array for array, _, _ in parts], *deps)
    return out.reshape(count * rows, width), done


def join_kernel(at_ref, own, other, out):
    @pl.when(pl.program_id(0) == 0)
    def _():
        out[...] = own[...]

    @pl.when(pl.program_id(0) == 1)
    def _():
        out[...] = other[...]


def join(mine, own, other, deps=()):
    rows, width = own.shape
    spec = pl.BlockSpec((rows, width), lambda j, at: (0, 0))
    return pl.pallas_call(
        without(join_kernel, 3, len(deps), -1),
        grid_spec=pltpu.PrefetchScalarGridSpec(
            num_scalar_prefetch=1,
            grid=(2,),
            in_specs=[spec, spec] + after(deps),
            out_specs=[pl.BlockSpec((rows, width), lambda j, at: ((at[0] + j) % 2, 0)), token_spec],
        ),
        out_shape=[jax.ShapeDtypeStruct((2 * rows, width), bf16), token_shape],
        compiler_params=params(16),
        name="join",
    )(jnp.reshape(mine, (1,)).astype(jnp.int32), own, other, *deps)


def over(value, axis):
    return lax.ppermute(value, axis, [(0, 1), (1, 0)])


def across(value, bit):
    size = lax.axis_size("dp")
    return lax.ppermute(value, "dp", [(i, i ^ bit) for i in range(size)])


def dp_bits():
    return [1 << k for k in range((lax.axis_size("dp") - 1).bit_length())]


def swap_halves(value):
    half = value.shape[-1] // 2
    return jnp.concatenate([value[:, half:], value[:, :half]], axis=1)


def sum_step(value, step, swaps):
    if step not in ("col", "row"):
        return value + across(value, step)
    other = over(value, step)
    rows = [swap_halves(other[k : k + 1]) if axis == step else other[k : k + 1] for k, axis in enumerate(swaps)]
    return value + jnp.concatenate(rows, axis=0)


def on_device(
    inputs,
    w_second,
    gain_second,
    shift_second,
    recur_second,
    w_third,
    gain_third,
    shift_third,
    recur_third,
    cotangent,
):
    steps, seq_group, width = inputs.shape
    share = cotangent.shape[1]
    seqs = share // lax.axis_size("row")
    pitch = round_up(steps + 2, 8)
    rows = seqs * pitch
    half = round_up(width, 2 * BLOCK)
    nb = half // BLOCK
    tiles = 2 * half // LANES
    pieces = lax.axis_size("dp")
    count = steps * seq_group * pieces
    row, col, place = lax.axis_index("row"), lax.axis_index("col"), lax.axis_index("dp")
    bits = dp_bits()

    def turned(order):
        return sum(((place // bit) % 2) << k for k, bit in enumerate(order))


    def pad_weight(w):
        return jnp.pad(w, ((0, half - w.shape[0]), (0, half - w.shape[1])))

    def pad_params(*vectors):
        return jnp.pad(jnp.stack(vectors), ((0, 0), (0, half - width)))

    def bit_of(bit):
        return (place // bit) % 2

    chunks = 2
    spread = len(bits) > 1 and half // (chunks * pieces) >= 16
    orders = [bits[::-1], bits[:1] + bits[:0:-1]]
    places = jnp.stack([col * share + row * seqs, col * share + (1 - row) * seqs]).astype(jnp.int32)
    parts = jnp.stack([row, 1 - row]).astype(jnp.int32)
    own_second = pad_params(gain_second, shift_second, recur_second)
    own_third = pad_params(gain_third, shift_third, recur_third)
    gains_second = jnp.concatenate([own_second, over(own_second, "col")], axis=1)
    deps = ()
    if spread:
        cut_second, cut_third = cut(w_second, w_third, [turned(order) for order in orders], chunks, pieces, half)
        tall = half // (chunks * pieces)
        deps = (cut_second, cut_third)
    if spread:
        cut_second, w_second, w_third = lax.optimization_barrier((cut_second, w_second, w_third))
        far_second, far_third = over(cut_second, "row"), over(cut_third, "row")
    nn2, nn3 = pad_weight(w_second), pad_weight(w_third)
    nf2, fn3 = over(nn2, "col"), over(nn3, "col")
    x_near, send0 = prep(inputs, places, seqs, pitch, half, 0, nb // 2, None, deps)
    x_near, send1 = prep(inputs, places, seqs, pitch, half, nb // 2, nb // 2, x_near)
    if spread:
        send0, send1, far_second, far_third = lax.optimization_barrier((send0, send1, far_second, far_third))
    x_far0 = over(send0, "row")
    x_far1 = over(send1, "row")
    proj_second, near_done = project([(x_near, 0, half)], [[nn2], [nf2]], tiles)
    cot_near, *cot_send, cot_done = prep_grads(jnp.transpose(cotangent, (1, 0, 2)), parts, seqs, pitch, half)
    if spread:
        fn2 = [far_second[k * tall : (k + 1) * tall] for k in range(chunks)]
        nf3 = far_third
        deps = (near_done,)
        for k in range(len(bits)):
            others = [across(piece, order[k]) for piece, order in zip(fn2, orders)]
            if k > 0:
                nf3_other = across(nf3, orders[0][k - 1])
            joined = [join(bit_of(order[k]), piece, other, deps) for piece, order, other in zip(fn2, orders, others)]
            fn2 = [piece for piece, _ in joined]
            if k == len(bits) - 1:
                break
            deps = (cot_done,)
            if k > 0:
                nf3, done = join(bit_of(orders[0][k - 1]), nf3, nf3_other, tuple(done for _, done in joined))
                deps = (done,)
            if k == len(bits) - 2:
                x_far0, nn3, *fn2 = lax.optimization_barrier((x_far0, nn3, *fn2))
        x_far1, *fn2 = lax.optimization_barrier((x_far1, *fn2))
    else:
        far = over(nn2, "row")
        fn2 = [far[: half // 2], far[half // 2 :]]
        nf3 = over(nn3, "row")
    ff2 = [over(chunk, "col") for chunk in fn2]
    x_parts = [(x_far0, 0, half // 2), (x_far1, 0, half // 2)]
    proj_second, sums_near = project(x_parts, [fn2], tiles, 0, proj_second, True, (cot_done,))
    cot_far0 = over(cot_send[0], "row")
    proj_second, sums_far = project(x_parts, [ff2], tiles, half // WIDE, proj_second, True, (cot_far0,))
    sums = jnp.concatenate([sums_near, sums_far], axis=1)
    if spread:
        nf3, done = join(bit_of(bits[1]), nf3, nf3_other, (sums,))
        sums, done = lax.optimization_barrier((sums, done))

    swaps = ("col", "col")
    sums = sum_step(sums, "row", swaps)
    sums, cot_send1 = lax.optimization_barrier((sums, cot_send[1]))
    cot_far1 = over(cot_send1, "row")
    if spread:
        sums = sum_step(sums, bits[0], swaps)
        sums, nf3 = lax.optimization_barrier((sums, nf3))
        nf3_other = across(nf3, bits[0])
    sums = sum_step(sums, "col", swaps)
    for bit in bits[1:] if spread else bits:
        sums = sum_step(sums, bit, swaps)
    sums_second = sums
    hidden, slopes_second, hidden_sums, proj_third, sums_near = first_layer(
        steps, seqs, count, proj_second, sums_second, gains_second, nn3, fn3
    )
    if spread:
        nf3, done = join(bit_of(bits[0]), nf3, nf3_other, (hidden_sums,))
    ff3 = [over(nf3[k * WIDE : (k + 1) * WIDE], "col") for k in range(half // WIDE)]
    hidden_parts = [(hidden, 0, half)] + [(hidden, (half + k * WIDE) // WIDE, WIDE) for k in range(half // WIDE)]
    proj_third, sums_far = project(
        hidden_parts, [[nf3, *ff3]], tiles, half // WIDE, proj_third, False, (cot_far1,)
    )

    swaps = ("row", "row", "col")
    sums = jnp.concatenate([jnp.concatenate([sums_near, sums_far], axis=1), hidden_sums], axis=0)
    for step in ("col", *bits):
        sums = sum_step(sums, step, swaps)
    other = over(jnp.concatenate([sums, own_third], axis=1), "row")
    sums = sums + jnp.concatenate([swap_halves(other[:2, : 2 * half]), other[2:3, : 2 * half]], axis=0)
    gains_third = jnp.concatenate([own_third, other[:, 2 * half :]], axis=1)
    sums_third, centre = sums[:2], (sums[2:3] / count).astype(bf16).astype(f32)
    states_near, out_send0, out_send1, arg_grads_third, sums = second_layer(
        steps, seqs, count, proj_third, sums_third, gains_third, cot_near, (cot_far0, cot_far1)
    )
    swaps = ("row", "row", "row")
    sums = sum_step(sums, "col", swaps)
    sums = sum_step(sums, "row", swaps)
    sums, out_send0 = lax.optimization_barrier((sums, out_send0))
    out_far0 = over(out_send0, "row")
    for bit in bits:
        sums = sum_step(sums, bit, swaps)
    totals_third = sums

    wide = half // WIDE
    cutting = half // 2
    grads = (arg_grads_third, proj_third, sums_third, gains_third, totals_third)
    low_third, columns, fn, ff, _ = weight_grad(steps, seqs, count, [(hidden, wide, wide)], grads, centre, wide)
    from_fn, from_ff = over(fn, "col"), over(ff, "col")
    nn, nf, done = weight_grad(steps, seqs, count, [(hidden, 0, wide)], (low_third,), centre, 0)

    def begin_across(nn, from_fn, nf, from_ff, deps):
        own, other = [(nn[None], 0), (from_fn[None], 0)], [(nf[None], 0), (from_ff[None], 0)]
        tall = cutting // 2
        stacks = [[(array, index, 2) for array, index in part] for part in (own, other)]
        return fold(bit_of(bits[0]), stacks, tall, deps, 56)

    class Chain:
        def __init__(self, stacks, rows, left):
            self.stacks, self.rows, self.left = stacks, rows, list(left)

        def step(self, deps):
            bit = self.left.pop(0)
            self.rows //= 2
            stacks = [[(array, index, 0) for array, index in stack] for stack in self.stacks]
            kept, sent, done = fold(bit_of(bit), stacks, self.rows, deps)
            other = across(sent, bit)
            self.stacks = [[(kept, k), (other, k)] for k in range(len(stacks))]
            return (done,)

        def piece(self, deps):
            while self.left:
                deps = self.step(deps)
            stacks = [[(array, index, 0) for array, index in stack] for stack in self.stacks]
            self.whole, done = total(stacks, self.rows, deps)
            self.back = list(reversed(bits))
            self.other = across(self.whole, self.back[0])
            return (done,)

        def gather(self, deps):
            bit = self.back.pop(0)
            self.whole, done = join(bit_of(bit), self.whole, self.other, deps)
            if self.back:
                self.other = across(self.whole, self.back[0])
            return (done,)

    x3, done = total([[(nf[None], 0, 0), (from_ff[None], 0, 0)]], cutting, (done,), 56)
    x3_come = over(x3, "row")
    kept, sent, done = begin_across(nn, from_fn, nf, from_ff, (done,))
    b3_kept, b3_other = kept, across(sent, bits[0])
    arg_grads_second, sums = first_back(
        steps, seqs, count, low_third, row_blocks(nn3, nf3) + row_blocks(fn3, ff3), slopes_second, hidden, proj_second, sums_second, gains_second,
        (done, out_far0),
    )
    swaps = ("col", "col", "col", "row")
    sums = jnp.concatenate([sums, columns], axis=0)
    sums, b3_other, x3_come = lax.optimization_barrier((sums, b3_other, x3_come))
    sums = sum_step(sums, "col", swaps)
    sums = sum_step(sums, "row", swaps)
    sums, b3_other = lax.optimization_barrier((sums, b3_other))

    def to_row(kept, other, deps):
        sent, done = total([[(kept, 1, 0), (other, 1, 0)]], cutting // 2, deps)
        return over(sent, "row")[None], done

    def to_across(nn, from_other, come, deps):
        stack = [(nn[None], 0, 0), (from_other[None], 0, 0), (come[None], 0, 0)]
        kept, sent, done = fold(bit_of(bits[0]), [stack], cutting // 2, deps, 56)
        return [(kept, 0), (across(sent, bits[0]), 0)], done

    b3_row, done = to_row(b3_kept, b3_other, ())
    sums = sum_step(sums, bits[0], swaps)
    sums, x3_come = lax.optimization_barrier((sums, x3_come))
    a3, done = to_across(nn, from_fn, x3_come, (done,))
    for bit in bits[1:]:
        sums = sum_step(sums, bit, swaps)
    totals_second, columns = sums[:3], sums[3:4]
    c3 = Chain([a3, [(b3_kept, 0), (b3_other, 0), (b3_row, 0)]], cutting // 2, bits[1:])
    totals_second, done, out_send1 = lax.optimization_barrier((totals_second, done, out_send1))
    out_far1 = over(out_send1, "row")
    seen = c3.step((done,))

    grads = (arg_grads_second, proj_second, sums_second, gains_second, totals_second)
    low_second, seen, fn, ff, _ = weight_grad(steps, seqs, count, [(x_far0, 0, 1), (x_far1, 0, 1)], grads, deps=seen)
    from_ff = over(ff, "col")
    seen = c3.step((seen, out_far1)) if c3.left else (seen, out_far1)
    nn, nf, done = weight_grad(steps, seqs, count, [(x_near, 0, wide)], (low_second,), deps=seen)
    from_nf = over(nf, "col")
    x2, done = total([[(fn[None], 0, 0), (from_ff[None], 0, 0)]], cutting, (done,), 56)
    x2_come = over(x2, "row")
    kept, sent, done = begin_across(nn, from_nf, fn, from_ff, (done,))
    b2_kept, b2_other = kept, across(sent, bits[0])
    grad_far, done = pull(low_second, fn2, ff2, bf16, (done,))
    seen = c3.piece((done,))
    output, done = combine(parts, x_near, states_near, (send0, send1), (out_far0, out_far1), seqs, steps, width, seen)
    b2_row, done = to_row(b2_kept, b2_other, (done,))
    a2, done = to_across(nn, from_nf, x2_come, (done,))
    seen = c3.gather((done,))
    grad_near, done = pull(low_second, nn2, nf2, f32, seen)
    seen = (done,)
    b2 = Chain([[(b2_kept, 0), (b2_other, 0), (b2_row, 0)]], cutting // 2, bits[1:])
    seen = b2.step(seen)
    grad_far, done = lax.optimization_barrier((grad_far, *seen))
    grad_far = over(grad_far, "row")
    a2 = Chain([a2], cutting // 2, bits[1:])
    seen = a2.step((done,))
    seen = c3.gather(seen) if c3.back else seen
    seen = b2.step(seen) if b2.left else seen
    seen = a2.step(seen) if a2.left else seen
    seen = b2.piece(seen)
    seen = c3.gather(seen) if c3.back else seen
    seen = a2.piece(seen)
    seen = b2.gather(seen)
    seen = a2.gather(seen)
    seen = b2.gather(seen)
    seen = a2.gather(seen)
    grad_inputs, done = combine(
        parts, cot_near, grad_near, cot_send, (grad_far,), seqs, steps, width, seen
    )
    seen = (done,)
    chains = [c3, b2, a2]
    while any(chain.back for chain in chains):
        for chain in chains:
            if chain.back:
                seen = chain.gather(seen)
    grad_w_third = jnp.transpose(c3.whole.reshape(pieces, 2, -1, half), (1, 0, 2, 3)).reshape(half, half)
    grad_w_second = jnp.concatenate([a2.whole, b2.whole], axis=0)

    output = jnp.transpose(output, (1, 0, 2))
    grad_inputs = jnp.transpose(grad_inputs, (1, 0, 2))
    restore = centre[0, :width, None] * columns[0, None, :width]
    return (
        output,
        grad_inputs,
        grad_w_second[:width, :width].astype(f32),
        totals_second[0, :width],
        totals_second[1, :width],
        totals_second[2, :width],
        grad_w_third[:width, :width].astype(f32) + restore,
        totals_third[0, :width],
        totals_third[1, :width],
        totals_third[2, :width],
    )


def solution(mesh):
    in_specs = (
        P(None, "dp", "row"),
        P("row", "col"),
        P("col"),
        P("col"),
        P("col"),
        P("col", "row"),
        P("row"),
        P("row"),
        P("row"),
        P(None, ("dp", "col"), "row"),
    )
    out_specs = (
        P(None, ("dp", "col"), "row"),
        P(None, ("dp", "col"), "row"),
        P("row", "col"),
        P("col"),
        P("col"),
        P("col"),
        P("col", "row"),
        P("row"),
        P("row"),
        P("row"),
    )
    return jax.shard_map(
        on_device, mesh=mesh, in_specs=in_specs, out_specs=out_specs, check_vma=False
    )
```

```python
import functools

import jax
import jax.numpy as jnp
from jax import lax
from jax.experimental import pallas as pl
from jax.experimental.pallas import tpu as pltpu
from jax.sharding import PartitionSpec as P

norm_eps = 1e-05
gelu_outer = 0.7978845608028654
gelu_inner = gelu_outer * 0.044715
LANES = 128
BLOCK = 256
WIDE = 512
f32 = jnp.float32
bf16 = jnp.bfloat16


def params(mebibytes=56):
    return pltpu.CompilerParams(vmem_limit_bytes=mebibytes * 2**20)


def round_up(value, unit):
    return -(-value // unit) * unit


def after(deps):
    return [pl.BlockSpec(memory_space=pl.ANY)] * len(deps)


def without(kernel, at, count, token=None):
    def body(*refs):
        refs = list(refs)
        if token is not None:
            refs.pop(token)[...] = jnp.zeros((8, LANES), f32)
        kernel(*refs[:at], *refs[at + count :])

    return body


token_spec = pl.BlockSpec((8, LANES), lambda *_: (0, 0))
token_shape = jax.ShapeDtypeStruct((8, LANES), f32)


def whole(shape):
    return pl.BlockSpec(shape, lambda *_: (0,) * len(shape), pipeline_mode=pl.Buffered(1))


def dot(left, right, dims):
    return lax.dot_general(left, right, (dims, ((), ())), preferred_element_type=f32)


def tile_of(j):
    return pl.ds(j * LANES, LANES)


def held(j, low, count):
    return jnp.clip(j - low, 0, count - 1)


def prep_kernel(seqs, pitch, width, base, at_ref, inputs, *refs):
    near, send, scratch, packed = refs[-4:]
    steps, group, block = inputs.shape
    lane = base + pl.program_id(0) * block + lax.broadcasted_iota(jnp.int32, (1, LANES), 1)
    rows = near.shape[0]
    for k in range(block // LANES):
        scratch[...] = inputs[:, :, tile_of(k)].astype(f32).reshape(steps * group, LANES)
        for place, out in ((0, near), (1, send)):
            first = at_ref[place]
            for s in range(seqs):
                packed[s * pitch : s * pitch + steps, :] = scratch[pl.ds(first + s, steps, stride=group), :]
                packed[s * pitch + steps : (s + 1) * pitch, :] = jnp.zeros((pitch - steps, LANES), f32)
            out[:, tile_of(k)] = jnp.where(lane + k * LANES < width, packed[...], 0.0).astype(bf16)


def prep(inputs, places, seqs, pitch, half, first, blocks, near=None, deps=()):
    steps, group, width = inputs.shape
    rows = seqs * pitch
    near_spec = pl.BlockSpec((rows, BLOCK), lambda j, at: (0, j + first))
    return pl.pallas_call(
        without(functools.partial(prep_kernel, seqs, pitch, width, first * BLOCK), 2, len(deps)),
        grid_spec=pltpu.PrefetchScalarGridSpec(
            num_scalar_prefetch=1,
            grid=(blocks,),
            in_specs=[pl.BlockSpec((steps, group, BLOCK), lambda j, at: (0, 0, j + first))]
            + after(deps)
            + ([] if near is None else [pl.BlockSpec(memory_space=pl.ANY)]),
            out_specs=[near_spec, pl.BlockSpec((rows, BLOCK), lambda j, at: (0, j))],
            scratch_shapes=[pltpu.VMEM((steps * group, LANES), f32), pltpu.VMEM((rows, LANES), f32)],
        ),
        out_shape=[
            jax.ShapeDtypeStruct((rows, half), bf16),
            jax.ShapeDtypeStruct((rows, blocks * BLOCK), bf16),
        ],
        input_output_aliases={} if near is None else {2 + len(deps): 0},
        compiler_params=params(),
        name="prep",
    )(places, inputs, *deps, *(() if near is None else (near,)))


def prep_grads_kernel(pitch, width, at_ref, own, other, near, send0, send1, packed):
    seqs, steps, block = own.shape
    lane = pl.program_id(0) * block + lax.broadcasted_iota(jnp.int32, (1, block), 1)

    def pack(part, out):
        for s in range(seqs):
            packed[s * pitch : s * pitch + steps, :] = part[s].astype(f32)
            packed[s * pitch + steps : (s + 1) * pitch, :] = jnp.zeros((pitch - steps, block), f32)
        out[...] = jnp.where(lane < width, packed[...], 0.0).astype(bf16)

    pack(own, near)
    pl.when(pl.program_id(0) == 0)(lambda: pack(other, send0))
    pl.when(pl.program_id(0) > 0)(lambda: pack(other, send1))


def prep_grads(grads, places, seqs, pitch, half):
    _, steps, width = grads.shape
    rows = seqs * pitch
    out = pl.BlockSpec((rows, BLOCK), lambda j, at: (0, j))
    return pl.pallas_call(
        without(functools.partial(prep_grads_kernel, pitch, width), 0, 0, -2),
        grid_spec=pltpu.PrefetchScalarGridSpec(
            num_scalar_prefetch=1,
            grid=(half // BLOCK,),
            in_specs=[
                pl.BlockSpec((seqs, steps, BLOCK), lambda j, at: (at[0], 0, j)),
                pl.BlockSpec((seqs, steps, BLOCK), lambda j, at: (at[1], 0, j)),
            ],
            out_specs=[
                out,
                pl.BlockSpec((rows, BLOCK), lambda j, at: (0, 0)),
                pl.BlockSpec((rows, BLOCK), lambda j, at: (0, jnp.maximum(j - 1, 0))),
                token_spec,
            ],
            scratch_shapes=[pltpu.VMEM((rows, BLOCK), f32)],
        ),
        out_shape=[jax.ShapeDtypeStruct((rows, lanes), bf16) for lanes in (half, BLOCK, half - BLOCK)] + [token_shape],
        compiler_params=params(),
        name="prep_grads",
    )(places, grads, grads)


def combine_kernel(pitch, counts, at_ref, *refs):
    *parts, out = refs
    seqs, steps, width = out.shape

    def put(a, b):
        a, b = (jnp.concatenate([part[...].astype(f32) for part in x], axis=1) for x in (a, b))
        total = a + b
        for s in range(seqs):
            out[s] = total[s * pitch : s * pitch + steps, :width]

    near, b_near, *far = parts
    cut = counts[0]
    pl.when(pl.program_id(0) == 0)(lambda: put([near], [b_near]))
    pl.when(pl.program_id(0) == 1)(lambda: put(far[:cut], far[cut:]))


def combine(places, a_near, b_near, a_far, b_far, seqs, steps, width, deps=()):
    rows = a_near.shape[0]
    pitch = rows // seqs
    group = 2 if seqs % 2 == 0 and 2 * pitch % 16 == 0 else seqs
    nb = seqs // group
    near_at = lambda p, j, at: (jnp.where(p == 0, j, nb - 1), 0)
    far_at = lambda p, j, at: (jnp.where(p == 0, 0, j), 0)
    operands = [a_near, b_near, *a_far, *b_far]
    specs = [pl.BlockSpec((group * pitch, x.shape[1]), near_at if k < 2 else far_at) for k, x in enumerate(operands)]
    return pl.pallas_call(
        without(functools.partial(combine_kernel, pitch, [len(a_far)]), 1 + len(operands), len(deps), -1),
        grid_spec=pltpu.PrefetchScalarGridSpec(
            num_scalar_prefetch=1,
            grid=(2, nb),
            in_specs=specs + after(deps),
            out_specs=[pl.BlockSpec((group, steps, width), lambda p, j, at: (at[p] * nb + j, 0, 0)), token_spec],
        ),
        out_shape=[jax.ShapeDtypeStruct((2 * seqs, steps, width), f32), token_shape],
        compiler_params=params(24),
        name="combine",
    )(places, *operands, *deps)


def cut_kernel(pieces, chunks, limit, at_ref, second, third, out_second, out_third):
    tall, wide = out_second.shape
    j = pl.program_id(0)
    lane = lax.broadcasted_iota(jnp.int32, (tall, wide), 1)
    for block, weight, out in ((j * pieces + at_ref[j], second, out_second), (at_ref[0] * chunks + j, third, out_third)):
        row = block * tall + lax.broadcasted_iota(jnp.int32, (tall, wide), 0)
        out[...] = jnp.where((row < limit) & (lane < limit), weight[...].astype(f32), 0.0).astype(bf16)


def cut(second, third, places, chunks, pieces, half):
    tall = half // (chunks * pieces)
    out_spec = pl.BlockSpec((tall, half), lambda j, at: (j, 0))
    return pl.pallas_call(
        functools.partial(cut_kernel, pieces, chunks, second.shape[0]),
        grid_spec=pltpu.PrefetchScalarGridSpec(
            num_scalar_prefetch=1,
            grid=(chunks,),
            in_specs=[
                pl.BlockSpec((tall, half), lambda j, at: (j * pieces + at[j], 0)),
                pl.BlockSpec((tall, half), lambda j, at: (at[0] * chunks + j, 0)),
            ],
            out_specs=[out_spec, out_spec],
        ),
        out_shape=[jax.ShapeDtypeStruct((chunks * tall, half), bf16)] * 2,
        compiler_params=params(),
        name="cut",
    )(jnp.stack(places).astype(jnp.int32), second, third)


def project_kernel(parts, halves, add, nb, *refs):
    xs = refs[:parts]
    ws = [refs[parts * (1 + h) : parts * (2 + h)] for h in range(halves)]
    refs = refs[parts * (1 + halves) :]
    proj, sums = refs[-2:]
    j = pl.program_id(0)

    def go(weights):
        acc = sum(dot(x[...], w[...], ((1,), (0,))) for x, w in zip(xs, weights))
        if add:
            acc = acc + jnp.concatenate([refs[0][k] for k in range(WIDE // LANES)], axis=1)
        for k in range(WIDE // LANES):
            proj[k] = acc[:, k * LANES : (k + 1) * LANES]
        sums[0:1, :] = jnp.sum(acc, axis=0, keepdims=True)
        sums[1:2, :] = jnp.sum(acc * acc, axis=0, keepdims=True)

    for h in range(halves):
        pl.when((j >= h * nb) & (j < (h + 1) * nb))(functools.partial(go, ws[h]))


def project(xs, ws, tiles, first=0, before=None, add=False, deps=()):
    rows = xs[0][0].shape[0]
    half = ws[0][0].shape[1]
    nb = half // WIDE
    specs, operands = [], []
    for x, at, depth in xs:
        specs.append(pl.BlockSpec((rows, depth), lambda j, at=at: (0, at), pipeline_mode=pl.Buffered(1)))
        operands.append(x)
    for h, weights in enumerate(ws):
        for w, (_, _, depth) in zip(weights, xs):
            specs.append(pl.BlockSpec((depth, WIDE), lambda j, h=h: (0, held(j, h * nb, nb))))
            operands.append(w)
    tile_spec = pl.BlockSpec((WIDE // LANES, rows, LANES), lambda j: (j + first, 0, 0))
    aliases = {}
    if before is not None:
        aliases = {len(operands): 0}
        operands.append(before)
        specs.append(tile_spec if add else pl.BlockSpec(memory_space=pl.ANY))
    width = len(ws) * half
    kernel = functools.partial(project_kernel, len(xs), len(ws), add, nb)
    return pl.pallas_call(
        without(kernel, len(operands), len(deps)),
        grid=(len(ws) * nb,),
        in_specs=specs + after(deps),
        out_specs=[tile_spec, pl.BlockSpec((2, WIDE), lambda j: (0, j))],
        out_shape=[
            jax.ShapeDtypeStruct((tiles, rows, LANES), f32),
            jax.ShapeDtypeStruct((2, width), f32),
        ],
        input_output_aliases=aliases,
        compiler_params=params(),
        name="project",
    )(*operands, *deps)


def stats_of(sums, gains, count, j):
    mean = sums[0:1, tile_of(j)] / count
    var = sums[1:2, tile_of(j)] / count - mean * mean
    scale = lax.rsqrt(var + norm_eps)
    return mean, scale


def clear_pads(steps, seqs, array):
    tiles, rows, _ = array.shape
    pitch = rows // seqs
    if pitch > steps:
        for j in range(tiles):
            for s in range(seqs):
                array[j, s * pitch + steps : (s + 1) * pitch, :] = jnp.zeros((pitch - steps, LANES), f32)


def run_forward(steps, seqs, tiles, norm, gains, states, slopes):
    recur = [jnp.broadcast_to(gains[2:3, tile_of(j)], (seqs, LANES)) for j in range(tiles)]
    pitch = norm.shape[1] // seqs

    def advance(t, before):
        now = []
        at = pl.ds(t, seqs, stride=pitch)
        for j in range(tiles):
            arg = norm[j, at, :] + recur[j] * before[j]
            poly = gelu_inner * (arg * arg) + gelu_outer
            gate = 0.5 * jnp.tanh(arg * poly) + 0.5
            state = arg * gate
            states[j, at, :] = state
            inner = 6.0 * poly - 4.0 * gelu_outer
            slopes[j, at, :] = gate + state * (1.0 - gate) * inner
            now.append(state)
        return tuple(now)

    unroll = next(k for k in (5, 3, 2, 1) if steps % k == 0)

    def several(i, before):
        for k in range(unroll):
            before = advance(i * unroll + k, before)
        return before

    zero = jnp.zeros((seqs, LANES), f32)
    lax.fori_loop(0, steps // unroll, several, (zero,) * tiles)
    clear_pads(steps, seqs, states)


def run_backward(steps, seqs, tiles, grads, gains, slopes, arg_grads):
    recur = [jnp.broadcast_to(gains[2:3, tile_of(j)], (seqs, LANES)) for j in range(tiles)]
    pitch = arg_grads.shape[1] // seqs

    def retreat(t, after):
        now = []
        at = pl.ds(t, seqs, stride=pitch)
        for j in range(tiles):
            grad = (grads[j, at, :] + recur[j] * after[j]) * slopes[j, at, :]
            arg_grads[j, at, :] = grad
            now.append(grad)
        return tuple(now)

    unroll = next(k for k in (2, 3, 1) if steps % k == 0)

    def several(i, after):
        for k in range(unroll):
            after = retreat(steps - 1 - (i * unroll + k), after)
        return after

    zero = jnp.zeros((seqs, LANES), f32)
    lax.fori_loop(0, steps // unroll, several, (zero,) * tiles)
    clear_pads(steps, seqs, arg_grads)


def back_sums(tiles, arg_grads, proj, states, sums, gains, count, out, shifted):
    rows = proj.shape[1]
    for j in range(tiles):
        mean, scale = stats_of(sums, gains, count, j)
        grad = arg_grads[j]
        out[0:1, tile_of(j)] = scale * jnp.sum(grad * (proj[j] - mean), axis=0, keepdims=True)
        out[1:2, tile_of(j)] = jnp.sum(grad, axis=0, keepdims=True)
        shifted[...] = states(j)
        out[2:3, tile_of(j)] = jnp.sum(
            arg_grads[j, 1:rows, :] * shifted[0 : rows - 1, :], axis=0, keepdims=True
        )


def make_norm(tiles, proj, sums, gains, count, norm):
    for j in tiles:
        mean, scale = stats_of(sums, gains, count, j)
        norm[j] = (proj[j] - mean) * (gains[0:1, tile_of(j)] * scale) + gains[1:2, tile_of(j)]


def load_norm(parts, proj_hbm, proj, sems, sums, gains, count, norm):
    tiles = proj.shape[0]
    size = tiles // parts
    copies = [
        pltpu.make_async_copy(proj_hbm.at[pl.ds(k * size, size)], proj.at[pl.ds(k * size, size)], sems.at[k])
        for k in range(parts)
    ]
    for copy in copies:
        copy.start()

    def finish():
        for k, copy in enumerate(copies):
            copy.wait()
            make_norm(range(k * size, (k + 1) * size), proj, sums, gains, count, norm)

    return finish


parts_in = 4


def first_layer_kernel(
    steps, seqs, count, proj_hbm, sums, gains, top_hbm, bottom_hbm,
    hidden, slopes_hbm, totals, proj_out, moments,
    proj, norm, states, slopes, top, bottom, sems, out_sems,
):
    tiles, rows, _ = proj.shape
    half = tiles * LANES // 2
    finish = load_norm(parts_in, proj_hbm, proj, sems, sums, gains, count, norm)
    weights = [
        pltpu.make_async_copy(top_hbm, top, sems.at[parts_in]),
        pltpu.make_async_copy(bottom_hbm, bottom, sems.at[parts_in + 1]),
    ]
    for copy in weights:
        copy.start()
    finish()
    run_forward(steps, seqs, tiles, norm, gains, states, slopes)
    keep = pltpu.make_async_copy(slopes, slopes_hbm, out_sems.at[0])
    keep.start()
    for j in range(tiles):
        hidden[:, tile_of(j)] = states[j].astype(bf16)
        totals[0:1, tile_of(j)] = jnp.sum(states[j], axis=0, keepdims=True)
    for copy in weights:
        copy.wait()
    sends = []
    for k in range(half // WIDE):
        lanes = pl.ds(k * WIDE, WIDE)
        acc = dot(hidden[:, :half], top[:, lanes], ((1,), (0,))) + dot(hidden[:, half:], bottom[:, lanes], ((1,), (0,)))
        moments[0:1, lanes] = jnp.sum(acc, axis=0, keepdims=True)
        moments[1:2, lanes] = jnp.sum(acc * acc, axis=0, keepdims=True)
        size = WIDE // LANES
        for i in range(size):
            norm[k * size + i] = acc[:, i * LANES : (i + 1) * LANES]
        place = pl.ds(k * size, size)
        sends.append(pltpu.make_async_copy(norm.at[place], proj_out.at[place], out_sems.at[1 + k]))
        sends[-1].start()
    for copy in [keep, *sends]:
        copy.wait()


def first_layer(steps, seqs, count, proj, sums, gains, top, bottom):
    tiles, rows, _ = proj.shape
    width = tiles * LANES
    half = width // 2
    vmem, hbm = pl.BlockSpec(memory_space=pltpu.VMEM), pl.BlockSpec(memory_space=pl.ANY)
    tiled = pltpu.VMEM((tiles, rows, LANES), f32)
    return pl.pallas_call(
        functools.partial(first_layer_kernel, steps, seqs, count),
        in_specs=[hbm, vmem, vmem, hbm, hbm],
        out_specs=[vmem, hbm, vmem, hbm, vmem],
        out_shape=[
            jax.ShapeDtypeStruct((rows, width), bf16),
            jax.ShapeDtypeStruct((tiles, rows, LANES), f32),
            jax.ShapeDtypeStruct((1, width), f32),
            jax.ShapeDtypeStruct((tiles, rows, LANES), f32),
            jax.ShapeDtypeStruct((2, half), f32),
        ],
        scratch_shapes=[tiled] * 4
        + [pltpu.VMEM((half, half), bf16)] * 2
        + [pltpu.SemaphoreType.DMA((parts_in + 2,)), pltpu.SemaphoreType.DMA((1 + half // WIDE,))],
        compiler_params=params(),
        name="first_layer",
    )(proj, sums, gains, top, bottom)


def second_layer_kernel(
    steps, seqs, count, proj_hbm, sums, gains, near_hbm, far_hbm0, far_hbm1,
    near_out, far_out0, far_out1, grads_out, out,
    proj, norm, states, slopes, near, far, shifted, sems, out_sems,
):
    tiles, rows, _ = proj.shape
    half = tiles // 2
    cut = far.shape[1] // 2
    finish = load_norm(parts_in, proj_hbm, proj, sems, sums, gains, count, norm)
    upstream = [
        pltpu.make_async_copy(near_hbm, near, sems.at[parts_in]),
        pltpu.make_async_copy(far_hbm0, far.at[:, :BLOCK], sems.at[parts_in + 1]),
        pltpu.make_async_copy(far_hbm1, far.at[:, BLOCK:], sems.at[parts_in + 2]),
    ]
    for copy in upstream:
        copy.start()
    finish()
    run_forward(steps, seqs, tiles, norm, gains, states, slopes)
    for copy in upstream:
        copy.wait()
    for j in range(half):
        for part, at in ((near, j), (far, half + j)):
            norm[at] = part[:, tile_of(j)].astype(f32)
            part[:, tile_of(j)] = states[at].astype(bf16)
    sends = [
        pltpu.make_async_copy(near, near_out, out_sems.at[0]),
        pltpu.make_async_copy(far.at[:, :cut], far_out0, out_sems.at[1]),
        pltpu.make_async_copy(far.at[:, cut:], far_out1, out_sems.at[2]),
        pltpu.make_async_copy(norm, grads_out, out_sems.at[3]),
    ]
    for copy in sends[:3]:
        copy.start()
    run_backward(steps, seqs, tiles, norm, gains, slopes, norm)
    sends[3].start()
    back_sums(tiles, norm, proj, lambda j: states[j], sums, gains, count, out, shifted)
    for copy in sends:
        copy.wait()


def second_layer(steps, seqs, count, proj, sums, gains, cot_near, cot_far):
    tiles, rows, _ = proj.shape
    width = tiles * LANES
    vmem, hbm = pl.BlockSpec(memory_space=pltpu.VMEM), pl.BlockSpec(memory_space=pl.ANY)
    low = jax.ShapeDtypeStruct((rows, width // 2), bf16)
    low_half = jax.ShapeDtypeStruct((rows, width // 4), bf16)
    return pl.pallas_call(
        functools.partial(second_layer_kernel, steps, seqs, count),
        in_specs=[hbm, vmem, vmem, hbm, hbm, hbm],
        out_specs=[hbm, hbm, hbm, hbm, vmem],
        out_shape=[low, low_half, low_half, jax.ShapeDtypeStruct((tiles, rows, LANES), f32), jax.ShapeDtypeStruct((3, width), f32)],
        scratch_shapes=[pltpu.VMEM((tiles, rows, LANES), f32)] * 4
        + [pltpu.VMEM((rows, width // 2), bf16)] * 2
        + [
            pltpu.VMEM((rows, LANES), f32),
            pltpu.SemaphoreType.DMA((parts_in + 3,)),
            pltpu.SemaphoreType.DMA((4,)),
        ],
        compiler_params=params(),
        name="second_layer",
    )(proj, sums, gains, cot_near, *cot_far)


def first_back_kernel(
    steps, seqs, count, blocks, low, *refs,
):
    nb = len(blocks)
    weights, refs = refs[: 2 * nb], refs[2 * nb :]
    (
        slopes_hbm, hidden_hbm, proj_hbm, sums, gains, grads_out, out,
        grads, slopes, hidden, proj, shifted, held_blocks, sems, block_sems,
    ) = refs
    tiles = proj.shape[0]
    j = pl.program_id(0)
    fetches = fetch_blocks(blocks, weights, held_blocks, block_sems)
    copies = [
        pltpu.make_async_copy(slopes_hbm, slopes, sems.at[0]),
        pltpu.make_async_copy(hidden_hbm, hidden, sems.at[1]),
        pltpu.make_async_copy(proj_hbm, proj, sems.at[2]),
    ]

    @pl.when(j == 0)
    def _():
        for copy in fetches + copies:
            copy.start()

    @pl.when(j < nb)
    def _():
        acc = block_product(low, held_blocks, block_sems, j)
        for k in range(WIDE // LANES):
            grads[j * (WIDE // LANES) + k] = acc[:, k * LANES : (k + 1) * LANES]

    @pl.when(j == nb)
    def _():
        for copy in copies:
            copy.wait()
        run_backward(steps, seqs, tiles, grads, gains, slopes, grads)
        send = pltpu.make_async_copy(grads, grads_out, sems.at[3])
        send.start()
        states = lambda k: hidden[:, tile_of(k)].astype(f32)
        back_sums(tiles, grads, proj, states, sums, gains, count, out, shifted)
        send.wait()


def first_back(steps, seqs, count, low, blocks, slopes, hidden, proj, sums, gains, deps=()):
    tiles, rows, _ = proj.shape
    width = tiles * LANES
    half = width // 2
    nb = len(blocks)
    hbm = pl.BlockSpec(memory_space=pl.ANY)
    operands = [x for pair in blocks for x, _ in pair]
    weights = [hbm] * len(operands)
    return pl.pallas_call(
        without(functools.partial(first_back_kernel, steps, seqs, count, blocks), 6 + 2 * nb, len(deps)),
        grid=(nb + 1,),
        in_specs=[whole((rows, width)), *weights, hbm, hbm, hbm, whole((2, width)), whole((3, width))] + after(deps),
        out_specs=[hbm, pl.BlockSpec((3, width), lambda j: (0, 0))],
        out_shape=[
            jax.ShapeDtypeStruct((tiles, rows, LANES), f32),
            jax.ShapeDtypeStruct((3, width), f32),
        ],
        scratch_shapes=[
            pltpu.VMEM((tiles, rows, LANES), f32),
            pltpu.VMEM((tiles, rows, LANES), f32),
            pltpu.VMEM((rows, width), bf16),
            pltpu.VMEM((tiles, rows, LANES), f32),
            pltpu.VMEM((rows, LANES), f32),
            pltpu.VMEM((nb, 2, WIDE, half), bf16),
            pltpu.SemaphoreType.DMA((4,)),
            pltpu.SemaphoreType.DMA((nb, 2)),
        ],
        compiler_params=params(),
        name="first_back",
    )(low, *operands, slopes, hidden, proj, sums, gains, *deps)


def norm_back(steps, seqs, arg_grads, proj, sums, gains, totals, count, low_ref, columns):
    tiles, rows, _ = proj.shape
    pitch = rows // seqs
    first = steps // 16 * 16
    row = first + lax.broadcasted_iota(jnp.int32, (16, LANES), 0)
    for j in range(tiles):
        mean, scale = stats_of(sums, gains, count, j)
        factor = gains[0:1, tile_of(j)] * scale
        shift_part = factor * totals[1:2, tile_of(j)] / count
        unit_part = factor * scale * totals[0:1, tile_of(j)] / count
        low = (factor * arg_grads[j] - shift_part - (proj[j] - mean) * unit_part).astype(bf16)
        low_ref[:, tile_of(j)] = low
        if columns is None:
            continue
        past = (mean * unit_part - shift_part).astype(bf16).astype(f32)
        column = jnp.sum(low.astype(f32), axis=0, keepdims=True) - (rows - seqs * steps) * past
        high_part = column.astype(bf16).astype(f32)
        low_part = (column - high_part).astype(bf16).astype(f32)
        columns[0:1, tile_of(j)] = high_part + low_part
        edge = low_ref[first : first + 16, tile_of(j)].astype(f32)
        edge = jnp.where(row == steps, high_part, jnp.where(row == steps + 1, low_part, edge))
        low_ref[first : first + 16, tile_of(j)] = edge.astype(bf16)


def weight_kernel(steps, seqs, count, parts, centred, norm_steps, *refs):
    xs, refs = refs[: len(parts)], refs[len(parts) :]
    if centred:
        centre, *refs = refs
    j = pl.program_id(0)
    if norm_steps:
        arg_grads, proj, sums, gains, totals, low_out, columns, left, right, low = refs

        @pl.when(j < norm_steps)
        def _():
            norm_back(steps, seqs, arg_grads, proj, sums, gains, totals, count, low_out, columns if centred else None)
            if not centred:
                columns[...] = jnp.zeros_like(columns)
            low[:, pl.ds(pl.multiple_of(j * WIDE, WIDE), WIDE)] = low_out[...]
    else:
        low, left, right = refs
    half = low.shape[1] // 2

    def go(x):
        value = x[...]
        if centred:
            row = lax.broadcasted_iota(jnp.int32, value.shape, 0)
            minus = jnp.broadcast_to(-centre[...], value.shape)
            value = jnp.where((row == steps) | (row == steps + 1), minus, value.astype(f32)).astype(bf16)
        acc = dot(value, low[...], ((0,), (0,)))
        left[...] = acc[:, :half].astype(left.dtype)
        right[...] = acc[:, half:].astype(right.dtype)

    at = norm_steps
    for x, blocks in zip(xs, parts):
        pl.when((j >= at) & (j < at + blocks))(functools.partial(go, x))
        at += blocks


def weight_grad(steps, seqs, count, xs, grads, centre=None, centre_at=0, deps=()):
    rows = grads[0].shape[-2]
    made = len(grads) == 1
    width = grads[0].shape[1] if made else grads[0].shape[0] * LANES
    half = width // 2
    nb = half // WIDE
    norm_steps = 0 if made else width // WIDE
    specs, start = [], norm_steps
    for _, first, blocks in xs:
        specs.append(
            pl.BlockSpec((rows, WIDE), lambda j, start=start, first=first, blocks=blocks: (0, first + held(j, start, blocks)))
        )
        start += blocks
    operands = [x for x, _, _ in xs]
    if centre is not None:
        specs.append(pl.BlockSpec((1, WIDE), lambda j: (0, centre_at + held(j, norm_steps, nb))))
        operands.append(centre)
    quarter = pl.BlockSpec((WIDE, half), lambda j: (held(j, norm_steps, nb), 0))
    out_specs, out_shape, scratch = [quarter] * 2, [jax.ShapeDtypeStruct((half, half), bf16)] * 2, []
    if made:
        specs.append(whole((rows, width)))
    else:
        tile_spec = pl.BlockSpec((WIDE // LANES, rows, LANES), lambda j: (held(j, 0, norm_steps), 0, 0))
        lanes = lambda tall: pl.BlockSpec((tall, WIDE), lambda j: (0, held(j, 0, norm_steps)))
        specs += [tile_spec, tile_spec, lanes(2), lanes(3), lanes(3)]
        out_specs = [lanes(rows), lanes(1)] + out_specs
        out_shape = [jax.ShapeDtypeStruct((rows, width), bf16), jax.ShapeDtypeStruct((1, width), f32)] + out_shape
        scratch = [pltpu.VMEM((rows, width), bf16)]
    kernel = functools.partial(
        weight_kernel, steps, seqs, count, [b for _, _, b in xs], centre is not None, norm_steps
    )
    return pl.pallas_call(
        without(kernel, len(specs), len(deps), -1 - len(scratch)),
        grid=(norm_steps + nb,),
        in_specs=specs + after(deps),
        out_specs=out_specs + [token_spec],
        out_shape=out_shape + [token_shape],
        scratch_shapes=scratch,
        compiler_params=params(),
        name="weight_grad",
    )(*operands, *grads, *deps)


def row_blocks(left, right):
    pairs = []
    for x in (left, right):
        if isinstance(x, (list, tuple)):
            pairs.append([(part, 0) for part in x])
        else:
            pairs.append([(x, k) for k in range(x.shape[0] // WIDE)])
    return list(zip(*pairs))


def fetch_blocks(blocks, arrays, held_blocks, sems):
    copies = []
    for k, pair in enumerate(blocks):
        for side, (_, at) in enumerate(pair):
            place = arrays[2 * k + side].at[pl.ds(at * WIDE, WIDE)]
            copies.append(pltpu.make_async_copy(place, held_blocks.at[k, side], sems.at[k, side]))
    return copies


def block_product(low, held_blocks, sems, k):
    half = low.shape[1] // 2
    for side in range(2):
        place = held_blocks.at[k, side]
        pltpu.make_async_copy(place, place, sems.at[k, side]).wait()
    acc = dot(low[:, :half], held_blocks[k, 0], ((1,), (1,)))
    return acc + dot(low[:, half:], held_blocks[k, 1], ((1,), (1,)))


def pull_kernel(nb, tiled, low, *refs):
    *weights, out = refs
    j = pl.program_id(0)
    half = weights[0].shape[1]

    def go(left, right):
        acc = dot(low[:, :half], left[...], ((1,), (1,))) + dot(low[:, half:], right[...], ((1,), (1,)))
        if tiled:
            for k in range(WIDE // LANES):
                out[k] = acc[:, k * LANES : (k + 1) * LANES]
        else:
            out[...] = acc.astype(out.dtype)

    for k in range(len(weights) // 2):
        pl.when((j >= k * nb) & (j < (k + 1) * nb))(functools.partial(go, *weights[2 * k : 2 * k + 2]))


def pull(low, left, right, dtype, deps=()):
    rows, width = low.shape
    half = width // 2
    blocks = row_blocks(left, right)
    operands = [x for pair in blocks for x, _ in pair]
    specs = [pl.BlockSpec((WIDE, half), lambda j, at=at: (at, 0)) for pair in blocks for _, at in pair]
    return pl.pallas_call(
        without(functools.partial(pull_kernel, 1, False), 1 + len(operands), len(deps), -1),
        grid=(len(blocks),),
        in_specs=[whole((rows, width))] + specs + after(deps),
        out_specs=[pl.BlockSpec((rows, WIDE), lambda j: (0, j)), token_spec],
        out_shape=[jax.ShapeDtypeStruct((rows, len(blocks) * WIDE), dtype), token_shape],
        compiler_params=params(),
        name="pull",
    )(low, *operands, *deps)


def fold_kernel(counts, at_ref, *refs):
    kept, sent = refs[-2:]
    at = 0
    for k, n in enumerate(counts):
        parts = refs[at : at + 2 * n]
        kept[k] = sum(p[...].astype(f32) for p in parts[:n])
        sent[k] = sum(p[...].astype(f32) for p in parts[n:]).astype(bf16)
        at += 2 * n


def fold(mine, stacks, rows, deps=(), mebibytes=16):
    specs, operands = [], []
    width = stacks[0][0][0].shape[-1]
    cuts = 2
    lanes = width // cuts
    for stack in stacks:
        for side in (0, 1):
            for array, index, base in stack:
                operands.append(array)
                specs.append(
                    pl.BlockSpec(
                        (None, rows, lanes),
                        lambda j, at, side=side, index=index, base=base: (index, base + (at[0] + side) % 2, j),
                    )
                )
    count = len(stacks)
    out_spec = pl.BlockSpec((count, rows, lanes), lambda j, at: (0, 0, j))
    kernel = functools.partial(fold_kernel, [len(stack) for stack in stacks])
    return pl.pallas_call(
        without(kernel, 1 + len(operands), len(deps), -1),
        grid_spec=pltpu.PrefetchScalarGridSpec(
            num_scalar_prefetch=1, grid=(cuts,), in_specs=specs + after(deps), out_specs=[out_spec, out_spec, token_spec]
        ),
        out_shape=[
            jax.ShapeDtypeStruct((count, rows, width), f32),
            jax.ShapeDtypeStruct((count, rows, width), bf16),
            token_shape,
        ],
        compiler_params=params(mebibytes),
        name="fold",
    )(jnp.reshape(mine, (1,)).astype(jnp.int32), *operands, *deps)


def total_kernel(counts, *refs):
    *parts, out = refs
    at = 0
    for k, n in enumerate(counts):
        out[k] = sum(p[...].astype(f32) for p in parts[at : at + n]).astype(bf16)
        at += n


def total(stacks, rows, deps=(), mebibytes=16):
    parts = [part for stack in stacks for part in stack]
    count, width = len(stacks), parts[0][0].shape[-1]
    cuts = 2
    lanes = width // cuts
    specs = [
        pl.BlockSpec((None, rows, lanes), lambda j, index=index, block=block: (index, block, j)) for _, index, block in parts
    ]
    out, done = pl.pallas_call(
        without(functools.partial(total_kernel, [len(stack) for stack in stacks]), len(parts), len(deps), -1),
        grid=(cuts,),
        in_specs=specs + after(deps),
        out_specs=[pl.BlockSpec((count, rows, lanes), lambda j: (0, 0, j)), token_spec],
        out_shape=[jax.ShapeDtypeStruct((count, rows, width), bf16), token_shape],
        compiler_params=params(mebibytes),
        name="total",
    )(*[array for array, _, _ in parts], *deps)
    return out.reshape(count * rows, width), done


def join_kernel(at_ref, own, other, out):
    @pl.when(pl.program_id(0) == 0)
    def _():
        out[...] = own[...]

    @pl.when(pl.program_id(0) == 1)
    def _():
        out[...] = other[...]


def join(mine, own, other, deps=()):
    rows, width = own.shape
    spec = pl.BlockSpec((rows, width), lambda j, at: (0, 0))
    return pl.pallas_call(
        without(join_kernel, 3, len(deps), -1),
        grid_spec=pltpu.PrefetchScalarGridSpec(
            num_scalar_prefetch=1,
            grid=(2,),
            in_specs=[spec, spec] + after(deps),
            out_specs=[pl.BlockSpec((rows, width), lambda j, at: ((at[0] + j) % 2, 0)), token_spec],
        ),
        out_shape=[jax.ShapeDtypeStruct((2 * rows, width), bf16), token_shape],
        compiler_params=params(16),
        name="join",
    )(jnp.reshape(mine, (1,)).astype(jnp.int32), own, other, *deps)


def over(value, axis):
    return lax.ppermute(value, axis, [(0, 1), (1, 0)])


def across(value, bit):
    size = lax.axis_size("dp")
    return lax.ppermute(value, "dp", [(i, i ^ bit) for i in range(size)])


def dp_bits():
    return [1 << k for k in range((lax.axis_size("dp") - 1).bit_length())]


def swap_halves(value):
    half = value.shape[-1] // 2
    return jnp.concatenate([value[:, half:], value[:, :half]], axis=1)


def sum_step(value, step, swaps):
    if step not in ("col", "row"):
        return value + across(value, step)
    other = over(value, step)
    rows = [swap_halves(other[k : k + 1]) if axis == step else other[k : k + 1] for k, axis in enumerate(swaps)]
    return value + jnp.concatenate(rows, axis=0)


def on_device(
    inputs,
    w_second,
    gain_second,
    shift_second,
    recur_second,
    w_third,
    gain_third,
    shift_third,
    recur_third,
    cotangent,
):
    steps, seq_group, width = inputs.shape
    share = cotangent.shape[1]
    seqs = share // lax.axis_size("row")
    pitch = round_up(steps + 2, 8)
    rows = seqs * pitch
    half = round_up(width, 2 * BLOCK)
    nb = half // BLOCK
    tiles = 2 * half // LANES
    pieces = lax.axis_size("dp")
    count = steps * seq_group * pieces
    row, col, place = lax.axis_index("row"), lax.axis_index("col"), lax.axis_index("dp")
    bits = dp_bits()

    def turned(order):
        return sum(((place // bit) % 2) << k for k, bit in enumerate(order))


    def pad_weight(w):
        return jnp.pad(w, ((0, half - w.shape[0]), (0, half - w.shape[1])))

    def pad_params(*vectors):
        return jnp.pad(jnp.stack(vectors), ((0, 0), (0, half - width)))

    def bit_of(bit):
        return (place // bit) % 2

    chunks = 2
    spread = len(bits) > 1 and half // (chunks * pieces) >= 16
    orders = [bits[::-1], bits[:1] + bits[:0:-1]]
    places = jnp.stack([col * share + row * seqs, col * share + (1 - row) * seqs]).astype(jnp.int32)
    parts = jnp.stack([row, 1 - row]).astype(jnp.int32)
    own_second = pad_params(gain_second, shift_second, recur_second)
    own_third = pad_params(gain_third, shift_third, recur_third)
    gains_second = jnp.concatenate([own_second, over(own_second, "col")], axis=1)
    deps = ()
    if spread:
        cut_second, cut_third = cut(w_second, w_third, [turned(order) for order in orders], chunks, pieces, half)
        tall = half // (chunks * pieces)
        deps = (cut_second, cut_third)
    if spread:
        cut_second, w_second, w_third = lax.optimization_barrier((cut_second, w_second, w_third))
        far_second, far_third = over(cut_second, "row"), over(cut_third, "row")
    nn2, nn3 = pad_weight(w_second), pad_weight(w_third)
    nf2, fn3 = over(nn2, "col"), over(nn3, "col")
    x_near, send0 = prep(inputs, places, seqs, pitch, half, 0, nb // 2, None, deps)
    x_near, send1 = prep(inputs, places, seqs, pitch, half, nb // 2, nb // 2, x_near)
    if spread:
        send0, send1, far_second, far_third = lax.optimization_barrier((send0, send1, far_second, far_third))
    x_far0 = over(send0, "row")
    x_far1 = over(send1, "row")
    proj_second, near_done = project([(x_near, 0, half)], [[nn2], [nf2]], tiles)
    cot_near, *cot_send, cot_done = prep_grads(jnp.transpose(cotangent, (1, 0, 2)), parts, seqs, pitch, half)
    if spread:
        fn2 = [far_second[k * tall : (k + 1) * tall] for k in range(chunks)]
        nf3 = far_third
        deps = (near_done,)
        for k in range(len(bits)):
            others = [across(piece, order[k]) for piece, order in zip(fn2, orders)]
            if k > 0:
                nf3_other = across(nf3, orders[0][k - 1])
            joined = [join(bit_of(order[k]), piece, other, deps) for piece, order, other in zip(fn2, orders, others)]
            fn2 = [piece for piece, _ in joined]
            if k == len(bits) - 1:
                break
            deps = (cot_done,)
            if k > 0:
                nf3, done = join(bit_of(orders[0][k - 1]), nf3, nf3_other, tuple(done for _, done in joined))
                deps = (done,)
            if k == len(bits) - 2:
                x_far0, nn3, *fn2 = lax.optimization_barrier((x_far0, nn3, *fn2))
        x_far1, *fn2 = lax.optimization_barrier((x_far1, *fn2))
    else:
        far = over(nn2, "row")
        fn2 = [far[: half // 2], far[half // 2 :]]
        nf3 = over(nn3, "row")
    ff2 = [over(chunk, "col") for chunk in fn2]
    x_parts = [(x_far0, 0, half // 2), (x_far1, 0, half // 2)]
    proj_second, sums_near = project(x_parts, [fn2], tiles, 0, proj_second, True, (cot_done,))
    cot_far0 = over(cot_send[0], "row")
    proj_second, sums_far = project(x_parts, [ff2], tiles, half // WIDE, proj_second, True, (cot_far0,))
    sums = jnp.concatenate([sums_near, sums_far], axis=1)
    if spread:
        nf3, done = join(bit_of(bits[1]), nf3, nf3_other, (sums,))
        sums, done = lax.optimization_barrier((sums, done))

    swaps = ("col", "col")
    sums = sum_step(sums, "row", swaps)
    sums, cot_send1 = lax.optimization_barrier((sums, cot_send[1]))
    cot_far1 = over(cot_send1, "row")
    if spread:
        sums = sum_step(sums, bits[0], swaps)
        sums, nf3 = lax.optimization_barrier((sums, nf3))
        nf3_other = across(nf3, bits[0])
    sums = sum_step(sums, "col", swaps)
    for bit in bits[1:] if spread else bits:
        sums = sum_step(sums, bit, swaps)
    sums_second = sums
    hidden, slopes_second, hidden_sums, proj_third, sums_near = first_layer(
        steps, seqs, count, proj_second, sums_second, gains_second, nn3, fn3
    )
    if spread:
        nf3, done = join(bit_of(bits[0]), nf3, nf3_other, (hidden_sums,))
    ff3 = [over(nf3[k * WIDE : (k + 1) * WIDE], "col") for k in range(half // WIDE)]
    hidden_parts = [(hidden, 0, half)] + [(hidden, (half + k * WIDE) // WIDE, WIDE) for k in range(half // WIDE)]
    proj_third, sums_far = project(
        hidden_parts, [[nf3, *ff3]], tiles, half // WIDE, proj_third, False, (cot_far1,)
    )

    swaps = ("row", "row", "col")
    sums = jnp.concatenate([jnp.concatenate([sums_near, sums_far], axis=1), hidden_sums], axis=0)
    for step in ("col", *bits):
        sums = sum_step(sums, step, swaps)
    other = over(jnp.concatenate([sums, own_third], axis=1), "row")
    sums = sums + jnp.concatenate([swap_halves(other[:2, : 2 * half]), other[2:3, : 2 * half]], axis=0)
    gains_third = jnp.concatenate([own_third, other[:, 2 * half :]], axis=1)
    sums_third, centre = sums[:2], (sums[2:3] / count).astype(bf16).astype(f32)
    states_near, out_send0, out_send1, arg_grads_third, sums = second_layer(
        steps, seqs, count, proj_third, sums_third, gains_third, cot_near, (cot_far0, cot_far1)
    )
    swaps = ("row", "row", "row")
    sums = sum_step(sums, "col", swaps)
    sums = sum_step(sums, "row", swaps)
    sums, out_send0 = lax.optimization_barrier((sums, out_send0))
    out_far0 = over(out_send0, "row")
    for bit in bits:
        sums = sum_step(sums, bit, swaps)
    totals_third = sums

    wide = half // WIDE
    cutting = half // 2
    grads = (arg_grads_third, proj_third, sums_third, gains_third, totals_third)
    low_third, columns, fn, ff, _ = weight_grad(steps, seqs, count, [(hidden, wide, wide)], grads, centre, wide)
    from_fn, from_ff = over(fn, "col"), over(ff, "col")
    nn, nf, done = weight_grad(steps, seqs, count, [(hidden, 0, wide)], (low_third,), centre, 0)

    def begin_across(nn, from_fn, nf, from_ff, deps):
        own, other = [(nn[None], 0), (from_fn[None], 0)], [(nf[None], 0), (from_ff[None], 0)]
        tall = cutting // 2
        stacks = [[(array, index, 2) for array, index in part] for part in (own, other)]
        return fold(bit_of(bits[0]), stacks, tall, deps, 56)

    class Chain:
        def __init__(self, stacks, rows, left):
            self.stacks, self.rows, self.left = stacks, rows, list(left)

        def step(self, deps):
            bit = self.left.pop(0)
            self.rows //= 2
            stacks = [[(array, index, 0) for array, index in stack] for stack in self.stacks]
            kept, sent, done = fold(bit_of(bit), stacks, self.rows, deps)
            other = across(sent, bit)
            self.stacks = [[(kept, k), (other, k)] for k in range(len(stacks))]
            return (done,)

        def piece(self, deps):
            while self.left:
                deps = self.step(deps)
            stacks = [[(array, index, 0) for array, index in stack] for stack in self.stacks]
            self.whole, done = total(stacks, self.rows, deps)
            self.back = list(reversed(bits))
            self.other = across(self.whole, self.back[0])
            return (done,)

        def gather(self, deps):
            bit = self.back.pop(0)
            self.whole, done = join(bit_of(bit), self.whole, self.other, deps)
            if self.back:
                self.other = across(self.whole, self.back[0])
            return (done,)

    x3, done = total([[(nf[None], 0, 0), (from_ff[None], 0, 0)]], cutting, (done,), 56)
    x3_come = over(x3, "row")
    kept, sent, done = begin_across(nn, from_fn, nf, from_ff, (done,))
    b3_kept, b3_other = kept, across(sent, bits[0])
    arg_grads_second, sums = first_back(
        steps, seqs, count, low_third, row_blocks(nn3, nf3) + row_blocks(fn3, ff3), slopes_second, hidden, proj_second, sums_second, gains_second,
        (done, out_far0),
    )
    swaps = ("col", "col", "col", "row")
    sums = jnp.concatenate([sums, columns], axis=0)
    sums, b3_other, x3_come = lax.optimization_barrier((sums, b3_other, x3_come))
    sums = sum_step(sums, "col", swaps)
    sums = sum_step(sums, "row", swaps)
    sums, b3_other = lax.optimization_barrier((sums, b3_other))

    def to_row(kept, other, deps):
        sent, done = total([[(kept, 1, 0), (other, 1, 0)]], cutting // 2, deps)
        return over(sent, "row")[None], done

    def to_across(nn, from_other, come, deps):
        stack = [(nn[None], 0, 0), (from_other[None], 0, 0), (come[None], 0, 0)]
        kept, sent, done = fold(bit_of(bits[0]), [stack], cutting // 2, deps, 56)
        return [(kept, 0), (across(sent, bits[0]), 0)], done

    b3_row, done = to_row(b3_kept, b3_other, ())
    sums = sum_step(sums, bits[0], swaps)
    sums, x3_come = lax.optimization_barrier((sums, x3_come))
    a3, done = to_across(nn, from_fn, x3_come, (done,))
    for bit in bits[1:]:
        sums = sum_step(sums, bit, swaps)
    totals_second, columns = sums[:3], sums[3:4]
    c3 = Chain([a3, [(b3_kept, 0), (b3_other, 0), (b3_row, 0)]], cutting // 2, bits[1:])
    totals_second, done, out_send1 = lax.optimization_barrier((totals_second, done, out_send1))
    out_far1 = over(out_send1, "row")
    seen = c3.step((done,))

    grads = (arg_grads_second, proj_second, sums_second, gains_second, totals_second)
    low_second, seen, fn, ff, _ = weight_grad(steps, seqs, count, [(x_far0, 0, 1), (x_far1, 0, 1)], grads, deps=seen)
    from_ff = over(ff, "col")
    seen = c3.step((seen, out_far1)) if c3.left else (seen, out_far1)
    nn, nf, done = weight_grad(steps, seqs, count, [(x_near, 0, wide)], (low_second,), deps=seen)
    from_nf = over(nf, "col")
    x2, done = total([[(fn[None], 0, 0), (from_ff[None], 0, 0)]], cutting, (done,), 56)
    x2_come = over(x2, "row")
    kept, sent, done = begin_across(nn, from_nf, fn, from_ff, (done,))
    b2_kept, b2_other = kept, across(sent, bits[0])
    grad_far, done = pull(low_second, fn2, ff2, bf16, (done,))
    seen = c3.piece((done,))
    output, done = combine(parts, x_near, states_near, (send0, send1), (out_far0, out_far1), seqs, steps, width, seen)
    b2_row, done = to_row(b2_kept, b2_other, (done,))
    a2, done = to_across(nn, from_nf, x2_come, (done,))
    seen = c3.gather((done,))
    grad_near, done = pull(low_second, nn2, nf2, f32, seen)
    seen = (done,)
    b2 = Chain([[(b2_kept, 0), (b2_other, 0), (b2_row, 0)]], cutting // 2, bits[1:])
    seen = b2.step(seen)
    grad_far, done = lax.optimization_barrier((grad_far, *seen))
    grad_far = over(grad_far, "row")
    a2 = Chain([a2], cutting // 2, bits[1:])
    seen = a2.step((done,))
    seen = c3.gather(seen) if c3.back else seen
    seen = b2.step(seen) if b2.left else seen
    seen = a2.step(seen) if a2.left else seen
    seen = b2.piece(seen)
    seen = c3.gather(seen) if c3.back else seen
    seen = a2.piece(seen)
    seen = b2.gather(seen)
    seen = a2.gather(seen)
    seen = b2.gather(seen)
    seen = a2.gather(seen)
    grad_inputs, done = combine(
        parts, cot_near, grad_near, cot_send, (grad_far,), seqs, steps, width, seen
    )
    seen = (done,)
    chains = [c3, b2, a2]
    while any(chain.back for chain in chains):
        for chain in chains:
            if chain.back:
                seen = chain.gather(seen)
    grad_w_third = jnp.transpose(c3.whole.reshape(pieces, 2, -1, half), (1, 0, 2, 3)).reshape(half, half)
    grad_w_second = jnp.concatenate([a2.whole, b2.whole], axis=0)

    output = jnp.transpose(output, (1, 0, 2))
    grad_inputs = jnp.transpose(grad_inputs, (1, 0, 2))
    restore = centre[0, :width, None] * columns[0, None, :width]
    return (
        output,
        grad_inputs,
        grad_w_second[:width, :width].astype(f32),
        totals_second[0, :width],
        totals_second[1, :width],
        totals_second[2, :width],
        grad_w_third[:width, :width].astype(f32) + restore,
        totals_third[0, :width],
        totals_third[1, :width],
        totals_third[2, :width],
    )


def solution(mesh):
    in_specs = (
        P(None, "dp", "row"),
        P("row", "col"),
        P("col"),
        P("col"),
        P("col"),
        P("col", "row"),
        P("row"),
        P("row"),
        P("row"),
        P(None, ("dp", "col"), "row"),
    )
    out_specs = (
        P(None, ("dp", "col"), "row"),
        P(None, ("dp", "col"), "row"),
        P("row", "col"),
        P("col"),
        P("col"),
        P("col"),
        P("col", "row"),
        P("row"),
        P("row"),
        P("row"),
    )
    return jax.shard_map(
        on_device, mesh=mesh, in_specs=in_specs, out_specs=out_specs, check_vma=False
    )
```
